32 devices in a mesh: node: 16 (over z, x, core), local: 2 (over y).
Axes of the slice: x: 2, y: 2, z: 4, core: 2. Of those that a mesh axis runs over, the one named last changes fastest.
Arguments:
- tokens: bfloat16 [2, 16, 3584], P('local', 'node'), may hold values from -6 to 6
- expert_ids: int32 [2, 16, 8], P('local', 'node'), may hold values from 0 to 15, all different within a row; in each aligned block of 16 rows (0 to 15, 16 to 31, ..., all dimensions but the last counted through in order) at most 16 rows name the same one
- route_probs: float32 [2, 16, 8], P('local', 'node'), may hold values from 0.05 to 1
- gate_weight: bfloat16 [16, 3584, 2048], P('node', None, 'local'), may hold values from -0.09375 to 0.09375
- up_weight: bfloat16 [16, 3584, 2048], P('node', None, 'local'), may hold values from -0.09375 to 0.09375
- down_weight: bfloat16 [16, 2048, 3584], P('node', None, 'local'), may hold values from -0.125 to 0.125
- out_grad: bfloat16 [2, 16, 3584], P('local', 'node'), may hold values from -6 to 6
Outputs:
- combined: bfloat16 [2, 16, 3584], P('local', 'node')
- input_grad: bfloat16 [2, 16, 3584], P('local', 'node')
- prob_grad: float32 [2, 16, 8], P('local', 'node')
The draws below stay inside these ranges and needn't reach their ends.
Inputs may be any that keep to these rules, and one draw needn't show every extreme that they name: `expert_ids`: each row names 8 different experts. Among the 16 rows of one token group (one index of the first dimension) no expert is named by more than 16 rows, a bound that some block reaches.
All inputs are finite; a program needn't handle non-finite values.
Results may differ from the reference program's by a relative error of at most 0.018.
Values may be sent and summed in bfloat16 or wider, within the bound.
No kernel may reach another device: no remote copies, remote signals or barrier semaphores. Data moves between devices by JAX's collectives and lax.ppermute only.
A program may use at most 64 MiB of HBM per device.

```python
import math
import jax
import jax.numpy as jnp
import numpy as np
from jax import lax

D = 3584
F = 2048
TOPK = 8
EXPERTS = 16
GROUPS = 2
COLROWS = 16
CAP = 16
N_LOCAL = 2


def steps_of(rng, dims, pieces, low, largest):
    loudness, own = 1.0, jax.random.fold_in(rng, 6)
    for position, shards_of in pieces:
        draws = jnp.exp(jax.random.uniform(jax.random.fold_in(own, position), (shards_of,), jnp.float32, low / len(pieces), largest / len(pieces)))
        loudness = loudness * jnp.repeat(draws, dims[position] // shards_of).reshape([-1 if axis == position else 1 for axis in range(len(dims))])
    return loudness


def assign_block(key, own, number, rows, amount, top, limit, slope):
    ranking = jax.random.permutation(key, amount)
    heavy_load, usual = load_shares(amount, rows * top, limit, slope, True), load_shares(amount, rows * top, limit, slope, False)
    places = jnp.arange(amount)

    def named(sizes, offset_by):
        used = int((sizes > 0).sum())
        fixed = max(1, used // 4)
        passed = fixed + (places - fixed + offset_by * (used - fixed)) % max(1, amount - fixed)
        return jnp.zeros((amount,), jnp.int32).at[ranking[jnp.where(places < fixed, places, passed)]].set(jnp.asarray(sizes, jnp.int32))

    sizes = jnp.where(number % 4 == 0, named(heavy_load, number // 4), named(usual, number - number // 4 - 1))
    mixed = jax.random.permutation(jax.random.fold_in(own, 3), amount)
    donor, sink = mixed[0:amount // 2 * 2:2], mixed[1:amount // 2 * 2:2]
    room = jnp.minimum(sizes[donor] - 1, limit - sizes[sink]) // 2
    room = jnp.where((donor == ranking[0]) | (sink == ranking[0]) | (sizes[sink] == 0), 0, jnp.maximum(room, 0))
    passed = jax.random.randint(jax.random.fold_in(own, 4), (amount // 2,), 0, 1 << 20) % (room + 1)
    sizes = sizes.at[donor].add(-passed).at[sink].add(passed)
    items = jnp.searchsorted(jnp.cumsum(sizes), jnp.arange(rows * top), side="right").astype(jnp.int32)
    grid = items.reshape(top, rows).T
    grid = grid[jax.random.permutation(jax.random.fold_in(own, 1), rows)]
    offset_by = jax.random.randint(jax.random.fold_in(own, 2), (rows, 1), 0, top)
    return jnp.take_along_axis(grid, (jnp.arange(top)[None, :] + offset_by) % top, axis=1)


def load_shares(amount, total, reach, skew, full):
    weights = [(1 << 20) // math.isqrt(grade ** skew) + 1 for grade in range(1, amount + 1)]
    largest = reach if full else min(reach, max(-(-total // amount), total * weights[0] // sum(weights)))
    least = 1 if total - largest >= amount - 1 else 0
    counts, rest = [largest] + [least] * (amount - 1), total - largest - least * (amount - 1)
    while rest > 0:
        free = [i for i in range(1, amount) if counts[i] < largest] or [i for i in range(1, amount) if counts[i] < reach]
        pool, remaining = sum([weights[i] for i in free]), rest
        for i in free:
            extra = min(reach - counts[i], max(1, remaining * weights[i] // pool), rest)
            counts[i] = counts[i] + extra
            rest = rest - extra
    return np.array(counts)


def centred(rng, shape, spread, most, shards=(), held_as=jnp.bfloat16):
    array = spread * jax.random.normal(rng, shape, jnp.float32)
    if shards:
        array = array * steps_of(rng, shape, shards, -0.22, 0.18)
    return jnp.clip(array, -most, most).astype(held_as)


def setup_inputs(seed: int = 0) -> dict:
    splits = jax.random.split(jax.random.key(seed), 8)
    tokens = centred(splits[0], (GROUPS, COLROWS, D), 1.0, 6.0, ((0, 2), (1, 16)))
    expert_ids_keys = jax.random.split(jax.random.fold_in(splits[1], 1), GROUPS * COLROWS // COLROWS)
    expert_ids_turns = jax.random.permutation(jax.random.fold_in(splits[1], 3), GROUPS * COLROWS // COLROWS)
    expert_ids = jax.vmap(lambda own, number: assign_block(jax.random.fold_in(splits[1], 2), own, number, COLROWS, EXPERTS, TOPK, CAP, 2))(expert_ids_keys, expert_ids_turns).reshape((GROUPS, COLROWS, TOPK))
    route_probs = jnp.clip(jnp.exp(math.log(1.0) - 2.9957323 * jax.random.uniform(splits[2], (GROUPS, COLROWS, TOPK), jnp.float32) ** steps_of(splits[2], (GROUPS, COLROWS, TOPK), ((0, 2), (1, 16)), -0.2, 0.2)), 0.05, 1.0)
    gate_weight = centred(splits[3], (EXPERTS, D, F), D ** -0.5, 0.09375, ((0, 16), (2, 2)))
    up_weight = centred(splits[4], (EXPERTS, D, F), D ** -0.5, 0.09375, ((0, 16), (2, 2)))
    down_weight = centred(splits[5], (EXPERTS, F, D), F ** -0.5, 0.125, ((0, 16), (2, 2)))
    out_grad = centred(splits[6], (GROUPS, COLROWS, D), 1.0, 6.0, ((0, 2), (1, 16)))
    return {"tokens": tokens, "expert_ids": expert_ids, "route_probs": route_probs, "gate_weight": gate_weight, "up_weight": up_weight, "down_weight": down_weight, "out_grad": out_grad}


def reference(tokens, expert_ids, route_probs, gate_weight, up_weight, down_weight, out_grad):
    group_count, column_rows, width = tokens.shape
    expert_count = gate_weight.shape[0]
    hidden_all = gate_weight.shape[2]
    width_block = width // N_LOCAL
    hidden_block = hidden_all // N_LOCAL
    onehot = (expert_ids[..., None] == jnp.arange(expert_count, dtype=jnp.int32)).astype(jnp.float32)
    weights = jnp.einsum('lmk,lmke->lme', route_probs.astype(jnp.float32), onehot)
    member = jnp.sum(onehot, axis=2)
    grad_wide = out_grad.astype(jnp.float32)
    tokens_wide = tokens.astype(jnp.float32)
    row_total = group_count * CAP

    def one_expert(carry, inputs):
        comb_acc, grad_acc = carry
        gate_w, up_w, down_w, index = inputs
        live = lax.dynamic_index_in_dim(member, index, 2, keepdims=False).astype(jnp.int32)
        route_weight = lax.dynamic_index_in_dim(weights, index, 2, keepdims=False)
        order = jnp.cumsum(live, axis=1) - live
        slot_ids = jnp.arange(CAP, dtype=jnp.int32)
        select = ((order[:, None, :] == slot_ids[None, :, None]) & (live[:, None, :] > 0)).astype(jnp.float32)
        rows = jnp.einsum('lcm,lmd->lcd', select, tokens_wide).reshape(row_total, width).astype(jnp.bfloat16)
        gate_pre = jnp.dot(rows, gate_w, preferred_element_type=jnp.float32)
        up_pre = jnp.dot(rows, up_w, preferred_element_type=jnp.float32)
        sigmoid_gate = jax.nn.sigmoid(gate_pre)
        silu_gate = gate_pre * sigmoid_gate
        hidden = (silu_gate * up_pre).astype(jnp.bfloat16)
        routed = jnp.dot(hidden, down_w, preferred_element_type=jnp.float32).astype(jnp.bfloat16)
        routed_tok = jnp.einsum('lcm,lcd->lmd', select, routed.astype(jnp.float32).reshape(group_count, CAP, width))
        comb_acc = comb_acc + route_weight[..., None] * routed_tok
        prob_term = jnp.sum(grad_wide * routed_tok, axis=2)
        scaled = (route_weight[..., None] * grad_wide).astype(jnp.bfloat16)
        scaled_rows = jnp.einsum('lcm,lmd->lcd', select, scaled.astype(jnp.float32)).reshape(row_total, width)
        scaled_blocks = scaled_rows.reshape(row_total, N_LOCAL, width_block)
        down_blocks = down_w.astype(jnp.float32).reshape(hidden_all, N_LOCAL, width_block)
        hidden_parts = jnp.einsum('rjd,fjd->jrf', scaled_blocks, down_blocks).astype(jnp.bfloat16)
        hidden_grad = jnp.sum(hidden_parts.astype(jnp.float32), axis=0)
        gate_grad = (hidden_grad * up_pre * sigmoid_gate * (1.0 + gate_pre * (1.0 - sigmoid_gate))).astype(jnp.bfloat16)
        up_grad = (hidden_grad * silu_gate).astype(jnp.bfloat16)
        gate_blocks = gate_grad.astype(jnp.float32).reshape(row_total, N_LOCAL, hidden_block)
        up_blocks = up_grad.astype(jnp.float32).reshape(row_total, N_LOCAL, hidden_block)
        gate_w_blocks = gate_w.astype(jnp.float32).reshape(width, N_LOCAL, hidden_block)
        up_w_blocks = up_w.astype(jnp.float32).reshape(width, N_LOCAL, hidden_block)
        input_parts = jnp.einsum('rjf,djf->jrd', gate_blocks, gate_w_blocks) + jnp.einsum('rjf,djf->jrd', up_blocks, up_w_blocks)
        input_parts = input_parts.astype(jnp.bfloat16)
        route_grad = jnp.sum(input_parts.astype(jnp.float32), axis=0).astype(jnp.bfloat16)
        grad_acc = grad_acc + jnp.einsum('lcm,lcd->lmd', select, route_grad.astype(jnp.float32).reshape(group_count, CAP, width))
        return (comb_acc, grad_acc), prob_term

    start_comb = jnp.zeros((group_count, column_rows, width), jnp.float32)
    start_grad = jnp.zeros((group_count, column_rows, width), jnp.float32)
    (comb_acc, grad_acc), prob_terms = lax.scan(one_expert, (start_comb, start_grad), (gate_weight, up_weight, down_weight, jnp.arange(expert_count, dtype=jnp.int32)))
    prob_grad = jnp.einsum('elm,lmke->lmk', prob_terms, onehot)
    return comb_acc.astype(jnp.bfloat16), grad_acc.astype(jnp.bfloat16), prob_grad
```

```python
import functools

import jax
import jax.numpy as jnp
from jax import lax
from jax.experimental import pallas as pl
from jax.experimental.pallas import tpu as pltpu
from jax.sharding import Mesh
from jax.sharding import PartitionSpec as P

BF16 = jnp.bfloat16
F32 = jnp.float32
LANES = 128
CHUNK = 512
DISPATCH_ROWS = 16
RETURN_ROWS = 16
COLS = 256

NT = (((1,), (1,)), ((), ()))
VMEM = pl.BlockSpec(memory_space=pltpu.VMEM)
SMEM = pl.BlockSpec(memory_space=pltpu.SMEM)


def ceil_div(a, b):
    return -(-a // b)


def call(body, outs, ins, scratch=(), flops=0, moved=0, limit=48 << 20):
    return pl.pallas_call(
        body,
        out_shape=tuple(jax.ShapeDtypeStruct(s, d) for s, d in outs),
        in_specs=ins,
        out_specs=tuple(VMEM for _ in outs),
        scratch_shapes=list(scratch),
        compiler_params=pltpu.CompilerParams(vmem_limit_bytes=limit),
        cost_estimate=pl.CostEstimate(flops=flops, bytes_accessed=moved, transcendentals=0),
    )


def dot(a, b):
    return jnp.dot(a, b, preferred_element_type=F32)


def dot_nt(a, b):
    return lax.dot_general(a, b, NT, preferred_element_type=F32)


def pack_body(parts, ids_ref, probs_ref, tok_ref, grad_ref, out_ref, wide):
    top = ids_ref.shape[2]
    lane = lax.broadcasted_iota(jnp.int32, (1, LANES), 1)
    weight = jnp.zeros((1, LANES), F32)
    for k in range(top):
        weight = jnp.where(lane == ids_ref[0, 0, k], probs_ref[0, 0, k], weight)
    high = weight.astype(BF16).astype(F32)
    wide[...] = jnp.zeros_like(wide)
    for i in range(parts):
        cols = pl.ds(i * CHUNK, CHUNK)
        wide[i : i + 1, :] = tok_ref[0, :, cols].astype(F32)
        wide[8 + i : 9 + i, :] = grad_ref[0, :, cols].astype(F32)
    wide[7:8, 0:LANES] = high
    wide[7:8, LANES : 2 * LANES] = weight - high
    out_ref[...] = jnp.broadcast_to(wide[...].astype(BF16)[None], out_ref.shape)


def first_body(
    own_ref, other_ref, gate_ref, up_ref, down_ref,
    send_ref, cot_ref, gate_out, up_out, weight_out,
    wide, rows, grads,
):
    count = own_ref.shape[0]
    parts = rows.shape[1] // CHUNK
    hidden = gate_ref.shape[1]
    feats = down_ref.shape[1]
    local = lax.axis_index("local")
    expert = lax.axis_index("chip") * 2 + lax.axis_index("core")
    lane = lax.broadcasted_iota(jnp.int32, (count, LANES), 1)
    for half, ref in enumerate((own_ref, other_ref)):
        at = pl.ds(half * count, count)
        wide[...] = ref[...].astype(F32)
        for i in range(parts):
            cols = pl.ds(i * CHUNK, CHUNK)
            rows[at, cols] = wide[:, i, :].astype(BF16)
            grads[at, cols] = wide[:, 8 + i, :].astype(BF16)
        both = wide[:, 7, 0:LANES] + wide[:, 7, LANES : 2 * LANES]
        both = jnp.sum(jnp.where(lane == expert, both, 0.0), axis=1, keepdims=True)
        weight_out[at, :] = jnp.broadcast_to(both, (count, LANES))
    grad_half = grads[:, pl.ds(pl.multiple_of(local * feats, LANES), feats)]
    steps = hidden // COLS

    def cot(n, carry):
        at = pl.multiple_of(n * COLS, COLS)
        own = dot_nt(grad_half, down_ref[pl.ds(pl.multiple_of(local * hidden + at, COLS), COLS), :])
        cot_ref[:, pl.ds(at, COLS)] = own
        away = dot_nt(
            grad_half, down_ref[pl.ds(pl.multiple_of((1 - local) * hidden + at, COLS), COLS), :]
        )
        send_ref[:, pl.ds(at, COLS)] = away.astype(BF16)
        return carry

    lax.fori_loop(0, steps, cot, 0)
    tokens = rows[...]

    def forward(n, carry):
        at = pl.multiple_of(n * COLS, COLS)
        cols = pl.ds(at, COLS)
        gate = dot(tokens, gate_ref[:, cols])
        up = dot(tokens, up_ref[:, cols])
        gate_out[:, cols] = gate
        up_out[:, cols] = up
        send_ref[:, pl.ds(pl.multiple_of(hidden + at, COLS), COLS)] = (
            gate * jax.nn.sigmoid(gate) * up
        ).astype(BF16)
        return carry

    lax.fori_loop(0, steps, forward, 0)


def routed_own_body(send_ref, down_ref, out_ref):
    hidden = send_ref.shape[1] // 2
    local = lax.axis_index("local")
    act = send_ref[:, hidden:]
    at = pl.ds(pl.multiple_of(local * hidden, COLS), hidden)

    def step(n, carry):
        cols = pl.ds(pl.multiple_of(n * COLS, COLS), COLS)
        out_ref[:, cols] = dot(act, down_ref[at, cols])
        return carry

    lax.fori_loop(0, out_ref.shape[1] // COLS, step, 0)


def second_body(
    send_ref, recv_ref, cot_ref, gate_in, up_in, weight_in, routed_in,
    gate_ref, up_ref, down_ref,
    mine_ref, other_ref,
    wide,
):
    total, width2 = send_ref.shape
    hidden = width2 // 2
    feats = routed_in.shape[1]
    width = gate_ref.shape[0]
    count = total // 2
    local = lax.axis_index("local")
    expert = lax.axis_index("chip") * 2 + lax.axis_index("core")
    weight = weight_in[:, 0:1]
    gate, up = gate_in[...], up_in[...]
    sig = jax.nn.sigmoid(gate)
    cot = cot_ref[...] + recv_ref[:, :hidden].astype(F32)
    prob = jnp.sum(cot * send_ref[:, hidden:].astype(F32), axis=1, keepdims=True)
    hidden_grad = cot * weight
    gate_grad = (hidden_grad * up * sig * (1.0 + gate * (1.0 - sig))).astype(BF16)
    up_grad = (hidden_grad * (gate * sig)).astype(BF16)

    def put(slot, value):
        wide[:, slot // 3, (slot % 3) * LANES : (slot % 3 + 1) * LANES] = value

    for n in range(width // COLS):
        at = pl.ds(n * COLS, COLS)
        part = dot_nt(gate_grad, gate_ref[at, :]) + dot_nt(up_grad, up_ref[at, :])
        for j in range(COLS // LANES):
            put(n * (COLS // LANES) + j, part[:, j * LANES : (j + 1) * LANES])
    base = width // LANES
    act = recv_ref[:, hidden:]
    at = pl.ds(pl.multiple_of((1 - local) * hidden, COLS), hidden)
    for n in range(feats // COLS):
        cols = slice(n * COLS, (n + 1) * COLS)
        part = (dot(act, down_ref[at, cols]) + routed_in[:, cols]).astype(BF16).astype(F32) * weight
        for j in range(COLS // LANES):
            put(base + n * (COLS // LANES) + j, part[:, j * LANES : (j + 1) * LANES])
    base += feats // LANES
    lane = lax.broadcasted_iota(jnp.int32, (total, LANES), 1)
    prob = jnp.where(lane == expert, prob, 0.0)
    high = prob.astype(BF16).astype(F32)
    put(base, high)
    put(base + 1, prob - high)
    for slot in range(base + 2, 3 * RETURN_ROWS):
        put(slot, jnp.zeros((total, LANES), F32))
    mine_ref[...] = wide[:count].astype(BF16)
    other_ref[...] = wide[count:].astype(BF16)


def final_body(in_ref, ids_ref, comb_ref, grad_ref, prob_ref, wide):
    groups = in_ref.shape[0]
    width = comb_ref.shape[2]
    feats = width // 2
    parts = [
        functools.reduce(lambda a, b: a + b, [in_ref[i].astype(F32) for i in range(j, groups, 2)])
        for j in range(2)
    ]
    wide[0], wide[1] = parts

    def get(j, slot):
        return wide[j, slot // 3 : slot // 3 + 1, (slot % 3) * LANES : (slot % 3 + 1) * LANES]

    base = width // LANES
    for c in range(base):
        grad_ref[0, :, c * LANES : (c + 1) * LANES] = (get(0, c) + get(1, c)).astype(BF16)
    for j in range(2):
        for c in range(feats // LANES):
            at = j * feats + c * LANES
            comb_ref[0, :, at : at + LANES] = get(j, base + c).astype(BF16)
    base += feats // LANES
    prob = get(0, base) + get(1, base) + get(0, base + 1) + get(1, base + 1)
    lane = lax.broadcasted_iota(jnp.int32, (1, LANES), 1)
    top = ids_ref.shape[2]
    out = jnp.zeros((1, LANES), F32)
    for k in range(top):
        value = jnp.sum(jnp.where(lane == ids_ref[0, 0, k], prob, 0.0), axis=1, keepdims=True)
        out = jnp.where(lane == k, value, out)
    prob_ref[0] = out[:, :top]


def swap(x, axis):
    return lax.ppermute(x, axis, [(0, 1), (1, 0)])


def fast_device(tokens, expert_ids, route_probs, gate_weight, up_weight, down_weight, out_grad):
    chips = lax.axis_size("chip")
    groups = chips * 2
    total = 2 * groups
    width = tokens.shape[2]
    gate_w, up_w, down_w = gate_weight[0], up_weight[0], down_weight[0]
    hidden = gate_w.shape[1]
    feats = down_w.shape[1]
    one = width * hidden * 2
    (packed,) = call(
        functools.partial(pack_body, width // CHUNK),
        [((groups, DISPATCH_ROWS, CHUNK), BF16)],
        [SMEM, SMEM, VMEM, VMEM],
        [pltpu.VMEM((DISPATCH_ROWS, CHUNK), F32)],
    )(expert_ids, route_probs, tokens, out_grad)
    own = lax.all_to_all(packed, ("chip", "local"), split_axis=0, concat_axis=0, tiled=True)
    other = swap(own, "core")
    send, cot, gate, up, weight = call(
        first_body,
        [
            ((total, 2 * hidden), BF16),
            ((total, hidden), F32),
            ((total, hidden), F32),
            ((total, hidden), F32),
            ((total, LANES), F32),
        ],
        [VMEM] * 5,
        [
            pltpu.VMEM((groups, DISPATCH_ROWS, CHUNK), F32),
            pltpu.VMEM((total, width), BF16),
            pltpu.VMEM((total, width), BF16),
        ],
        flops=total * 3 * one,
        moved=3 * one,
    )(own, other, gate_w, up_w, down_w)
    recv = swap(send, "local")
    (routed_own,) = call(
        routed_own_body,
        [((total, feats), F32)],
        [VMEM] * 2,
        flops=total * one // 2,
        moved=one // 2,
    )(send, down_w)
    mine, away = call(
        second_body,
        [((groups, RETURN_ROWS, 3 * LANES), BF16)] * 2,
        [VMEM] * 10,
        [pltpu.VMEM((total, RETURN_ROWS, 3 * LANES), F32)],
        flops=total * 5 * one // 2,
        moved=5 * one // 2,
    )(send, recv, cot, gate, up, weight, routed_own, gate_w, up_w, down_w)
    summed = (mine.astype(F32) + swap(away, "core").astype(F32)).astype(BF16)
    back = lax.all_to_all(summed, ("chip", "local"), split_axis=0, concat_axis=0, tiled=True)
    return call(
        final_body,
        [((1, 1, width), BF16), ((1, 1, width), BF16), (expert_ids.shape, F32)],
        [VMEM, SMEM],
        [pltpu.VMEM((2, RETURN_ROWS, 3 * LANES), F32)],
    )(back, expert_ids)


def selector(flags, capacity):
    live = (flags > 0).astype(jnp.int32)
    order = jnp.cumsum(live) - live
    slot_ids = lax.broadcasted_iota(jnp.int32, (capacity, flags.shape[0]), 0)
    return ((slot_ids == order[None, :]) & (live[None, :] > 0)).astype(jnp.bfloat16)


def per_device(tokens, expert_ids, route_probs, gate_weight, up_weight, down_weight, out_grad):
    node_count = lax.axis_size("node")
    token_count = tokens.shape[1]
    width = tokens.shape[2]
    top_count = expert_ids.shape[2]
    column_rows = token_count * node_count
    capacity = min(column_rows, 5 * column_rows * top_count // (2 * node_count))
    slot_count = node_count * token_count
    gate_w = gate_weight[0]
    up_w = up_weight[0]
    down_w = down_weight[0]
    hidden_dev = gate_w.shape[1]
    onehot = (expert_ids[0][..., None] == jnp.arange(node_count, dtype=jnp.int32)).astype(
        jnp.float32
    )
    weights = jnp.einsum("tk,tke->te", route_probs[0], onehot)
    member = jnp.sum(onehot, axis=1)
    own_rows = tokens[0]
    zero_value = jnp.zeros((), jnp.bfloat16)
    own_flags = member.T.astype(jnp.bfloat16)
    send_rows = jnp.where(own_flags[:, :, None] > 0, own_rows[None], zero_value)
    recv_rows, recv_flags = (
        lax.all_to_all(send_rows, "node", split_axis=0, concat_axis=0, tiled=True),
        lax.all_to_all(own_flags, "node", split_axis=0, concat_axis=0, tiled=True),
    )
    select = selector(recv_flags.reshape(slot_count), capacity)
    packed_rows = jnp.dot(
        select, recv_rows.reshape(slot_count, width), preferred_element_type=jnp.float32
    ).astype(jnp.bfloat16)
    piece = lax.all_gather(packed_rows, "local", axis=0, tiled=True)
    gate_part = jnp.dot(piece, gate_w, preferred_element_type=jnp.float32)
    up_part = jnp.dot(piece, up_w, preferred_element_type=jnp.float32)
    joined = jnp.concatenate([gate_part, up_part], axis=1)
    gate_pre = joined[:, :hidden_dev]
    up_pre = joined[:, hidden_dev:]
    sigmoid_gate = jax.nn.sigmoid(gate_pre)
    silu_gate = gate_pre * sigmoid_gate
    hidden = (silu_gate * up_pre).astype(jnp.bfloat16)
    block = down_w
    routed_part = jnp.dot(
        lax.all_gather(hidden, "local", axis=1, tiled=True),
        block,
        preferred_element_type=jnp.float32,
    )
    routed_cols = routed_part.astype(jnp.bfloat16)
    routed_own = lax.all_to_all(routed_cols, "local", split_axis=0, concat_axis=1, tiled=True)
    routed_slots = jnp.dot(select.T, routed_own, preferred_element_type=jnp.float32).astype(
        jnp.bfloat16
    )
    routed_back = lax.all_to_all(
        routed_slots.reshape(node_count, token_count, width),
        "node",
        split_axis=0,
        concat_axis=0,
        tiled=True,
    )
    routed_wide = routed_back.astype(jnp.float32)
    combined = jnp.einsum("te,etd->td", weights, routed_wide).astype(jnp.bfloat16)
    grad_wide = out_grad[0].astype(jnp.float32)
    prob_terms = jnp.einsum("td,etd->te", grad_wide, routed_wide)
    prob_grad = jnp.einsum("te,tke->tk", prob_terms, onehot)
    scaled = (weights.T[:, :, None] * grad_wide[None]).astype(jnp.bfloat16)
    grad_recv = lax.all_to_all(scaled, "node", split_axis=0, concat_axis=0, tiled=True)
    grad_own = jnp.dot(
        select, grad_recv.reshape(slot_count, width), preferred_element_type=jnp.float32
    ).astype(jnp.bfloat16)
    grad_cols = lax.all_to_all(grad_own, "local", split_axis=1, concat_axis=0, tiled=True)
    block = down_w
    hidden_grad = (
        lax.psum_scatter(
            lax.dot_general(
                block, grad_cols, (((1,), (1,)), ((), ())), preferred_element_type=jnp.float32
            ).astype(jnp.bfloat16),
            "local",
            scatter_dimension=0,
            tiled=True,
        )
        .astype(jnp.float32)
        .T
    )
    gate_grad = (
        hidden_grad * up_pre * sigmoid_gate * (1.0 + gate_pre * (1.0 - sigmoid_gate))
    ).astype(jnp.bfloat16)
    up_grad = (hidden_grad * silu_gate).astype(jnp.bfloat16)
    first = lax.dot_general(
        gate_grad, gate_w, (((1,), (1,)), ((), ())), preferred_element_type=jnp.float32
    )
    second = lax.dot_general(
        up_grad, up_w, (((1,), (1,)), ((), ())), preferred_element_type=jnp.float32
    )
    input_own = lax.psum_scatter(
        (first + second).astype(jnp.bfloat16), "local", scatter_dimension=0, tiled=True
    )
    input_slots = jnp.dot(select.T, input_own, preferred_element_type=jnp.float32).astype(
        jnp.bfloat16
    )
    input_back = lax.all_to_all(
        input_slots.reshape(node_count, token_count, width),
        "node",
        split_axis=0,
        concat_axis=0,
        tiled=True,
    )
    input_grad = jnp.sum(input_back.astype(jnp.float32), axis=0).astype(jnp.bfloat16)
    return (combined[None], input_grad[None], prob_grad[None])


def solution(mesh):
    node, local = mesh.shape["node"], mesh.shape["local"]
    if local == 2 and node % 2 == 0 and node <= 16:
        mesh = Mesh(mesh.devices.reshape(node // 2, 2, local), ("chip", "core", "local"))
        body, nodes = fast_device, ("chip", "core")
    else:
        body, nodes = per_device, "node"
    rows = P("local", nodes, None)
    weights = P(nodes, None, "local")
    return jax.shard_map(
        body,
        mesh=mesh,
        in_specs=(rows, rows, rows, weights, weights, weights, rows),
        out_specs=(rows, rows, rows),
        check_vma=False,
    )
```

```python
import functools

import jax
import jax.numpy as jnp
from jax import lax
from jax.experimental import pallas as pl
from jax.experimental.pallas import tpu as pltpu
from jax.sharding import Mesh
from jax.sharding import PartitionSpec as P

BF16 = jnp.bfloat16
F32 = jnp.float32
LANES = 128
COLS = 256
ROWS = 16
SPAN = COLS + LANES

NT = (((1,), (1,)), ((), ()))
VMEM = pl.BlockSpec(memory_space=pltpu.VMEM)
ANY = pl.BlockSpec(memory_space=pl.ANY)
SMEM = pl.BlockSpec(memory_space=pltpu.SMEM)


def call(body, outs, ins, scratch=(), products=0, moved=0):
    return pl.pallas_call(
        body,
        out_shape=tuple(outs),
        in_specs=ins,
        out_specs=tuple(VMEM for _ in outs),
        scratch_shapes=list(scratch),
        compiler_params=pltpu.CompilerParams(vmem_limit_bytes=12 << 20),
        cost_estimate=pl.CostEstimate(
            flops=int(products), bytes_accessed=int(moved), transcendentals=0
        ),
    )


def shaped(shape, dtype):
    return jax.ShapeDtypeStruct(shape, dtype)


def in_hbm(*arrays):
    return tuple(pltpu.with_memory_space_constraint(a, pltpu.HBM) for a in arrays)


def dot(a, b):
    return jnp.dot(a, b, preferred_element_type=F32)


def dot_nt(a, b):
    return lax.dot_general(a, b, NT, preferred_element_type=F32)


def high_low(x):
    high = x.astype(BF16).astype(F32)
    return high, x - high


def pack_body(
    ids_hbm, probs_hbm, tok_hbm, grad_hbm, out_ref, wide, ids_ref, probs_ref, tok_ref, grad_ref, sems
):
    pairs = ((ids_hbm, ids_ref), (probs_hbm, probs_ref), (tok_hbm, tok_ref), (grad_hbm, grad_ref))
    copies = [pltpu.make_async_copy(a, b, sems.at[i]) for i, (a, b) in enumerate(pairs)]
    for copy in copies:
        copy.start()
    wide[...] = jnp.zeros_like(wide)
    lane = lax.broadcasted_iota(jnp.int32, (1, LANES), 1)
    weight = jnp.zeros((1, LANES), F32)
    for copy in copies:
        copy.wait()
    for k in range(ids_ref.shape[2]):
        weight = jnp.where(lane == ids_ref[0, 0, k], probs_ref[0, 0, k], weight)
    width = tok_ref.shape[2]
    meta = width // COLS
    half = width // 2
    for i in range(meta):
        wide[i : i + 1, 0:COLS] = tok_ref[0, :, i * COLS : (i + 1) * COLS].astype(F32)
    high, low = high_low(weight)
    wide[meta : meta + 1, 0:LANES] = high
    wide[meta : meta + 1, LANES:COLS] = low
    for j in range(2):
        for i in range(half // LANES):
            at = j * half + i * LANES
            wide[i : i + 1, COLS:SPAN] = grad_ref[0, :, at : at + LANES].astype(F32)
        block = wide[...].astype(BF16)
        for i in range(j, out_ref.shape[0], 2):
            out_ref[i] = block


def cot_body(
    own_ref, other_ref, down_hbm, gate_hbm,
    away_ref, cot_ref, weight_out, rows, down_ref, gate_ref,
    wide, grads, sems,
):
    count = own_ref.shape[0]
    width = rows.shape[1]
    hidden = cot_ref.shape[1]
    feats = down_ref.shape[1]
    local = lax.axis_index("local")
    expert = lax.axis_index("chip") * 2 + lax.axis_index("core")
    steps = hidden // COLS
    copies = []
    for n in range(2 * steps):
        base = (1 - local) * hidden if n < steps else local * hidden
        at = pl.ds(pl.multiple_of(base + (n % steps) * COLS, COLS), COLS)
        copies.append((pltpu.make_async_copy(down_hbm.at[0, at, :], down_ref.at[at, :], sems.at[n]), at))
    gate_copy = pltpu.make_async_copy(
        gate_hbm.at[0, :, 0 : gate_ref.shape[1]], gate_ref, sems.at[2 * steps]
    )
    for copy, _ in copies:
        copy.start()
    gate_copy.start()
    lane = lax.broadcasted_iota(jnp.int32, (count, LANES), 1)
    meta = width // COLS
    for half, ref in enumerate((own_ref, other_ref)):
        at = pl.ds(half * count, count)
        wide[...] = ref[...].astype(F32)
        for i in range(meta):
            rows[at, i * COLS : (i + 1) * COLS] = wide[:, i, 0:COLS].astype(BF16)
        for i in range(feats // LANES):
            grads[at, i * LANES : (i + 1) * LANES] = wide[:, i, COLS:SPAN].astype(BF16)
        both = wide[:, meta, 0:LANES] + wide[:, meta, LANES:COLS]
        both = jnp.sum(jnp.where(lane == expert, both, 0.0), axis=1, keepdims=True)
        weight_out[at, :] = jnp.broadcast_to(both, (count, LANES))
    grad = grads[...]
    for n, (copy, at) in enumerate(copies):
        copy.wait()
        part = dot_nt(grad, down_ref[at, :])
        cols = slice((n % steps) * COLS, (n % steps + 1) * COLS)
        if n < steps:
            away_ref[:, cols] = part.astype(BF16)
        else:
            cot_ref[:, cols] = part
    gate_copy.wait()


def forward_body(
    rows_ref, first_ref, gate_hbm, up_hbm,
    gate_out, up_out, act_ref, second_ref, up_ref,
    sems,
):
    split = first_ref.shape[1]
    hidden = up_ref.shape[1]
    steps = hidden // COLS
    ups, gates = [], []
    for n in range(steps):
        cols = slice(n * COLS, (n + 1) * COLS)
        ups.append(pltpu.make_async_copy(up_hbm.at[0, :, cols], up_ref.at[:, cols], sems.at[n]))
        if n * COLS >= split:
            into = slice(n * COLS - split, (n + 1) * COLS - split)
            gates.append(
                pltpu.make_async_copy(
                    gate_hbm.at[0, :, cols], second_ref.at[:, into], sems.at[steps + n]
                )
            )
        else:
            gates.append(None)
    for n in range(steps):
        ups[n].start()
        if gates[n] is not None:
            gates[n].start()
    tokens = rows_ref[...]
    for n in range(steps):
        cols = slice(n * COLS, (n + 1) * COLS)
        if gates[n] is not None:
            gates[n].wait()
            weight = second_ref[:, n * COLS - split : (n + 1) * COLS - split]
        else:
            weight = first_ref[:, cols]
        gate = dot(tokens, weight)
        ups[n].wait()
        up = dot(tokens, up_ref[:, cols])
        gate_out[:, cols] = gate
        up_out[:, cols] = up
        act_ref[:, cols] = (gate * jax.nn.sigmoid(gate) * up).astype(BF16)


def input_body(
    cot_ref, recv_ref, gate_in, up_in, act_ref, weight_in, first_ref, second_ref, up_ref,
    mine_ref, other_ref,
    wide,
):
    total = cot_ref.shape[0]
    count = total // 2
    width = up_ref.shape[0]
    split = first_ref.shape[1]
    expert = lax.axis_index("chip") * 2 + lax.axis_index("core")
    gate, up = gate_in[...], up_in[...]
    sig = jax.nn.sigmoid(gate)
    cot = cot_ref[...] + recv_ref[...].astype(F32)
    prob = jnp.sum(cot * act_ref[...].astype(F32), axis=1, keepdims=True)
    hidden_grad = cot * weight_in[:, 0:1]
    gate_grad = (hidden_grad * up * sig * (1.0 + gate * (1.0 - sig))).astype(BF16)
    up_grad = (hidden_grad * (gate * sig)).astype(BF16)
    steps = width // COLS
    for n in range(steps):
        at = slice(n * COLS, (n + 1) * COLS)
        wide[:, n, :] = (
            dot_nt(gate_grad[:, :split], first_ref[at, :])
            + dot_nt(gate_grad[:, split:], second_ref[at, :])
            + dot_nt(up_grad, up_ref[at, :])
        )
    lane = lax.broadcasted_iota(jnp.int32, (total, LANES), 1)
    high, low = high_low(jnp.where(lane == expert, prob, 0.0))
    wide[:, steps, 0:LANES] = high
    wide[:, steps, LANES:COLS] = low
    for n in range(steps + 1, ROWS):
        wide[:, n, :] = jnp.zeros((total, COLS), F32)
    mine_ref[...] = wide[:count].astype(BF16)
    other_ref[...] = wide[count:].astype(BF16)


def routed_body(act_ref, recv_ref, weight_in, down_ref, after_ref, mine_ref, other_ref, wide):
    total, hidden = act_ref.shape
    count = total // 2
    feats = down_ref.shape[1]
    local = lax.axis_index("local")
    weight = weight_in[:, 0:1]
    act, recv = act_ref[...], recv_ref[...]
    own = pl.ds(pl.multiple_of(local * hidden, COLS), hidden)
    away = pl.ds(pl.multiple_of((1 - local) * hidden, COLS), hidden)
    for n in range(feats // COLS):
        cols = slice(n * COLS, (n + 1) * COLS)
        part = dot(act, down_ref[own, cols]) + dot(recv, down_ref[away, cols])
        part = part.astype(BF16).astype(F32) * weight
        wide[:, 2 * n, :] = part[:, :LANES]
        wide[:, 2 * n + 1, :] = part[:, LANES:]
    for n in range(feats // LANES, ROWS):
        wide[:, n, :] = jnp.zeros((total, LANES), F32)
    mine_ref[...] = wide[:count].astype(BF16)
    other_ref[...] = wide[count:].astype(BF16)


def final_body(in_ref, ids_ref, comb_ref, grad_ref, prob_ref, wide):
    groups = in_ref.shape[0]
    width = comb_ref.shape[2]
    half = width // 2
    for j in range(2):
        total = in_ref[j].astype(F32)
        for i in range(j + 2, groups, 2):
            total = total + in_ref[i].astype(F32)
        wide[j] = total
    meta = width // COLS
    for c in range(meta):
        grad_ref[0, :, c * COLS : (c + 1) * COLS] = (
            wide[0, c : c + 1, 0:COLS] + wide[1, c : c + 1, 0:COLS]
        ).astype(BF16)
    for j in range(2):
        for c in range(half // LANES):
            at = j * half + c * LANES
            comb_ref[0, :, at : at + LANES] = wide[j, c : c + 1, COLS:SPAN].astype(BF16)
    prob = wide[0, meta : meta + 1, 0:COLS] + wide[1, meta : meta + 1, 0:COLS]
    prob = prob[:, 0:LANES] + prob[:, LANES:COLS]
    lane = lax.broadcasted_iota(jnp.int32, (1, LANES), 1)
    top = ids_ref.shape[2]
    out = jnp.zeros((1, LANES), F32)
    for k in range(top):
        value = jnp.sum(jnp.where(lane == ids_ref[0, 0, k], prob, 0.0), axis=1, keepdims=True)
        out = jnp.where(lane == k, value, out)
    prob_ref[0] = out[:, :top]


def swap(x, axis):
    return lax.ppermute(x, axis, [(0, 1), (1, 0)])


def fast_device(tokens, expert_ids, route_probs, gate_weight, up_weight, down_weight, out_grad):
    groups = lax.axis_size("chip") * 2
    total = 2 * groups
    width = tokens.shape[2]
    hidden = gate_weight.shape[2]
    feats = down_weight.shape[2]
    split = hidden // 2
    one = width * hidden * 2
    gate_hbm, up_hbm, down_hbm = in_hbm(gate_weight, up_weight, down_weight)
    (packed,) = call(
        pack_body,
        [shaped((groups, ROWS, SPAN), BF16)],
        [ANY] * 4,
        [
            pltpu.VMEM((ROWS, SPAN), F32),
            pltpu.SMEM(expert_ids.shape, expert_ids.dtype),
            pltpu.SMEM(route_probs.shape, route_probs.dtype),
            pltpu.VMEM(tokens.shape, BF16),
            pltpu.VMEM(out_grad.shape, BF16),
            pltpu.SemaphoreType.DMA((4,)),
        ],
    )(*in_hbm(expert_ids, route_probs, tokens, out_grad))
    own = lax.all_to_all(packed, ("chip", "local"), split_axis=0, concat_axis=0, tiled=True)
    other = swap(own, "core")
    away, cot, weight, rows, down_w, gate_first = call(
        cot_body,
        [
            shaped((total, hidden), BF16),
            shaped((total, hidden), F32),
            shaped((total, LANES), F32),
            shaped((total, width), BF16),
            pltpu.VMEM((2 * hidden, feats), BF16),
            pltpu.VMEM((width, split), BF16),
        ],
        [VMEM, VMEM, ANY, ANY],
        [
            pltpu.VMEM((groups, ROWS, SPAN), F32),
            pltpu.VMEM((total, feats), BF16),
            pltpu.SemaphoreType.DMA((2 * hidden // COLS + 1,)),
        ],
        products=total * one,
        moved=3 * one // 2,
    )(own, other, down_hbm, gate_hbm)
    cot_recv = swap(away, "local")
    gate, up, act, gate_second, up_w = call(
        forward_body,
        [
            shaped((total, hidden), F32),
            shaped((total, hidden), F32),
            shaped((total, hidden), BF16),
            pltpu.VMEM((width, hidden - split), BF16),
            pltpu.VMEM((width, hidden), BF16),
        ],
        [VMEM, VMEM, ANY, ANY],
        [pltpu.SemaphoreType.DMA((2 * hidden // COLS,))],
        products=total * 2 * one,
        moved=3 * one // 2,
    )(rows, gate_first, gate_hbm, up_hbm)
    act_recv = swap(act, "local")
    in_mine, in_away = call(
        input_body,
        [shaped((groups, ROWS, COLS), BF16)] * 2,
        [VMEM] * 9,
        [pltpu.VMEM((total, ROWS, COLS), F32)],
        products=total * 2 * one,
        moved=2 * one,
    )(cot, cot_recv, gate, up, act, weight, gate_first, gate_second, up_w)
    in_recv = swap(in_away, "core")
    routed_mine, routed_away = call(
        routed_body,
        [shaped((groups, ROWS, LANES), BF16)] * 2,
        [VMEM] * 4 + [ANY],
        [pltpu.VMEM((total, ROWS, LANES), F32)],
        products=total * one,
        moved=one,
    )(act, act_recv, weight, down_w, in_mine)
    routed_recv = swap(routed_away, "core")
    summed = jnp.concatenate(
        [
            (in_mine.astype(F32) + in_recv.astype(F32)).astype(BF16),
            (routed_mine.astype(F32) + routed_recv.astype(F32)).astype(BF16),
        ],
        axis=2,
    )
    back = lax.all_to_all(summed, ("chip", "local"), split_axis=0, concat_axis=0, tiled=True)
    return call(
        final_body,
        [
            shaped((1, 1, width), BF16),
            shaped((1, 1, width), BF16),
            shaped(expert_ids.shape, F32),
        ],
        [VMEM, SMEM],
        [pltpu.VMEM((2, ROWS, SPAN), F32)],
    )(back, expert_ids)


def selector(flags, capacity):
    live = (flags > 0).astype(jnp.int32)
    order = jnp.cumsum(live) - live
    slot_ids = lax.broadcasted_iota(jnp.int32, (capacity, flags.shape[0]), 0)
    return ((slot_ids == order[None, :]) & (live[None, :] > 0)).astype(jnp.bfloat16)


def per_device(tokens, expert_ids, route_probs, gate_weight, up_weight, down_weight, out_grad):
    node_count = lax.axis_size("node")
    token_count = tokens.shape[1]
    width = tokens.shape[2]
    top_count = expert_ids.shape[2]
    column_rows = token_count * node_count
    capacity = min(column_rows, 5 * column_rows * top_count // (2 * node_count))
    slot_count = node_count * token_count
    gate_w = gate_weight[0]
    up_w = up_weight[0]
    down_w = down_weight[0]
    hidden_dev = gate_w.shape[1]
    onehot = (expert_ids[0][..., None] == jnp.arange(node_count, dtype=jnp.int32)).astype(
        jnp.float32
    )
    weights = jnp.einsum("tk,tke->te", route_probs[0], onehot)
    member = jnp.sum(onehot, axis=1)
    own_rows = tokens[0]
    zero_value = jnp.zeros((), jnp.bfloat16)
    own_flags = member.T.astype(jnp.bfloat16)
    send_rows = jnp.where(own_flags[:, :, None] > 0, own_rows[None], zero_value)
    recv_rows, recv_flags = (
        lax.all_to_all(send_rows, "node", split_axis=0, concat_axis=0, tiled=True),
        lax.all_to_all(own_flags, "node", split_axis=0, concat_axis=0, tiled=True),
    )
    select = selector(recv_flags.reshape(slot_count), capacity)
    packed_rows = jnp.dot(
        select, recv_rows.reshape(slot_count, width), preferred_element_type=jnp.float32
    ).astype(jnp.bfloat16)
    piece = lax.all_gather(packed_rows, "local", axis=0, tiled=True)
    gate_part = jnp.dot(piece, gate_w, preferred_element_type=jnp.float32)
    up_part = jnp.dot(piece, up_w, preferred_element_type=jnp.float32)
    joined = jnp.concatenate([gate_part, up_part], axis=1)
    gate_pre = joined[:, :hidden_dev]
    up_pre = joined[:, hidden_dev:]
    sigmoid_gate = jax.nn.sigmoid(gate_pre)
    silu_gate = gate_pre * sigmoid_gate
    hidden = (silu_gate * up_pre).astype(jnp.bfloat16)
    block = down_w
    routed_part = jnp.dot(
        lax.all_gather(hidden, "local", axis=1, tiled=True),
        block,
        preferred_element_type=jnp.float32,
    )
    routed_cols = routed_part.astype(jnp.bfloat16)
    routed_own = lax.all_to_all(routed_cols, "local", split_axis=0, concat_axis=1, tiled=True)
    routed_slots = jnp.dot(select.T, routed_own, preferred_element_type=jnp.float32).astype(
        jnp.bfloat16
    )
    routed_back = lax.all_to_all(
        routed_slots.reshape(node_count, token_count, width),
        "node",
        split_axis=0,
        concat_axis=0,
        tiled=True,
    )
    routed_wide = routed_back.astype(jnp.float32)
    combined = jnp.einsum("te,etd->td", weights, routed_wide).astype(jnp.bfloat16)
    grad_wide = out_grad[0].astype(jnp.float32)
    prob_terms = jnp.einsum("td,etd->te", grad_wide, routed_wide)
    prob_grad = jnp.einsum("te,tke->tk", prob_terms, onehot)
    scaled = (weights.T[:, :, None] * grad_wide[None]).astype(jnp.bfloat16)
    grad_recv = lax.all_to_all(scaled, "node", split_axis=0, concat_axis=0, tiled=True)
    grad_own = jnp.dot(
        select, grad_recv.reshape(slot_count, width), preferred_element_type=jnp.float32
    ).astype(jnp.bfloat16)
    grad_cols = lax.all_to_all(grad_own, "local", split_axis=1, concat_axis=0, tiled=True)
    block = down_w
    hidden_grad = (
        lax.psum_scatter(
            lax.dot_general(
                block, grad_cols, (((1,), (1,)), ((), ())), preferred_element_type=jnp.float32
            ).astype(jnp.bfloat16),
            "local",
            scatter_dimension=0,
            tiled=True,
        )
        .astype(jnp.float32)
        .T
    )
    gate_grad = (
        hidden_grad * up_pre * sigmoid_gate * (1.0 + gate_pre * (1.0 - sigmoid_gate))
    ).astype(jnp.bfloat16)
    up_grad = (hidden_grad * silu_gate).astype(jnp.bfloat16)
    first = lax.dot_general(
        gate_grad, gate_w, (((1,), (1,)), ((), ())), preferred_element_type=jnp.float32
    )
    second = lax.dot_general(
        up_grad, up_w, (((1,), (1,)), ((), ())), preferred_element_type=jnp.float32
    )
    input_own = lax.psum_scatter(
        (first + second).astype(jnp.bfloat16), "local", scatter_dimension=0, tiled=True
    )
    input_slots = jnp.dot(select.T, input_own, preferred_element_type=jnp.float32).astype(
        jnp.bfloat16
    )
    input_back = lax.all_to_all(
        input_slots.reshape(node_count, token_count, width),
        "node",
        split_axis=0,
        concat_axis=0,
        tiled=True,
    )
    input_grad = jnp.sum(input_back.astype(jnp.float32), axis=0).astype(jnp.bfloat16)
    return (combined[None], input_grad[None], prob_grad[None])


def solution(mesh):
    node, local = mesh.shape["node"], mesh.shape["local"]
    if local == 2 and node % 2 == 0 and node <= 16:
        mesh = Mesh(mesh.devices.reshape(node // 2, 2, local), ("chip", "core", "local"))
        body, nodes = fast_device, ("chip", "core")
    else:
        body, nodes = per_device, "node"
    rows = P("local", nodes, None)
    weights = P(nodes, None, "local")
    return jax.shard_map(
        body,
        mesh=mesh,
        in_specs=(rows, rows, rows, weights, weights, weights, rows),
        out_specs=(rows, rows, rows),
        check_vma=False,
    )
```

```python
import functools
import math

import jax
import jax.numpy as jnp
from jax import lax
from jax.experimental import pallas as pl
from jax.experimental.pallas import tpu as pltpu
from jax.sharding import Mesh
from jax.sharding import PartitionSpec as P

BF16 = jnp.bfloat16
F32 = jnp.float32
LANES = 128
COLS = 256
ROWS = 16
SPAN = COLS + LANES
TAKE = 2 * COLS

NT = (((1,), (1,)), ((), ()))
VMEM = pl.BlockSpec(memory_space=pltpu.VMEM)
ANY = pl.BlockSpec(memory_space=pl.ANY)
SMEM = pl.BlockSpec(memory_space=pltpu.SMEM)


def call(body, outs, ins, scratch=(), products=0, moved=0):
    return pl.pallas_call(
        body,
        out_shape=tuple(outs),
        in_specs=ins,
        out_specs=tuple(VMEM for _ in outs),
        scratch_shapes=list(scratch),
        compiler_params=pltpu.CompilerParams(vmem_limit_bytes=12 << 20),
        cost_estimate=pl.CostEstimate(
            flops=int(products), bytes_accessed=int(moved), transcendentals=0
        ),
    )


def shaped(shape, dtype):
    return jax.ShapeDtypeStruct(shape, dtype)


def in_hbm(*arrays):
    return tuple(pltpu.with_memory_space_constraint(a, pltpu.HBM) for a in arrays)


def dot(a, b):
    return jnp.dot(a, b, preferred_element_type=F32)


def dot_nt(a, b):
    return lax.dot_general(a, b, NT, preferred_element_type=F32)


def high_low(x):
    high = x.astype(BF16).astype(F32)
    return high, x - high


def pack_body(
    ids_hbm, probs_hbm, tok_hbm, grad_hbm, out_ref, wide, ids_ref, probs_ref, tok_ref, grad_ref, sems
):
    pairs = ((ids_hbm, ids_ref), (probs_hbm, probs_ref), (tok_hbm, tok_ref), (grad_hbm, grad_ref))
    copies = [pltpu.make_async_copy(a, b, sems.at[i]) for i, (a, b) in enumerate(pairs)]
    for copy in copies:
        copy.start()
    wide[...] = jnp.zeros_like(wide)
    lane = lax.broadcasted_iota(jnp.int32, (1, LANES), 1)
    weight = jnp.zeros((1, LANES), F32)
    for copy in copies:
        copy.wait()
    for k in range(ids_ref.shape[2]):
        weight = jnp.where(lane == ids_ref[0, 0, k], probs_ref[0, 0, k], weight)
    width = tok_ref.shape[2]
    meta = width // COLS
    half = width // 2
    for i in range(meta):
        wide[i : i + 1, 0:COLS] = tok_ref[0, :, i * COLS : (i + 1) * COLS].astype(F32)
    high, low = high_low(weight)
    wide[meta : meta + 1, 0:LANES] = high
    wide[meta : meta + 1, LANES:COLS] = low
    for j in range(2):
        cols = slice(COLS + j * LANES, COLS + (j + 1) * LANES)
        for i in range(half // LANES):
            at = j * half + i * LANES
            wide[i : i + 1, cols] = grad_ref[0, :, at : at + LANES].astype(F32)
    out_ref[0] = wide[...].astype(BF16)


def load_body(*refs, parts):
    count = len(parts)
    sems = refs[-1]
    copies = []
    for i, (rows, cols) in enumerate(parts):
        src = refs[i].at[0, slice(*rows), slice(*cols)]
        copies.append(pltpu.make_async_copy(src, refs[count + 1 + i], sems.at[i]))
    for copy in copies:
        copy.start()
    refs[-2][...] = jnp.zeros_like(refs[-2])
    for copy in copies:
        copy.wait()


def load(parts, after):
    bounds = tuple((rows, cols) for _, rows, cols in parts)
    shapes = [(r[1] - r[0], c[1] - c[0]) for r, c in bounds]
    return call(
        functools.partial(load_body, parts=bounds),
        [pltpu.VMEM(shape, BF16) for shape in shapes] + [pltpu.VMEM((8, LANES), F32)],
        [ANY] * (len(parts) + 1),
        [pltpu.SemaphoreType.DMA((len(parts),))],
        moved=sum(4 * a * b for a, b in shapes),
    )(*(w for w, _, _ in parts), after)


def cot_body(
    rows_in, low_ref, high_ref, *refs
):
    away_ref, cot_ref, weight_out, rows, wide, grads = refs[-6:]
    total = rows_in.shape[0]
    width = rows.shape[1]
    hidden = cot_ref.shape[1]
    feats = low_ref.shape[1]
    local = lax.axis_index("local")
    expert = lax.axis_index("chip") * 2 + lax.axis_index("core")
    lane = lax.broadcasted_iota(jnp.int32, (total, LANES), 1)
    meta = width // COLS
    wide[...] = rows_in[...].astype(F32)
    side = pl.ds(pl.multiple_of(COLS + local * LANES, LANES), LANES)
    for i in range(feats // LANES):
        grads[:, i * LANES : (i + 1) * LANES] = wide[:, i, side].astype(BF16)
    grad = grads[...]

    def products(own, away):
        for n in range(hidden // COLS):
            at = slice(n * COLS, (n + 1) * COLS)
            away_ref[:, at] = dot_nt(grad, away[at, :]).astype(BF16)
        for n in range(hidden // COLS):
            at = slice(n * COLS, (n + 1) * COLS)
            cot_ref[:, at] = dot_nt(grad, own[at, :])

    @pl.when(local == 0)
    def _():
        products(low_ref, high_ref)

    @pl.when(local == 1)
    def _():
        products(high_ref, low_ref)

    for i in range(meta):
        rows[:, i * COLS : (i + 1) * COLS] = wide[:, i, 0:COLS].astype(BF16)
    both = wide[:, meta, 0:LANES] + wide[:, meta, LANES:COLS]
    both = jnp.sum(jnp.where(lane == expert, both, 0.0), axis=1, keepdims=True)
    weight_out[...] = jnp.broadcast_to(both, (total, LANES))


def forward_body(rows_ref, gate_first, gate_second, up_first, up_second, gate_out, up_out, act_ref):
    split = gate_first.shape[1]
    hidden = act_ref.shape[1]
    tokens = rows_ref[...]
    for n in range(hidden // COLS):
        cols = slice(n * COLS, (n + 1) * COLS)
        if n * COLS < split:
            gate, up = dot(tokens, gate_first[:, cols]), dot(tokens, up_first[:, cols])
        else:
            at = slice(n * COLS - split, (n + 1) * COLS - split)
            gate, up = dot(tokens, gate_second[:, at]), dot(tokens, up_second[:, at])
        gate_out[:, cols] = gate
        up_out[:, cols] = up
        act_ref[:, cols] = (gate * jax.nn.sigmoid(gate) * up).astype(BF16)


def place(ref, block):
    count = ref.shape[0]
    chip, local = lax.axis_index("chip"), lax.axis_index("local")
    for r in range(count):
        step = r % (count // 2)
        chip_to = jnp.bitwise_xor(chip, arrival(step, count // 2))
        local_to = jnp.bitwise_xor(local, r // (count // 2))
        ref[chip_to * 2 + local_to] = block(r).astype(BF16)


def crossed(x):
    size = x.shape[0] // 4
    return jnp.concatenate([x[i * size : (i + 1) * size] for i in (1, 0, 3, 2)], axis=0)


def arrival(step, chips):
    return sum(mask for i, mask in enumerate(chip_masks(chips)) if step >> i & 1)


def chip_masks(chips):
    masks, bit = [], 1
    while bit < chips:
        masks.append(bit)
        bit *= 2
    return masks[1:] + masks[:1]


def input_body(
    cot_ref, recv_ref, gate_in, up_in, act_ref, weight_in,
    gate_first, gate_second, up_first, up_second,
    mine_ref, other_ref,
    wide,
):
    total = cot_ref.shape[0]
    count = total // 2
    width, split = gate_first.shape
    expert = lax.axis_index("chip") * 2 + lax.axis_index("core")
    gate, up = gate_in[...], up_in[...]
    sig = jax.nn.sigmoid(gate)
    cot = cot_ref[...] + crossed(recv_ref[...].astype(F32))
    prob = jnp.sum(cot * act_ref[...].astype(F32), axis=1, keepdims=True)
    hidden_grad = cot * weight_in[:, 0:1]
    gate_grad = (hidden_grad * up * sig * (1.0 + gate * (1.0 - sig))).astype(BF16)
    up_grad = (hidden_grad * (gate * sig)).astype(BF16)
    steps = width // COLS
    for n in range(steps):
        at = slice(n * COLS, (n + 1) * COLS)
        wide[:, n, :] = (
            dot_nt(gate_grad[:, :split], gate_first[at, :])
            + dot_nt(gate_grad[:, split:], gate_second[at, :])
            + dot_nt(up_grad[:, :split], up_first[at, :])
            + dot_nt(up_grad[:, split:], up_second[at, :])
        )
    lane = lax.broadcasted_iota(jnp.int32, (total, LANES), 1)
    high, low = high_low(jnp.where(lane == expert, prob, 0.0))
    wide[:, steps, 0:LANES] = high
    wide[:, steps, LANES:COLS] = low
    for n in range(steps + 1, ROWS):
        wide[:, n, :] = jnp.zeros((total, COLS), F32)
    place(mine_ref, lambda r: wide[r])
    place(other_ref, lambda r: wide[count + r])


def routed_body(act_ref, recv_ref, weight_in, low_ref, high_ref, after_ref, mine_ref, other_ref, wide):
    total, hidden = act_ref.shape
    count = total // 2
    feats = low_ref.shape[1]
    local = lax.axis_index("local")
    weight = weight_in[:, 0:1]
    act, recv = act_ref[...], crossed(recv_ref[...].astype(F32)).astype(BF16)
    low = jnp.where(local == 0, act, recv)
    high = jnp.where(local == 0, recv, act)
    for n in range(feats // COLS):
        cols = slice(n * COLS, (n + 1) * COLS)
        part = dot(low, low_ref[:, cols]) + dot(high, high_ref[:, cols])
        part = part.astype(BF16).astype(F32) * weight
        wide[:, 2 * n, :] = part[:, :LANES]
        wide[:, 2 * n + 1, :] = part[:, LANES:]
    for n in range(feats // LANES, ROWS):
        wide[:, n, :] = jnp.zeros((total, LANES), F32)
    place(mine_ref, lambda r: wide[r])
    place(other_ref, lambda r: wide[count + r])


def final_body(in_ref, ids_ref, comb_ref, grad_ref, prob_ref, wide):
    groups = in_ref.shape[0]
    width = comb_ref.shape[2]
    half = width // 2
    for j in range(2):
        total = in_ref[j].astype(F32)
        for i in range(j + 2, groups, 2):
            total = total + in_ref[i].astype(F32)
        wide[j] = total
    meta = width // COLS
    for c in range(meta):
        grad_ref[0, :, c * COLS : (c + 1) * COLS] = (
            wide[0, c : c + 1, 0:COLS] + wide[1, c : c + 1, 0:COLS]
        ).astype(BF16)
    for j in range(2):
        for c in range(half // LANES):
            at = j * half + c * LANES
            comb_ref[0, :, at : at + LANES] = wide[j, c : c + 1, COLS:SPAN].astype(BF16)
    prob = wide[0, meta : meta + 1, 0:COLS] + wide[1, meta : meta + 1, 0:COLS]
    prob = prob[:, 0:LANES] + prob[:, LANES:COLS]
    lane = lax.broadcasted_iota(jnp.int32, (1, LANES), 1)
    top = ids_ref.shape[2]
    out = jnp.zeros((1, LANES), F32)
    for k in range(top):
        value = jnp.sum(jnp.where(lane == ids_ref[0, 0, k], prob, 0.0), axis=1, keepdims=True)
        out = jnp.where(lane == k, value, out)
    prob_ref[0] = out[:, :top]


def swap(x, axis):
    return lax.ppermute(x, axis, [(0, 1), (1, 0)])


def trade(x, mask):
    axes = ("chip", "core", "local")
    size = math.prod(lax.axis_size(axis) for axis in axes)
    return lax.ppermute(x, axes, [(i, i ^ mask) for i in range(size)])


def fast_device(tokens, expert_ids, route_probs, gate_weight, up_weight, down_weight, out_grad):
    chips = lax.axis_size("chip")
    groups = chips * 2
    total = 2 * groups
    width = tokens.shape[2]
    hidden = gate_weight.shape[2]
    feats = down_weight.shape[2]
    split = hidden // 2
    one = width * hidden * 2
    gate_hbm, up_hbm, down_hbm = in_hbm(gate_weight, up_weight, down_weight)
    (packed,) = call(
        pack_body,
        [shaped((1, ROWS, TAKE), BF16)],
        [ANY] * 4,
        [
            pltpu.VMEM((ROWS, TAKE), F32),
            pltpu.SMEM(expert_ids.shape, expert_ids.dtype),
            pltpu.SMEM(route_probs.shape, route_probs.dtype),
            pltpu.VMEM(tokens.shape, BF16),
            pltpu.VMEM(out_grad.shape, BF16),
            pltpu.SemaphoreType.DMA((4,)),
        ],
    )(*in_hbm(expert_ids, route_probs, tokens, out_grad))
    first, second = (0, split), (split, hidden)
    pieces = [
        (down_hbm, (0, hidden), (0, feats)),
        (down_hbm, (hidden, 2 * hidden), (0, feats)),
        (gate_hbm, (0, width), first),
        (gate_hbm, (0, width), second),
        (up_hbm, (0, width), first),
        (up_hbm, (0, width), second),
    ]
    masks = [4 * mask for mask in chip_masks(chips)] + [1, 2]
    loaded, gathered, after = [], packed, []
    for step, mask in enumerate(masks):
        left = len(masks) - step
        take = -(-len(pieces) // left) if step >= len(masks) - 2 else min(1, len(pieces))
        moved = trade(gathered, mask)
        *parts, token = load(pieces[:take], gathered)
        pieces = pieces[take:]
        loaded += parts
        after.append(token)
        gathered = jnp.concatenate([gathered, moved], axis=0)
        gathered, after[-1] = lax.optimization_barrier((gathered, after[-1]))
    down_low, down_high, gate_first, gate_second, up_first, up_second = loaded
    away, cot, weight, rows = call(
        cot_body,
        [
            shaped((total, hidden), BF16),
            shaped((total, hidden), F32),
            shaped((total, LANES), F32),
            shaped((total, width), BF16),
        ],
        [VMEM] * 3 + [ANY] * len(after),
        [
            pltpu.VMEM((total, ROWS, TAKE), F32),
            pltpu.VMEM((total, feats), BF16),
        ],
        products=total * one,
        moved=one,
    )(gathered, down_low, down_high, *after)
    cot_recv = swap(away, "local")
    gate, up, act = call(
        forward_body,
        [
            shaped((total, hidden), F32),
            shaped((total, hidden), F32),
            shaped((total, hidden), BF16),
        ],
        [VMEM] * 5,
        products=total * 2 * one,
        moved=2 * one,
    )(rows, gate_first, gate_second, up_first, up_second)
    act_recv = swap(act, "local")
    in_mine, in_away = call(
        input_body,
        [shaped((groups, ROWS, COLS), BF16)] * 2,
        [VMEM] * 10,
        [pltpu.VMEM((total, ROWS, COLS), F32)],
        products=total * 2 * one,
        moved=2 * one,
    )(cot, cot_recv, gate, up, act, weight, gate_first, gate_second, up_first, up_second)
    in_recv = swap(in_away, "core")
    routed_mine, routed_away = call(
        routed_body,
        [shaped((groups, ROWS, LANES), BF16)] * 2,
        [VMEM] * 5 + [ANY],
        [pltpu.VMEM((total, ROWS, LANES), F32)],
        products=total * one,
        moved=one,
    )(act, act_recv, weight, down_low, down_high, in_mine)
    routed_recv = swap(routed_away, "core")
    summed = jnp.concatenate(
        [
            (in_mine.astype(F32) + in_recv.astype(F32)).astype(BF16),
            (routed_mine.astype(F32) + routed_recv.astype(F32)).astype(BF16),
        ],
        axis=2,
    )
    back = lax.all_to_all(summed, ("chip", "local"), split_axis=0, concat_axis=0, tiled=True)
    return call(
        final_body,
        [
            shaped((1, 1, width), BF16),
            shaped((1, 1, width), BF16),
            shaped(expert_ids.shape, F32),
        ],
        [VMEM, SMEM],
        [pltpu.VMEM((2, ROWS, SPAN), F32)],
    )(back, expert_ids)


def selector(flags, capacity):
    live = (flags > 0).astype(jnp.int32)
    order = jnp.cumsum(live) - live
    slot_ids = lax.broadcasted_iota(jnp.int32, (capacity, flags.shape[0]), 0)
    return ((slot_ids == order[None, :]) & (live[None, :] > 0)).astype(jnp.bfloat16)


def per_device(tokens, expert_ids, route_probs, gate_weight, up_weight, down_weight, out_grad):
    node_count = lax.axis_size("node")
    token_count = tokens.shape[1]
    width = tokens.shape[2]
    top_count = expert_ids.shape[2]
    column_rows = token_count * node_count
    capacity = min(column_rows, 5 * column_rows * top_count // (2 * node_count))
    slot_count = node_count * token_count
    gate_w = gate_weight[0]
    up_w = up_weight[0]
    down_w = down_weight[0]
    hidden_dev = gate_w.shape[1]
    onehot = (expert_ids[0][..., None] == jnp.arange(node_count, dtype=jnp.int32)).astype(
        jnp.float32
    )
    weights = jnp.einsum("tk,tke->te", route_probs[0], onehot)
    member = jnp.sum(onehot, axis=1)
    own_rows = tokens[0]
    zero_value = jnp.zeros((), jnp.bfloat16)
    own_flags = member.T.astype(jnp.bfloat16)
    send_rows = jnp.where(own_flags[:, :, None] > 0, own_rows[None], zero_value)
    recv_rows, recv_flags = (
        lax.all_to_all(send_rows, "node", split_axis=0, concat_axis=0, tiled=True),
        lax.all_to_all(own_flags, "node", split_axis=0, concat_axis=0, tiled=True),
    )
    select = selector(recv_flags.reshape(slot_count), capacity)
    packed_rows = jnp.dot(
        select, recv_rows.reshape(slot_count, width), preferred_element_type=jnp.float32
    ).astype(jnp.bfloat16)
    piece = lax.all_gather(packed_rows, "local", axis=0, tiled=True)
    gate_part = jnp.dot(piece, gate_w, preferred_element_type=jnp.float32)
    up_part = jnp.dot(piece, up_w, preferred_element_type=jnp.float32)
    joined = jnp.concatenate([gate_part, up_part], axis=1)
    gate_pre = joined[:, :hidden_dev]
    up_pre = joined[:, hidden_dev:]
    sigmoid_gate = jax.nn.sigmoid(gate_pre)
    silu_gate = gate_pre * sigmoid_gate
    hidden = (silu_gate * up_pre).astype(jnp.bfloat16)
    block = down_w
    routed_part = jnp.dot(
        lax.all_gather(hidden, "local", axis=1, tiled=True),
        block,
        preferred_element_type=jnp.float32,
    )
    routed_cols = routed_part.astype(jnp.bfloat16)
    routed_own = lax.all_to_all(routed_cols, "local", split_axis=0, concat_axis=1, tiled=True)
    routed_slots = jnp.dot(select.T, routed_own, preferred_element_type=jnp.float32).astype(
        jnp.bfloat16
    )
    routed_back = lax.all_to_all(
        routed_slots.reshape(node_count, token_count, width),
        "node",
        split_axis=0,
        concat_axis=0,
        tiled=True,
    )
    routed_wide = routed_back.astype(jnp.float32)
    combined = jnp.einsum("te,etd->td", weights, routed_wide).astype(jnp.bfloat16)
    grad_wide = out_grad[0].astype(jnp.float32)
    prob_terms = jnp.einsum("td,etd->te", grad_wide, routed_wide)
    prob_grad = jnp.einsum("te,tke->tk", prob_terms, onehot)
    scaled = (weights.T[:, :, None] * grad_wide[None]).astype(jnp.bfloat16)
    grad_recv = lax.all_to_all(scaled, "node", split_axis=0, concat_axis=0, tiled=True)
    grad_own = jnp.dot(
        select, grad_recv.reshape(slot_count, width), preferred_element_type=jnp.float32
    ).astype(jnp.bfloat16)
    grad_cols = lax.all_to_all(grad_own, "local", split_axis=1, concat_axis=0, tiled=True)
    block = down_w
    hidden_grad = (
        lax.psum_scatter(
            lax.dot_general(
                block, grad_cols, (((1,), (1,)), ((), ())), preferred_element_type=jnp.float32
            ).astype(jnp.bfloat16),
            "local",
            scatter_dimension=0,
            tiled=True,
        )
        .astype(jnp.float32)
        .T
    )
    gate_grad = (
        hidden_grad * up_pre * sigmoid_gate * (1.0 + gate_pre * (1.0 - sigmoid_gate))
    ).astype(jnp.bfloat16)
    up_grad = (hidden_grad * silu_gate).astype(jnp.bfloat16)
    first = lax.dot_general(
        gate_grad, gate_w, (((1,), (1,)), ((), ())), preferred_element_type=jnp.float32
    )
    second = lax.dot_general(
        up_grad, up_w, (((1,), (1,)), ((), ())), preferred_element_type=jnp.float32
    )
    input_own = lax.psum_scatter(
        (first + second).astype(jnp.bfloat16), "local", scatter_dimension=0, tiled=True
    )
    input_slots = jnp.dot(select.T, input_own, preferred_element_type=jnp.float32).astype(
        jnp.bfloat16
    )
    input_back = lax.all_to_all(
        input_slots.reshape(node_count, token_count, width),
        "node",
        split_axis=0,
        concat_axis=0,
        tiled=True,
    )
    input_grad = jnp.sum(input_back.astype(jnp.float32), axis=0).astype(jnp.bfloat16)
    return (combined[None], input_grad[None], prob_grad[None])


def solution(mesh):
    node, local = mesh.shape["node"], mesh.shape["local"]
    if local == 2 and node % 2 == 0 and node <= 16:
        mesh = Mesh(mesh.devices.reshape(node // 2, 2, local), ("chip", "core", "local"))
        body, nodes = fast_device, ("chip", "core")
    else:
        body, nodes = per_device, "node"
    rows = P("local", nodes, None)
    weights = P(nodes, None, "local")
    return jax.shard_map(
        body,
        mesh=mesh,
        in_specs=(rows, rows, rows, weights, weights, weights, rows),
        out_specs=(rows, rows, rows),
        check_vma=False,
    )
```

```python
import functools

import jax
import jax.numpy as jnp
from jax import lax
from jax.experimental import pallas as pl
from jax.experimental.pallas import tpu as pltpu
from jax.sharding import Mesh
from jax.sharding import PartitionSpec as P

BF16 = jnp.bfloat16
F32 = jnp.float32
LANES = 128
COLS = 256
DEPTH = 512
ROWS = 16
SPAN = COLS + LANES

NT = (((1,), (1,)), ((), ()))
VMEM = pl.BlockSpec(memory_space=pltpu.VMEM)
ANY = pl.BlockSpec(memory_space=pl.ANY)
SMEM = pl.BlockSpec(memory_space=pltpu.SMEM)


def call(body, outs, ins, scratch=(), products=0, moved=0):
    return pl.pallas_call(
        body,
        out_shape=tuple(outs),
        in_specs=ins,
        out_specs=tuple(VMEM for _ in outs),
        scratch_shapes=list(scratch),
        compiler_params=pltpu.CompilerParams(vmem_limit_bytes=12 << 20),
        cost_estimate=pl.CostEstimate(
            flops=int(products), bytes_accessed=int(moved), transcendentals=0
        ),
    )


def shaped(shape, dtype):
    return jax.ShapeDtypeStruct(shape, dtype)


def in_hbm(*arrays):
    return tuple(pltpu.with_memory_space_constraint(a, pltpu.HBM) for a in arrays)


def dot(a, b):
    return jnp.dot(a, b, preferred_element_type=F32)


def dot_nt(a, b):
    return lax.dot_general(a, b, NT, preferred_element_type=F32)


def from_rows(weight, turned):
    return dot(weight, turned).T


def high_low(x):
    high = x.astype(BF16).astype(F32)
    return high, x - high


def pack_body(
    ids_hbm, probs_hbm, tok_hbm, grad_hbm, out_ref, wide, ids_ref, probs_ref, tok_ref, grad_ref, sems
):
    pairs = ((ids_hbm, ids_ref), (probs_hbm, probs_ref), (tok_hbm, tok_ref), (grad_hbm, grad_ref))
    copies = [pltpu.make_async_copy(a, b, sems.at[i]) for i, (a, b) in enumerate(pairs)]
    for copy in copies:
        copy.start()
    wide[...] = jnp.zeros_like(wide)
    lane = lax.broadcasted_iota(jnp.int32, (1, LANES), 1)
    weight = jnp.zeros((1, LANES), F32)
    for copy in copies:
        copy.wait()
    for k in range(ids_ref.shape[2]):
        weight = jnp.where(lane == ids_ref[0, 0, k], probs_ref[0, 0, k], weight)
    width = tok_ref.shape[2]
    meta = width // COLS
    half = width // 2
    for i in range(meta):
        wide[i : i + 1, 0:COLS] = tok_ref[0, :, i * COLS : (i + 1) * COLS].astype(F32)
    high, low = high_low(weight)
    wide[meta : meta + 1, 0:LANES] = high
    wide[meta : meta + 1, LANES:COLS] = low
    for j in range(2):
        for i in range(half // LANES):
            at = j * half + i * LANES
            wide[i : i + 1, COLS:SPAN] = grad_ref[0, :, at : at + LANES].astype(F32)
        block = wide[...].astype(BF16)
        for i in range(j, out_ref.shape[0], 2):
            out_ref[i] = block


def side_rows(local, hidden, n):
    return pl.ds(pl.multiple_of(local * hidden + n * COLS, COLS), COLS)


def load_body(down_hbm, after_ref, away_ref, token_ref, sems):
    hidden = away_ref.shape[0]
    away = 1 - lax.axis_index("local")
    copies = [
        pltpu.make_async_copy(
            down_hbm.at[0, side_rows(away, hidden, n), :],
            away_ref.at[n * COLS : (n + 1) * COLS, :],
            sems.at[n],
        )
        for n in range(hidden // COLS)
    ]
    for copy in copies:
        copy.start()
    token_ref[...] = jnp.zeros_like(token_ref)
    for copy in copies:
        copy.wait()


def cot_body(
    own_ref, other_ref, loaded_ref, after_ref, down_hbm, gate_hbm,
    away_ref, cot_ref, weight_out, rows, down_ref, gate_ref,
    wide, grads, sems,
):
    count = own_ref.shape[0]
    width = rows.shape[1]
    hidden = cot_ref.shape[1]
    feats = down_ref.shape[1]
    local = lax.axis_index("local")
    expert = lax.axis_index("chip") * 2 + lax.axis_index("core")
    steps = hidden // COLS
    copies = []
    for n in range(steps):
        into = down_ref.at[n * COLS : (n + 1) * COLS, :]
        copies.append(
            pltpu.make_async_copy(down_hbm.at[0, side_rows(local, hidden, n), :], into, sems.at[n])
        )
    for n in range(width // DEPTH):
        at = slice(n * DEPTH, (n + 1) * DEPTH)
        copies.append(
            pltpu.make_async_copy(gate_hbm.at[0, at, :], gate_ref.at[at, :], sems.at[steps + n])
        )
    for copy in copies:
        copy.start()

    lane = lax.broadcasted_iota(jnp.int32, (count, LANES), 1)
    meta = width // COLS
    for half, ref in enumerate((own_ref, other_ref)):
        at = pl.ds(half * count, count)
        wide[...] = ref[...].astype(F32)
        for i in range(feats // LANES):
            grads[at, i * LANES : (i + 1) * LANES] = wide[:, i, COLS:SPAN].astype(BF16)
        for i in range(meta):
            rows[at, i * COLS : (i + 1) * COLS] = wide[:, i, 0:COLS].astype(BF16)
        both = wide[:, meta, 0:LANES] + wide[:, meta, LANES:COLS]
        both = jnp.sum(jnp.where(lane == expert, both, 0.0), axis=1, keepdims=True)
        weight_out[at, :] = jnp.broadcast_to(both, (count, LANES))
    grad = grads[...].T
    for n in range(steps):
        at = slice(n * COLS, (n + 1) * COLS)
        away_ref[:, at] = from_rows(loaded_ref[at, :], grad).astype(BF16)
    for n in range(steps):
        at = slice(n * COLS, (n + 1) * COLS)
        copies[n].wait()
        cot_ref[:, at] = from_rows(down_ref[at, :], grad)
    for copy in copies[steps:]:
        copy.wait()


def forward_body(rows_ref, gate_ref, up_hbm, gate_out, up_out, act_ref, up_ref, sems):
    width, hidden = gate_ref.shape
    pieces = [slice(n * DEPTH, (n + 1) * DEPTH) for n in range(width // DEPTH)]
    columns = [slice(n * COLS, (n + 1) * COLS) for n in range(hidden // COLS)]
    copies = [
        pltpu.make_async_copy(up_hbm.at[0, at, :], up_ref.at[at, :], sems.at[n])
        for n, at in enumerate(pieces)
    ]
    for copy in copies:
        copy.start()
    for cols in columns:
        gate_out[:, cols] = dot(rows_ref[...], gate_ref[:, cols])
    for n, at in enumerate(pieces):
        copies[n].wait()
        for cols in columns:
            part = dot(rows_ref[:, at], up_ref[at, cols])
            up_out[:, cols] = part if n == 0 else up_out[:, cols] + part
    for cols in columns:
        gate = gate_out[:, cols]
        act_ref[:, cols] = (gate * jax.nn.sigmoid(gate) * up_out[:, cols]).astype(BF16)


def input_body(
    cot_ref, recv_ref, gate_in, up_in, act_ref, weight_in, gate_ref, up_ref,
    mine_ref, other_ref,
    wide,
):
    total = cot_ref.shape[0]
    count = total // 2
    width = up_ref.shape[0]
    expert = lax.axis_index("chip") * 2 + lax.axis_index("core")
    gate, up = gate_in[...], up_in[...]
    sig = jax.nn.sigmoid(gate)
    cot = cot_ref[...] + recv_ref[...].astype(F32)
    prob = jnp.sum(cot * act_ref[...].astype(F32), axis=1, keepdims=True)
    hidden_grad = cot * weight_in[:, 0:1]
    gate_grad = (hidden_grad * up * sig * (1.0 + gate * (1.0 - sig))).astype(BF16)
    up_grad = (hidden_grad * (gate * sig)).astype(BF16)
    gate_turned, up_turned = gate_grad.T, up_grad.T
    steps = width // COLS
    for n in range(steps):
        at = slice(n * COLS, (n + 1) * COLS)
        wide[:, n, :] = (dot(gate_ref[at, :], gate_turned) + dot(up_ref[at, :], up_turned)).T
    lane = lax.broadcasted_iota(jnp.int32, (total, LANES), 1)
    high, low = high_low(jnp.where(lane == expert, prob, 0.0))
    wide[:, steps, 0:LANES] = high
    wide[:, steps, LANES:COLS] = low
    for n in range(steps + 1, ROWS):
        wide[:, n, :] = jnp.zeros((total, COLS), F32)
    mine_ref[...] = wide[:count].astype(BF16)
    other_ref[...] = wide[count:].astype(BF16)


def routed_body(
    act_ref, recv_ref, weight_in, own_ref, away_ref, after_ref, mine_ref, other_ref, wide
):
    total = act_ref.shape[0]
    count = total // 2
    feats = own_ref.shape[1]
    weight = weight_in[:, 0:1]
    act, recv = act_ref[...], recv_ref[...]
    for n in range(feats // COLS):
        cols = slice(n * COLS, (n + 1) * COLS)
        part = dot(act, own_ref[:, cols]) + dot(recv, away_ref[:, cols])
        part = part.astype(BF16).astype(F32) * weight
        wide[:, 2 * n, :] = part[:, :LANES]
        wide[:, 2 * n + 1, :] = part[:, LANES:]
    for n in range(feats // LANES, ROWS):
        wide[:, n, :] = jnp.zeros((total, LANES), F32)
    mine_ref[...] = wide[:count].astype(BF16)
    other_ref[...] = wide[count:].astype(BF16)


def final_body(in_ref, ids_ref, comb_ref, grad_ref, prob_ref, wide):
    groups = in_ref.shape[0]
    width = comb_ref.shape[2]
    half = width // 2
    for j in range(2):
        total = in_ref[j].astype(F32)
        for i in range(j + 2, groups, 2):
            total = total + in_ref[i].astype(F32)
        wide[j] = total
    meta = width // COLS
    for c in range(meta):
        grad_ref[0, :, c * COLS : (c + 1) * COLS] = (
            wide[0, c : c + 1, 0:COLS] + wide[1, c : c + 1, 0:COLS]
        ).astype(BF16)
    for j in range(2):
        for c in range(half // LANES):
            at = j * half + c * LANES
            comb_ref[0, :, at : at + LANES] = wide[j, c : c + 1, COLS:SPAN].astype(BF16)
    prob = wide[0, meta : meta + 1, 0:COLS] + wide[1, meta : meta + 1, 0:COLS]
    prob = prob[:, 0:LANES] + prob[:, LANES:COLS]
    lane = lax.broadcasted_iota(jnp.int32, (1, LANES), 1)
    top = ids_ref.shape[2]
    out = jnp.zeros((1, LANES), F32)
    for k in range(top):
        value = jnp.sum(jnp.where(lane == ids_ref[0, 0, k], prob, 0.0), axis=1, keepdims=True)
        out = jnp.where(lane == k, value, out)
    prob_ref[0] = out[:, :top]


def swap(x, axis):
    return lax.ppermute(x, axis, [(0, 1), (1, 0)])


def fast_device(tokens, expert_ids, route_probs, gate_weight, up_weight, down_weight, out_grad):
    groups = lax.axis_size("chip") * 2
    total = 2 * groups
    width = tokens.shape[2]
    hidden = gate_weight.shape[2]
    feats = down_weight.shape[2]
    one = width * hidden * 2
    gate_hbm, up_hbm, down_hbm = in_hbm(gate_weight, up_weight, down_weight)
    (packed,) = call(
        pack_body,
        [shaped((groups, ROWS, SPAN), BF16)],
        [ANY] * 4,
        [
            pltpu.VMEM((ROWS, SPAN), F32),
            pltpu.SMEM(expert_ids.shape, expert_ids.dtype),
            pltpu.SMEM(route_probs.shape, route_probs.dtype),
            pltpu.VMEM(tokens.shape, BF16),
            pltpu.VMEM(out_grad.shape, BF16),
            pltpu.SemaphoreType.DMA((4,)),
        ],
    )(*in_hbm(expert_ids, route_probs, tokens, out_grad))
    own = lax.all_to_all(packed, ("chip", "local"), split_axis=0, concat_axis=0, tiled=True)
    other = swap(own, "core")
    down_away, loaded = call(
        load_body,
        [pltpu.VMEM((hidden, feats), BF16), pltpu.VMEM((8, LANES), F32)],
        [ANY, ANY],
        [pltpu.SemaphoreType.DMA((hidden // COLS,))],
        moved=one,
    )(down_hbm, own)
    away, cot, weight, rows, down_own, gate_w = call(
        cot_body,
        [
            shaped((total, hidden), BF16),
            shaped((total, hidden), F32),
            shaped((total, LANES), F32),
            shaped((total, width), BF16),
            pltpu.VMEM((hidden, feats), BF16),
            pltpu.VMEM((width, hidden), BF16),
        ],
        [VMEM, VMEM, VMEM, ANY, ANY, ANY],
        [
            pltpu.VMEM((groups, ROWS, SPAN), F32),
            pltpu.VMEM((total, feats), BF16),
            pltpu.SemaphoreType.DMA((hidden // COLS + width // DEPTH,)),
        ],
        products=total * one,
        moved=2 * one,
    )(own, other, down_away, loaded, down_hbm, gate_hbm)
    cot_recv = swap(away, "local")
    gate, up, act, up_w = call(
        forward_body,
        [
            shaped((total, hidden), F32),
            shaped((total, hidden), F32),
            shaped((total, hidden), BF16),
            pltpu.VMEM((width, hidden), BF16),
        ],
        [VMEM, VMEM, ANY],
        [pltpu.SemaphoreType.DMA((width // DEPTH,))],
        products=total * 2 * one,
        moved=3 * one // 2,
    )(rows, gate_w, up_hbm)
    act_recv = swap(act, "local")
    in_mine, in_away = call(
        input_body,
        [shaped((groups, ROWS, COLS), BF16)] * 2,
        [VMEM] * 8,
        [pltpu.VMEM((total, ROWS, COLS), F32)],
        products=total * 2 * one,
        moved=2 * one,
    )(cot, cot_recv, gate, up, act, weight, gate_w, up_w)
    in_recv = swap(in_away, "core")
    routed_mine, routed_away = call(
        routed_body,
        [shaped((groups, ROWS, LANES), BF16)] * 2,
        [VMEM] * 5 + [ANY],
        [pltpu.VMEM((total, ROWS, LANES), F32)],
        products=total * one,
        moved=one,
    )(act, act_recv, weight, down_own, down_away, in_mine)
    routed_recv = swap(routed_away, "core")
    summed = jnp.concatenate(
        [
            (in_mine.astype(F32) + in_recv.astype(F32)).astype(BF16),
            (routed_mine.astype(F32) + routed_recv.astype(F32)).astype(BF16),
        ],
        axis=2,
    )
    back = lax.all_to_all(summed, ("chip", "local"), split_axis=0, concat_axis=0, tiled=True)
    return call(
        final_body,
        [
            shaped((1, 1, width), BF16),
            shaped((1, 1, width), BF16),
            shaped(expert_ids.shape, F32),
        ],
        [VMEM, SMEM],
        [pltpu.VMEM((2, ROWS, SPAN), F32)],
    )(back, expert_ids)


def selector(flags, capacity):
    live = (flags > 0).astype(jnp.int32)
    order = jnp.cumsum(live) - live
    slot_ids = lax.broadcasted_iota(jnp.int32, (capacity, flags.shape[0]), 0)
    return ((slot_ids == order[None, :]) & (live[None, :] > 0)).astype(jnp.bfloat16)


def per_device(tokens, expert_ids, route_probs, gate_weight, up_weight, down_weight, out_grad):
    node_count = lax.axis_size("node")
    token_count = tokens.shape[1]
    width = tokens.shape[2]
    top_count = expert_ids.shape[2]
    column_rows = token_count * node_count
    capacity = min(column_rows, 5 * column_rows * top_count // (2 * node_count))
    slot_count = node_count * token_count
    gate_w = gate_weight[0]
    up_w = up_weight[0]
    down_w = down_weight[0]
    hidden_dev = gate_w.shape[1]
    onehot = (expert_ids[0][..., None] == jnp.arange(node_count, dtype=jnp.int32)).astype(
        jnp.float32
    )
    weights = jnp.einsum("tk,tke->te", route_probs[0], onehot)
    member = jnp.sum(onehot, axis=1)
    own_rows = tokens[0]
    zero_value = jnp.zeros((), jnp.bfloat16)
    own_flags = member.T.astype(jnp.bfloat16)
    send_rows = jnp.where(own_flags[:, :, None] > 0, own_rows[None], zero_value)
    recv_rows, recv_flags = (
        lax.all_to_all(send_rows, "node", split_axis=0, concat_axis=0, tiled=True),
        lax.all_to_all(own_flags, "node", split_axis=0, concat_axis=0, tiled=True),
    )
    select = selector(recv_flags.reshape(slot_count), capacity)
    packed_rows = jnp.dot(
        select, recv_rows.reshape(slot_count, width), preferred_element_type=jnp.float32
    ).astype(jnp.bfloat16)
    piece = lax.all_gather(packed_rows, "local", axis=0, tiled=True)
    gate_part = jnp.dot(piece, gate_w, preferred_element_type=jnp.float32)
    up_part = jnp.dot(piece, up_w, preferred_element_type=jnp.float32)
    joined = jnp.concatenate([gate_part, up_part], axis=1)
    gate_pre = joined[:, :hidden_dev]
    up_pre = joined[:, hidden_dev:]
    sigmoid_gate = jax.nn.sigmoid(gate_pre)
    silu_gate = gate_pre * sigmoid_gate
    hidden = (silu_gate * up_pre).astype(jnp.bfloat16)
    block = down_w
    routed_part = jnp.dot(
        lax.all_gather(hidden, "local", axis=1, tiled=True),
        block,
        preferred_element_type=jnp.float32,
    )
    routed_cols = routed_part.astype(jnp.bfloat16)
    routed_own = lax.all_to_all(routed_cols, "local", split_axis=0, concat_axis=1, tiled=True)
    routed_slots = jnp.dot(select.T, routed_own, preferred_element_type=jnp.float32).astype(
        jnp.bfloat16
    )
    routed_back = lax.all_to_all(
        routed_slots.reshape(node_count, token_count, width),
        "node",
        split_axis=0,
        concat_axis=0,
        tiled=True,
    )
    routed_wide = routed_back.astype(jnp.float32)
    combined = jnp.einsum("te,etd->td", weights, routed_wide).astype(jnp.bfloat16)
    grad_wide = out_grad[0].astype(jnp.float32)
    prob_terms = jnp.einsum("td,etd->te", grad_wide, routed_wide)
    prob_grad = jnp.einsum("te,tke->tk", prob_terms, onehot)
    scaled = (weights.T[:, :, None] * grad_wide[None]).astype(jnp.bfloat16)
    grad_recv = lax.all_to_all(scaled, "node", split_axis=0, concat_axis=0, tiled=True)
    grad_own = jnp.dot(
        select, grad_recv.reshape(slot_count, width), preferred_element_type=jnp.float32
    ).astype(jnp.bfloat16)
    grad_cols = lax.all_to_all(grad_own, "local", split_axis=1, concat_axis=0, tiled=True)
    block = down_w
    hidden_grad = (
        lax.psum_scatter(
            lax.dot_general(
                block, grad_cols, (((1,), (1,)), ((), ())), preferred_element_type=jnp.float32
            ).astype(jnp.bfloat16),
            "local",
            scatter_dimension=0,
            tiled=True,
        )
        .astype(jnp.float32)
        .T
    )
    gate_grad = (
        hidden_grad * up_pre * sigmoid_gate * (1.0 + gate_pre * (1.0 - sigmoid_gate))
    ).astype(jnp.bfloat16)
    up_grad = (hidden_grad * silu_gate).astype(jnp.bfloat16)
    first = lax.dot_general(
        gate_grad, gate_w, (((1,), (1,)), ((), ())), preferred_element_type=jnp.float32
    )
    second = lax.dot_general(
        up_grad, up_w, (((1,), (1,)), ((), ())), preferred_element_type=jnp.float32
    )
    input_own = lax.psum_scatter(
        (first + second).astype(jnp.bfloat16), "local", scatter_dimension=0, tiled=True
    )
    input_slots = jnp.dot(select.T, input_own, preferred_element_type=jnp.float32).astype(
        jnp.bfloat16
    )
    input_back = lax.all_to_all(
        input_slots.reshape(node_count, token_count, width),
        "node",
        split_axis=0,
        concat_axis=0,
        tiled=True,
    )
    input_grad = jnp.sum(input_back.astype(jnp.float32), axis=0).astype(jnp.bfloat16)
    return (combined[None], input_grad[None], prob_grad[None])


def solution(mesh):
    node, local = mesh.shape["node"], mesh.shape["local"]
    if local == 2 and node % 2 == 0 and node <= 16:
        mesh = Mesh(mesh.devices.reshape(node // 2, 2, local), ("chip", "core", "local"))
        body, nodes = fast_device, ("chip", "core")
    else:
        body, nodes = per_device, "node"
    rows = P("local", nodes, None)
    weights = P(nodes, None, "local")
    return jax.shard_map(
        body,
        mesh=mesh,
        in_specs=(rows, rows, rows, weights, weights, weights, rows),
        out_specs=(rows, rows, rows),
        check_vma=False,
    )
```

```python
import functools

import jax
import jax.numpy as jnp
from jax import lax
from jax.experimental import pallas as pl
from jax.experimental.pallas import tpu as pltpu
from jax.sharding import Mesh
from jax.sharding import PartitionSpec as P

BF16 = jnp.bfloat16
F32 = jnp.float32
LANES = 128
COLS = 256
DEPTH = 512
ROWS = 16
SPAN = COLS + LANES

NT = (((1,), (1,)), ((), ()))
VMEM = pl.BlockSpec(memory_space=pltpu.VMEM)
ANY = pl.BlockSpec(memory_space=pl.ANY)
SMEM = pl.BlockSpec(memory_space=pltpu.SMEM)


def call(body, outs, ins, scratch=(), products=0, moved=0):
    return pl.pallas_call(
        body,
        out_shape=tuple(outs),
        in_specs=ins,
        out_specs=tuple(VMEM for _ in outs),
        scratch_shapes=list(scratch),
        compiler_params=pltpu.CompilerParams(vmem_limit_bytes=12 << 20),
        cost_estimate=pl.CostEstimate(
            flops=int(products), bytes_accessed=int(moved), transcendentals=0
        ),
    )


def shaped(shape, dtype):
    return jax.ShapeDtypeStruct(shape, dtype)


def in_hbm(*arrays):
    return tuple(pltpu.with_memory_space_constraint(a, pltpu.HBM) for a in arrays)


def dot(a, b):
    return jnp.dot(a, b, preferred_element_type=F32)


def dot_nt(a, b):
    return lax.dot_general(a, b, NT, preferred_element_type=F32)


def high_low(x):
    high = x.astype(BF16).astype(F32)
    return high, x - high


def pack_body(
    ids_hbm, probs_hbm, tok_hbm, grad_hbm, out_ref, wide, ids_ref, probs_ref, tok_ref, grad_ref, sems
):
    pairs = ((ids_hbm, ids_ref), (probs_hbm, probs_ref), (tok_hbm, tok_ref), (grad_hbm, grad_ref))
    copies = [pltpu.make_async_copy(a, b, sems.at[i]) for i, (a, b) in enumerate(pairs)]
    for copy in copies:
        copy.start()
    wide[...] = jnp.zeros_like(wide)
    lane = lax.broadcasted_iota(jnp.int32, (1, LANES), 1)
    weight = jnp.zeros((1, LANES), F32)
    for copy in copies:
        copy.wait()
    for k in range(ids_ref.shape[2]):
        weight = jnp.where(lane == ids_ref[0, 0, k], probs_ref[0, 0, k], weight)
    width = tok_ref.shape[2]
    meta = width // COLS
    half = width // 2
    for i in range(meta):
        wide[i : i + 1, 0:COLS] = tok_ref[0, :, i * COLS : (i + 1) * COLS].astype(F32)
    high, low = high_low(weight)
    wide[meta : meta + 1, 0:LANES] = high
    wide[meta : meta + 1, LANES:COLS] = low
    for j in range(2):
        for i in range(half // LANES):
            at = j * half + i * LANES
            wide[i : i + 1, COLS:SPAN] = grad_ref[0, :, at : at + LANES].astype(F32)
        block = wide[...].astype(BF16)
        for i in range(j, out_ref.shape[0], 2):
            out_ref[i] = block


def side_rows(local, hidden, n):
    return pl.ds(pl.multiple_of(local * hidden + n * COLS, COLS), COLS)


def unpack_grads(wide, grads, first):
    count = wide.shape[0]
    for i in range(grads.shape[1] // LANES):
        grads[first : first + count, i * LANES : (i + 1) * LANES] = wide[:, i, COLS:SPAN].astype(BF16)


def unpack_row(wide, rows, first, i):
    count = wide.shape[0]
    rows[first : first + count, i * COLS : (i + 1) * COLS] = wide[:, i, 0:COLS].astype(BF16)


def unpack_weight(wide, weight_out, first, meta):
    count = wide.shape[0]
    expert = lax.axis_index("chip") * 2 + lax.axis_index("core")
    lane = lax.broadcasted_iota(jnp.int32, (count, LANES), 1)
    both = wide[:, meta, 0:LANES] + wide[:, meta, LANES:COLS]
    both = jnp.sum(jnp.where(lane == expert, both, 0.0), axis=1, keepdims=True)
    weight_out[first : first + count, :] = jnp.broadcast_to(both, (count, LANES))


def load_body(down_hbm, in_ref, away_ref, rows, grads, weight_out, wide, sems):
    hidden = away_ref.shape[0]
    away = 1 - lax.axis_index("local")
    copies = [
        pltpu.make_async_copy(
            down_hbm.at[0, side_rows(away, hidden, n), :],
            away_ref.at[n * COLS : (n + 1) * COLS, :],
            sems.at[n],
        )
        for n in range(hidden // COLS)
    ]
    for copy in copies:
        copy.start()
    meta = rows.shape[1] // COLS
    wide[...] = in_ref[...].astype(F32)
    unpack_grads(wide, grads, 0)
    for i in range(meta):
        unpack_row(wide, rows, 0, i)
    unpack_weight(wide, weight_out, 0, meta)
    for copy in copies:
        copy.wait()


def cot_body(
    other_ref, rows_in, grads_in, weight_in, loaded_ref, down_hbm, gate_hbm,
    away_ref, cot_ref, weight_out, rows, down_ref, gate_ref,
    wide, grads, sems,
):
    count = other_ref.shape[0]
    width = rows.shape[1]
    hidden = cot_ref.shape[1]
    local = lax.axis_index("local")
    steps = hidden // COLS
    copies = []
    for n in range(steps):
        into = down_ref.at[n * COLS : (n + 1) * COLS, :]
        copies.append(
            pltpu.make_async_copy(down_hbm.at[0, side_rows(local, hidden, n), :], into, sems.at[n])
        )
    for n in range(gate_ref.shape[0] // DEPTH):
        at = slice(n * DEPTH, (n + 1) * DEPTH)
        copies.append(
            pltpu.make_async_copy(gate_hbm.at[0, at, :], gate_ref.at[at, :], sems.at[steps + n])
        )
    for copy in copies:
        copy.start()
    meta = width // COLS
    wide[...] = other_ref[...].astype(F32)
    unpack_grads(wide, grads, count)
    grads[:count, :] = grads_in[...]
    grad = grads[...]
    for n in range(steps):
        at = slice(n * COLS, (n + 1) * COLS)
        away_ref[:, at] = dot_nt(grad, loaded_ref[at, :]).astype(BF16)
        for i in range(n, meta, steps):
            unpack_row(wide, rows, count, i)
    unpack_weight(wide, weight_out, count, meta)
    weight_out[:count, :] = weight_in[...]
    rows[:count, :] = rows_in[...]
    for n in range(steps):
        at = slice(n * COLS, (n + 1) * COLS)
        copies[n].wait()
        cot_ref[:, at] = dot_nt(grad, down_ref[at, :])
    for copy in copies[steps:]:
        copy.wait()


def forward_body(
    rows_ref, gate_ref, gate_hbm, up_hbm, gate_out, up_out, act_ref, gate_rest, up_ref, sems
):
    early, hidden = gate_ref.shape
    width = up_ref.shape[0]
    columns = [slice(n * COLS, (n + 1) * COLS) for n in range(hidden // COLS)]
    pieces = []
    for n in range(early // DEPTH, width // DEPTH):
        at = slice(n * DEPTH, (n + 1) * DEPTH)
        held = gate_rest.at[n * DEPTH - early : (n + 1) * DEPTH - early, :]
        pieces.append((gate_hbm.at[0, at, :], held, at, gate_out, False))
    for n in range(width // DEPTH):
        at = slice(n * DEPTH, (n + 1) * DEPTH)
        pieces.append((up_hbm.at[0, at, :], up_ref.at[at, :], at, up_out, n == 0))
    copies = [
        pltpu.make_async_copy(piece[0], piece[1], sems.at[i]) for i, piece in enumerate(pieces)
    ]
    for copy in copies:
        copy.start()
    for cols in columns:
        gate_out[:, cols] = dot(rows_ref[:, :early], gate_ref[:, cols])
    for copy, (_, held, at, out, fresh) in zip(copies, pieces):
        copy.wait()
        for cols in columns:
            part = dot(rows_ref[:, at], held[:, cols])
            out[:, cols] = part if fresh else out[:, cols] + part
    for cols in columns:
        gate = gate_out[:, cols]
        act_ref[:, cols] = (gate * jax.nn.sigmoid(gate) * up_out[:, cols]).astype(BF16)


def input_body(
    cot_ref, recv_ref, gate_in, up_in, act_ref, weight_in, gate_ref, gate_rest, up_ref,
    mine_ref, other_ref,
    wide,
):
    total = cot_ref.shape[0]
    count = total // 2
    width, early = up_ref.shape[0], gate_ref.shape[0]
    expert = lax.axis_index("chip") * 2 + lax.axis_index("core")
    gate, up = gate_in[...], up_in[...]
    sig = jax.nn.sigmoid(gate)
    cot = cot_ref[...] + recv_ref[...].astype(F32)
    prob = jnp.sum(cot * act_ref[...].astype(F32), axis=1, keepdims=True)
    hidden_grad = cot * weight_in[:, 0:1]
    gate_grad = (hidden_grad * up * sig * (1.0 + gate * (1.0 - sig))).astype(BF16)
    up_grad = (hidden_grad * (gate * sig)).astype(BF16)
    gate_turned, up_turned = gate_grad.T, up_grad.T
    steps = width // COLS
    for n in range(steps):
        at = slice(n * COLS, (n + 1) * COLS)
        if n * COLS < early:
            part = dot(gate_ref[at, :], gate_turned)
        else:
            part = dot(gate_rest[n * COLS - early : (n + 1) * COLS - early, :], gate_turned)
        part += dot(up_ref[at, :], up_turned)
        wide[:, n, :] = part.astype(BF16).T.astype(F32)
    lane = lax.broadcasted_iota(jnp.int32, (total, LANES), 1)
    high, low = high_low(jnp.where(lane == expert, prob, 0.0))
    wide[:, steps, 0:LANES] = high
    wide[:, steps, LANES:COLS] = low
    for n in range(steps + 1, ROWS):
        wide[:, n, :] = jnp.zeros((total, COLS), F32)
    mine_ref[...] = wide[:count].astype(BF16)
    other_ref[...] = wide[count:].astype(BF16)


def routed_body(
    act_ref, recv_ref, weight_in, own_ref, away_ref, after_ref, mine_ref, other_ref, wide
):
    total = act_ref.shape[0]
    count = total // 2
    feats = own_ref.shape[1]
    weight = weight_in[:, 0:1]
    act, recv = act_ref[...], recv_ref[...]
    for n in range(feats // COLS):
        cols = slice(n * COLS, (n + 1) * COLS)
        part = dot(act, own_ref[:, cols]) + dot(recv, away_ref[:, cols])
        part = part.astype(BF16).astype(F32) * weight
        wide[:, 2 * n, :] = part[:, :LANES]
        wide[:, 2 * n + 1, :] = part[:, LANES:]
    for n in range(feats // LANES, ROWS):
        wide[:, n, :] = jnp.zeros((total, LANES), F32)
    mine_ref[...] = wide[:count].astype(BF16)
    other_ref[...] = wide[count:].astype(BF16)


def final_body(in_ref, ids_ref, comb_ref, grad_ref, prob_ref, wide):
    groups = in_ref.shape[0]
    width = comb_ref.shape[2]
    half = width // 2
    for j in range(2):
        total = in_ref[j].astype(F32)
        for i in range(j + 2, groups, 2):
            total = total + in_ref[i].astype(F32)
        wide[j] = total
    meta = width // COLS
    for c in range(meta):
        grad_ref[0, :, c * COLS : (c + 1) * COLS] = (
            wide[0, c : c + 1, 0:COLS] + wide[1, c : c + 1, 0:COLS]
        ).astype(BF16)
    for j in range(2):
        for c in range(half // LANES):
            at = j * half + c * LANES
            comb_ref[0, :, at : at + LANES] = wide[j, c : c + 1, COLS:SPAN].astype(BF16)
    prob = wide[0, meta : meta + 1, 0:COLS] + wide[1, meta : meta + 1, 0:COLS]
    prob = prob[:, 0:LANES] + prob[:, LANES:COLS]
    lane = lax.broadcasted_iota(jnp.int32, (1, LANES), 1)
    top = ids_ref.shape[2]
    out = jnp.zeros((1, LANES), F32)
    for k in range(top):
        value = jnp.sum(jnp.where(lane == ids_ref[0, 0, k], prob, 0.0), axis=1, keepdims=True)
        out = jnp.where(lane == k, value, out)
    prob_ref[0] = out[:, :top]


def swap(x, axis):
    return lax.ppermute(x, axis, [(0, 1), (1, 0)])


def fast_device(tokens, expert_ids, route_probs, gate_weight, up_weight, down_weight, out_grad):
    groups = lax.axis_size("chip") * 2
    total = 2 * groups
    width = tokens.shape[2]
    hidden = gate_weight.shape[2]
    feats = down_weight.shape[2]
    one = width * hidden * 2
    early = width // DEPTH * 5 // 7 * DEPTH
    gate_hbm, up_hbm, down_hbm = in_hbm(gate_weight, up_weight, down_weight)
    (packed,) = call(
        pack_body,
        [shaped((groups, ROWS, SPAN), BF16)],
        [ANY] * 4,
        [
            pltpu.VMEM((ROWS, SPAN), F32),
            pltpu.SMEM(expert_ids.shape, expert_ids.dtype),
            pltpu.SMEM(route_probs.shape, route_probs.dtype),
            pltpu.VMEM(tokens.shape, BF16),
            pltpu.VMEM(out_grad.shape, BF16),
            pltpu.SemaphoreType.DMA((4,)),
        ],
    )(*in_hbm(expert_ids, route_probs, tokens, out_grad))
    own = lax.all_to_all(packed, ("chip", "local"), split_axis=0, concat_axis=0, tiled=True)
    other = swap(own, "core")
    down_away, own_rows, own_grads, own_weight = call(
        load_body,
        [
            pltpu.VMEM((hidden, feats), BF16),
            shaped((groups, width), BF16),
            shaped((groups, feats), BF16),
            shaped((groups, LANES), F32),
        ],
        [ANY, VMEM],
        [pltpu.VMEM((groups, ROWS, SPAN), F32), pltpu.SemaphoreType.DMA((hidden // COLS,))],
        moved=one,
    )(down_hbm, own)
    away, cot, weight, rows, down_own, gate_w = call(
        cot_body,
        [
            shaped((total, hidden), BF16),
            shaped((total, hidden), F32),
            shaped((total, LANES), F32),
            shaped((total, width), BF16),
            pltpu.VMEM((hidden, feats), BF16),
            pltpu.VMEM((early, hidden), BF16),
        ],
        [VMEM] * 5 + [ANY] * 2,
        [
            pltpu.VMEM((groups, ROWS, SPAN), F32),
            pltpu.VMEM((total, feats), BF16),
            pltpu.SemaphoreType.DMA((hidden // COLS + early // DEPTH,)),
        ],
        products=total * one,
        moved=2 * one,
    )(other, own_rows, own_grads, own_weight, down_away, down_hbm, gate_hbm)
    cot_recv = swap(away, "local")
    gate, up, act, gate_rest, up_w = call(
        forward_body,
        [
            shaped((total, hidden), F32),
            shaped((total, hidden), F32),
            shaped((total, hidden), BF16),
            pltpu.VMEM((width - early, hidden), BF16),
            pltpu.VMEM((width, hidden), BF16),
        ],
        [VMEM, VMEM, ANY, ANY],
        [pltpu.SemaphoreType.DMA(((2 * width - early) // DEPTH,))],
        products=total * 2 * one,
        moved=3 * one // 2,
    )(rows, gate_w, gate_hbm, up_hbm)
    act_recv = swap(act, "local")
    in_mine, in_away = call(
        input_body,
        [shaped((groups, ROWS, COLS), BF16)] * 2,
        [VMEM] * 9,
        [pltpu.VMEM((total, ROWS, COLS), F32)],
        products=total * 2 * one,
        moved=2 * one,
    )(cot, cot_recv, gate, up, act, weight, gate_w, gate_rest, up_w)
    in_recv = swap(in_away, "core")
    routed_mine, routed_away = call(
        routed_body,
        [shaped((groups, ROWS, LANES), BF16)] * 2,
        [VMEM] * 5 + [ANY],
        [pltpu.VMEM((total, ROWS, LANES), F32)],
        products=total * one,
        moved=one,
    )(act, act_recv, weight, down_own, down_away, in_mine)
    routed_recv = swap(routed_away, "core")
    summed = jnp.concatenate(
        [
            (in_mine.astype(F32) + in_recv.astype(F32)).astype(BF16),
            (routed_mine.astype(F32) + routed_recv.astype(F32)).astype(BF16),
        ],
        axis=2,
    )
    back = lax.all_to_all(summed, ("chip", "local"), split_axis=0, concat_axis=0, tiled=True)
    return call(
        final_body,
        [
            shaped((1, 1, width), BF16),
            shaped((1, 1, width), BF16),
            shaped(expert_ids.shape, F32),
        ],
        [VMEM, SMEM],
        [pltpu.VMEM((2, ROWS, SPAN), F32)],
    )(back, expert_ids)


def selector(flags, capacity):
    live = (flags > 0).astype(jnp.int32)
    order = jnp.cumsum(live) - live
    slot_ids = lax.broadcasted_iota(jnp.int32, (capacity, flags.shape[0]), 0)
    return ((slot_ids == order[None, :]) & (live[None, :] > 0)).astype(jnp.bfloat16)


def per_device(tokens, expert_ids, route_probs, gate_weight, up_weight, down_weight, out_grad):
    node_count = lax.axis_size("node")
    token_count = tokens.shape[1]
    width = tokens.shape[2]
    top_count = expert_ids.shape[2]
    column_rows = token_count * node_count
    capacity = min(column_rows, 5 * column_rows * top_count // (2 * node_count))
    slot_count = node_count * token_count
    gate_w = gate_weight[0]
    up_w = up_weight[0]
    down_w = down_weight[0]
    hidden_dev = gate_w.shape[1]
    onehot = (expert_ids[0][..., None] == jnp.arange(node_count, dtype=jnp.int32)).astype(
        jnp.float32
    )
    weights = jnp.einsum("tk,tke->te", route_probs[0], onehot)
    member = jnp.sum(onehot, axis=1)
    own_rows = tokens[0]
    zero_value = jnp.zeros((), jnp.bfloat16)
    own_flags = member.T.astype(jnp.bfloat16)
    send_rows = jnp.where(own_flags[:, :, None] > 0, own_rows[None], zero_value)
    recv_rows, recv_flags = (
        lax.all_to_all(send_rows, "node", split_axis=0, concat_axis=0, tiled=True),
        lax.all_to_all(own_flags, "node", split_axis=0, concat_axis=0, tiled=True),
    )
    select = selector(recv_flags.reshape(slot_count), capacity)
    packed_rows = jnp.dot(
        select, recv_rows.reshape(slot_count, width), preferred_element_type=jnp.float32
    ).astype(jnp.bfloat16)
    piece = lax.all_gather(packed_rows, "local", axis=0, tiled=True)
    gate_part = jnp.dot(piece, gate_w, preferred_element_type=jnp.float32)
    up_part = jnp.dot(piece, up_w, preferred_element_type=jnp.float32)
    joined = jnp.concatenate([gate_part, up_part], axis=1)
    gate_pre = joined[:, :hidden_dev]
    up_pre = joined[:, hidden_dev:]
    sigmoid_gate = jax.nn.sigmoid(gate_pre)
    silu_gate = gate_pre * sigmoid_gate
    hidden = (silu_gate * up_pre).astype(jnp.bfloat16)
    block = down_w
    routed_part = jnp.dot(
        lax.all_gather(hidden, "local", axis=1, tiled=True),
        block,
        preferred_element_type=jnp.float32,
    )
    routed_cols = routed_part.astype(jnp.bfloat16)
    routed_own = lax.all_to_all(routed_cols, "local", split_axis=0, concat_axis=1, tiled=True)
    routed_slots = jnp.dot(select.T, routed_own, preferred_element_type=jnp.float32).astype(
        jnp.bfloat16
    )
    routed_back = lax.all_to_all(
        routed_slots.reshape(node_count, token_count, width),
        "node",
        split_axis=0,
        concat_axis=0,
        tiled=True,
    )
    routed_wide = routed_back.astype(jnp.float32)
    combined = jnp.einsum("te,etd->td", weights, routed_wide).astype(jnp.bfloat16)
    grad_wide = out_grad[0].astype(jnp.float32)
    prob_terms = jnp.einsum("td,etd->te", grad_wide, routed_wide)
    prob_grad = jnp.einsum("te,tke->tk", prob_terms, onehot)
    scaled = (weights.T[:, :, None] * grad_wide[None]).astype(jnp.bfloat16)
    grad_recv = lax.all_to_all(scaled, "node", split_axis=0, concat_axis=0, tiled=True)
    grad_own = jnp.dot(
        select, grad_recv.reshape(slot_count, width), preferred_element_type=jnp.float32
    ).astype(jnp.bfloat16)
    grad_cols = lax.all_to_all(grad_own, "local", split_axis=1, concat_axis=0, tiled=True)
    block = down_w
    hidden_grad = (
        lax.psum_scatter(
            lax.dot_general(
                block, grad_cols, (((1,), (1,)), ((), ())), preferred_element_type=jnp.float32
            ).astype(jnp.bfloat16),
            "local",
            scatter_dimension=0,
            tiled=True,
        )
        .astype(jnp.float32)
        .T
    )
    gate_grad = (
        hidden_grad * up_pre * sigmoid_gate * (1.0 + gate_pre * (1.0 - sigmoid_gate))
    ).astype(jnp.bfloat16)
    up_grad = (hidden_grad * silu_gate).astype(jnp.bfloat16)
    first = lax.dot_general(
        gate_grad, gate_w, (((1,), (1,)), ((), ())), preferred_element_type=jnp.float32
    )
    second = lax.dot_general(
        up_grad, up_w, (((1,), (1,)), ((), ())), preferred_element_type=jnp.float32
    )
    input_own = lax.psum_scatter(
        (first + second).astype(jnp.bfloat16), "local", scatter_dimension=0, tiled=True
    )
    input_slots = jnp.dot(select.T, input_own, preferred_element_type=jnp.float32).astype(
        jnp.bfloat16
    )
    input_back = lax.all_to_all(
        input_slots.reshape(node_count, token_count, width),
        "node",
        split_axis=0,
        concat_axis=0,
        tiled=True,
    )
    input_grad = jnp.sum(input_back.astype(jnp.float32), axis=0).astype(jnp.bfloat16)
    return (combined[None], input_grad[None], prob_grad[None])


def solution(mesh):
    node, local = mesh.shape["node"], mesh.shape["local"]
    if local == 2 and node % 2 == 0 and node <= 16:
        mesh = Mesh(mesh.devices.reshape(node // 2, 2, local), ("chip", "core", "local"))
        body, nodes = fast_device, ("chip", "core")
    else:
        body, nodes = per_device, "node"
    rows = P("local", nodes, None)
    weights = P(nodes, None, "local")
    return jax.shard_map(
        body,
        mesh=mesh,
        in_specs=(rows, rows, rows, weights, weights, weights, rows),
        out_specs=(rows, rows, rows),
        check_vma=False,
    )
```

```python
import functools

import jax
import jax.numpy as jnp
from jax import lax
from jax.experimental import pallas as pl
from jax.experimental.pallas import tpu as pltpu
from jax.sharding import Mesh
from jax.sharding import PartitionSpec as P

BF16 = jnp.bfloat16
F32 = jnp.float32
LANES = 128
COLS = 256
ROWS = 16
SPAN = COLS + LANES

NT = (((1,), (1,)), ((), ()))
VMEM = pl.BlockSpec(memory_space=pltpu.VMEM)
ANY = pl.BlockSpec(memory_space=pl.ANY)
SMEM = pl.BlockSpec(memory_space=pltpu.SMEM)


def call(body, outs, ins, scratch=(), products=0, moved=0):
    return pl.pallas_call(
        body,
        out_shape=tuple(outs),
        in_specs=ins,
        out_specs=tuple(VMEM for _ in outs),
        scratch_shapes=list(scratch),
        compiler_params=pltpu.CompilerParams(vmem_limit_bytes=12 << 20),
        cost_estimate=pl.CostEstimate(
            flops=int(products), bytes_accessed=int(moved), transcendentals=0
        ),
    )


def shaped(shape, dtype):
    return jax.ShapeDtypeStruct(shape, dtype)


def in_hbm(*arrays):
    return tuple(pltpu.with_memory_space_constraint(a, pltpu.HBM) for a in arrays)


def dot(a, b):
    return jnp.dot(a, b, preferred_element_type=F32)


def dot_nt(a, b):
    return lax.dot_general(a, b, NT, preferred_element_type=F32)


def high_low(x):
    high = x.astype(BF16).astype(F32)
    return high, x - high


def pack_body(
    ids_hbm, probs_hbm, tok_hbm, grad_hbm, gate_hbm, up_hbm, down_hbm, out_ref, wide, ids_ref, probs_ref, tok_ref, grad_ref, sems
):
    pairs = ((ids_hbm, ids_ref), (probs_hbm, probs_ref), (tok_hbm, tok_ref), (grad_hbm, grad_ref))
    copies = [pltpu.make_async_copy(a, b, sems.at[i]) for i, (a, b) in enumerate(pairs)]
    for copy in copies:
        copy.start()
    wide[...] = jnp.zeros_like(wide)
    lane = lax.broadcasted_iota(jnp.int32, (1, LANES), 1)
    weight = jnp.zeros((1, LANES), F32)
    for copy in copies:
        copy.wait()
    for k in range(ids_ref.shape[2]):
        weight = jnp.where(lane == ids_ref[0, 0, k], probs_ref[0, 0, k], weight)
    width = tok_ref.shape[2]
    meta = width // COLS
    half = width // 2
    for i in range(meta):
        wide[i : i + 1, 0:COLS] = tok_ref[0, :, i * COLS : (i + 1) * COLS].astype(F32)
    high, low = high_low(weight)
    wide[meta : meta + 1, 0:LANES] = high
    wide[meta : meta + 1, LANES:COLS] = low
    for j in range(2):
        for i in range(half // LANES):
            at = j * half + i * LANES
            wide[i : i + 1, COLS:SPAN] = grad_ref[0, :, at : at + LANES].astype(F32)
        block = wide[...].astype(BF16)
        for i in range(j, out_ref.shape[0], 2):
            out_ref[i] = block


def side_rows(local, hidden, n):
    return pl.ds(pl.multiple_of(local * hidden + n * COLS, COLS), COLS)


def unpack_grads(wide, grads, first):
    count = wide.shape[0]
    for i in range(grads.shape[1] // LANES):
        grads[first : first + count, i * LANES : (i + 1) * LANES] = wide[:, i, COLS:SPAN].astype(BF16)


def unpack_row(wide, rows, first, i):
    count = wide.shape[0]
    rows[first : first + count, i * COLS : (i + 1) * COLS] = wide[:, i, 0:COLS].astype(BF16)


def unpack_weight(wide, weight_out, first, meta):
    count = wide.shape[0]
    expert = lax.axis_index("chip") * 2 + lax.axis_index("core")
    lane = lax.broadcasted_iota(jnp.int32, (count, LANES), 1)
    both = wide[:, meta, 0:LANES] + wide[:, meta, LANES:COLS]
    both = jnp.sum(jnp.where(lane == expert, both, 0.0), axis=1, keepdims=True)
    weight_out[first : first + count, :] = jnp.broadcast_to(both, (count, LANES))


def unpack_body(in_ref, rows, grads, weight_out, wide):
    meta = rows.shape[1] // COLS
    wide[...] = in_ref[...].astype(F32)
    unpack_grads(wide, grads, 0)
    for i in range(meta):
        unpack_row(wide, rows, 0, i)
    unpack_weight(wide, weight_out, 0, meta)


def cot_body(
    other_ref, rows_in, grads_in, weight_in, down_ref,
    away_ref, cot_ref, weight_out, rows,
    wide, grads,
):
    count = other_ref.shape[0]
    width = rows.shape[1]
    hidden = cot_ref.shape[1]
    local = lax.axis_index("local")
    steps = hidden // COLS
    meta = width // COLS
    wide[...] = other_ref[...].astype(F32)
    unpack_grads(wide, grads, count)
    grads[:count, :] = grads_in[...]
    grad = grads[...]
    for n in range(steps):
        at = slice(n * COLS, (n + 1) * COLS)
        away_ref[:, at] = dot_nt(grad, down_ref[side_rows(1 - local, hidden, n), :]).astype(BF16)
    for n in range(steps):
        at = slice(n * COLS, (n + 1) * COLS)
        cot_ref[:, at] = dot_nt(grad, down_ref[side_rows(local, hidden, n), :])
    for i in range(meta):
        unpack_row(wide, rows, count, i)
    unpack_weight(wide, weight_out, count, meta)
    weight_out[:count, :] = weight_in[...]
    rows[:count, :] = rows_in[...]


def forward_body(rows_ref, gate_ref, up_ref, gate_out, up_out, act_ref):
    tokens = rows_ref[...]
    for n in range(gate_ref.shape[1] // COLS):
        cols = slice(n * COLS, (n + 1) * COLS)
        gate, up = dot(tokens, gate_ref[:, cols]), dot(tokens, up_ref[:, cols])
        gate_out[:, cols] = gate
        up_out[:, cols] = up
        act_ref[:, cols] = (gate * jax.nn.sigmoid(gate) * up).astype(BF16)


def input_body(
    cot_ref, recv_ref, gate_in, up_in, act_ref, weight_in, gate_ref, up_ref,
    mine_ref, other_ref,
    wide,
):
    total = cot_ref.shape[0]
    count = total // 2
    width = up_ref.shape[0]
    expert = lax.axis_index("chip") * 2 + lax.axis_index("core")
    gate, up = gate_in[...], up_in[...]
    sig = jax.nn.sigmoid(gate)
    cot = cot_ref[...] + recv_ref[...].astype(F32)
    prob = jnp.sum(cot * act_ref[...].astype(F32), axis=1, keepdims=True)
    hidden_grad = cot * weight_in[:, 0:1]
    gate_grad = (hidden_grad * up * sig * (1.0 + gate * (1.0 - sig))).astype(BF16)
    up_grad = (hidden_grad * (gate * sig)).astype(BF16)
    gate_turned, up_turned = gate_grad.T, up_grad.T
    steps = width // COLS
    for n in range(steps):
        at = slice(n * COLS, (n + 1) * COLS)
        wide[:, n, :] = (dot(gate_ref[at, :], gate_turned) + dot(up_ref[at, :], up_turned)).T
    lane = lax.broadcasted_iota(jnp.int32, (total, LANES), 1)
    high, low = high_low(jnp.where(lane == expert, prob, 0.0))
    wide[:, steps, 0:LANES] = high
    wide[:, steps, LANES:COLS] = low
    for n in range(steps + 1, ROWS):
        wide[:, n, :] = jnp.zeros((total, COLS), F32)
    mine_ref[...] = wide[:count].astype(BF16)
    other_ref[...] = wide[count:].astype(BF16)


def routed_body(act_ref, recv_ref, weight_in, down_ref, after_ref, mine_ref, other_ref, wide):
    total, hidden = act_ref.shape
    count = total // 2
    feats = down_ref.shape[1]
    local = lax.axis_index("local")
    weight = weight_in[:, 0:1]
    act, recv = act_ref[...], recv_ref[...]
    own = pl.ds(pl.multiple_of(local * hidden, COLS), hidden)
    away = pl.ds(pl.multiple_of((1 - local) * hidden, COLS), hidden)
    for n in range(feats // COLS):
        cols = slice(n * COLS, (n + 1) * COLS)
        part = dot(act, down_ref[own, cols]) + dot(recv, down_ref[away, cols])
        part = part.astype(BF16).astype(F32) * weight
        wide[:, 2 * n, :] = part[:, :LANES]
        wide[:, 2 * n + 1, :] = part[:, LANES:]
    for n in range(feats // LANES, ROWS):
        wide[:, n, :] = jnp.zeros((total, LANES), F32)
    mine_ref[...] = wide[:count].astype(BF16)
    other_ref[...] = wide[count:].astype(BF16)


def final_body(in_ref, ids_ref, comb_ref, grad_ref, prob_ref, wide):
    groups = in_ref.shape[0]
    width = comb_ref.shape[2]
    half = width // 2
    for j in range(2):
        total = in_ref[j].astype(F32)
        for i in range(j + 2, groups, 2):
            total = total + in_ref[i].astype(F32)
        wide[j] = total
    meta = width // COLS
    for c in range(meta):
        grad_ref[0, :, c * COLS : (c + 1) * COLS] = (
            wide[0, c : c + 1, 0:COLS] + wide[1, c : c + 1, 0:COLS]
        ).astype(BF16)
    for j in range(2):
        for c in range(half // LANES):
            at = j * half + c * LANES
            comb_ref[0, :, at : at + LANES] = wide[j, c : c + 1, COLS:SPAN].astype(BF16)
    prob = wide[0, meta : meta + 1, 0:COLS] + wide[1, meta : meta + 1, 0:COLS]
    prob = prob[:, 0:LANES] + prob[:, LANES:COLS]
    lane = lax.broadcasted_iota(jnp.int32, (1, LANES), 1)
    top = ids_ref.shape[2]
    out = jnp.zeros((1, LANES), F32)
    for k in range(top):
        value = jnp.sum(jnp.where(lane == ids_ref[0, 0, k], prob, 0.0), axis=1, keepdims=True)
        out = jnp.where(lane == k, value, out)
    prob_ref[0] = out[:, :top]


def swap(x, axis):
    return lax.ppermute(x, axis, [(0, 1), (1, 0)])


def fast_device(tokens, expert_ids, route_probs, gate_weight, up_weight, down_weight, out_grad):
    groups = lax.axis_size("chip") * 2
    total = 2 * groups
    width = tokens.shape[2]
    hidden = gate_weight.shape[2]
    feats = down_weight.shape[2]
    one = width * hidden * 2
    gate_w, up_w, down_w = gate_weight[0], up_weight[0], down_weight[0]
    (packed,) = call(
        pack_body,
        [shaped((groups, ROWS, SPAN), BF16)],
        [ANY] * 7,
        [
            pltpu.VMEM((ROWS, SPAN), F32),
            pltpu.SMEM(expert_ids.shape, expert_ids.dtype),
            pltpu.SMEM(route_probs.shape, route_probs.dtype),
            pltpu.VMEM(tokens.shape, BF16),
            pltpu.VMEM(out_grad.shape, BF16),
            pltpu.SemaphoreType.DMA((4,)),
        ],
        moved=12 * one,
    )(*in_hbm(expert_ids, route_probs, tokens, out_grad, gate_w, up_w, down_w))
    own = lax.all_to_all(packed, ("chip", "local"), split_axis=0, concat_axis=0, tiled=True)
    other = swap(own, "core")
    own_rows, own_grads, own_weight = call(
        unpack_body,
        [
            shaped((groups, width), BF16),
            shaped((groups, feats), BF16),
            shaped((groups, LANES), F32),
        ],
        [VMEM],
        [pltpu.VMEM((groups, ROWS, SPAN), F32)],
        moved=one // 4,
    )(own)
    away, cot, weight, rows = call(
        cot_body,
        [
            shaped((total, hidden), BF16),
            shaped((total, hidden), F32),
            shaped((total, LANES), F32),
            shaped((total, width), BF16),
        ],
        [VMEM] * 5,
        [pltpu.VMEM((groups, ROWS, SPAN), F32), pltpu.VMEM((total, feats), BF16)],
        products=total * one,
        moved=one,
    )(other, own_rows, own_grads, own_weight, down_w)
    cot_recv = swap(away, "local")
    gate, up, act = call(
        forward_body,
        [
            shaped((total, hidden), F32),
            shaped((total, hidden), F32),
            shaped((total, hidden), BF16),
        ],
        [VMEM] * 3,
        products=total * 2 * one,
        moved=2 * one,
    )(rows, gate_w, up_w)
    act_recv = swap(act, "local")
    in_mine, in_away = call(
        input_body,
        [shaped((groups, ROWS, COLS), BF16)] * 2,
        [VMEM] * 8,
        [pltpu.VMEM((total, ROWS, COLS), F32)],
        products=total * 2 * one,
        moved=2 * one,
    )(cot, cot_recv, gate, up, act, weight, gate_w, up_w)
    in_recv = swap(in_away, "core")
    routed_mine, routed_away = call(
        routed_body,
        [shaped((groups, ROWS, LANES), BF16)] * 2,
        [VMEM] * 4 + [ANY],
        [pltpu.VMEM((total, ROWS, LANES), F32)],
        products=total * one,
        moved=one,
    )(act, act_recv, weight, down_w, in_mine)
    routed_recv = swap(routed_away, "core")
    summed = jnp.concatenate(
        [
            (in_mine.astype(F32) + in_recv.astype(F32)).astype(BF16),
            (routed_mine.astype(F32) + routed_recv.astype(F32)).astype(BF16),
        ],
        axis=2,
    )
    back = lax.all_to_all(summed, ("chip", "local"), split_axis=0, concat_axis=0, tiled=True)
    return call(
        final_body,
        [
            shaped((1, 1, width), BF16),
            shaped((1, 1, width), BF16),
            shaped(expert_ids.shape, F32),
        ],
        [VMEM, SMEM],
        [pltpu.VMEM((2, ROWS, SPAN), F32)],
    )(back, expert_ids)


def selector(flags, capacity):
    live = (flags > 0).astype(jnp.int32)
    order = jnp.cumsum(live) - live
    slot_ids = lax.broadcasted_iota(jnp.int32, (capacity, flags.shape[0]), 0)
    return ((slot_ids == order[None, :]) & (live[None, :] > 0)).astype(jnp.bfloat16)


def per_device(tokens, expert_ids, route_probs, gate_weight, up_weight, down_weight, out_grad):
    node_count = lax.axis_size("node")
    token_count = tokens.shape[1]
    width = tokens.shape[2]
    top_count = expert_ids.shape[2]
    column_rows = token_count * node_count
    capacity = min(column_rows, 5 * column_rows * top_count // (2 * node_count))
    slot_count = node_count * token_count
    gate_w = gate_weight[0]
    up_w = up_weight[0]
    down_w = down_weight[0]
    hidden_dev = gate_w.shape[1]
    onehot = (expert_ids[0][..., None] == jnp.arange(node_count, dtype=jnp.int32)).astype(
        jnp.float32
    )
    weights = jnp.einsum("tk,tke->te", route_probs[0], onehot)
    member = jnp.sum(onehot, axis=1)
    own_rows = tokens[0]
    zero_value = jnp.zeros((), jnp.bfloat16)
    own_flags = member.T.astype(jnp.bfloat16)
    send_rows = jnp.where(own_flags[:, :, None] > 0, own_rows[None], zero_value)
    recv_rows, recv_flags = (
        lax.all_to_all(send_rows, "node", split_axis=0, concat_axis=0, tiled=True),
        lax.all_to_all(own_flags, "node", split_axis=0, concat_axis=0, tiled=True),
    )
    select = selector(recv_flags.reshape(slot_count), capacity)
    packed_rows = jnp.dot(
        select, recv_rows.reshape(slot_count, width), preferred_element_type=jnp.float32
    ).astype(jnp.bfloat16)
    piece = lax.all_gather(packed_rows, "local", axis=0, tiled=True)
    gate_part = jnp.dot(piece, gate_w, preferred_element_type=jnp.float32)
    up_part = jnp.dot(piece, up_w, preferred_element_type=jnp.float32)
    joined = jnp.concatenate([gate_part, up_part], axis=1)
    gate_pre = joined[:, :hidden_dev]
    up_pre = joined[:, hidden_dev:]
    sigmoid_gate = jax.nn.sigmoid(gate_pre)
    silu_gate = gate_pre * sigmoid_gate
    hidden = (silu_gate * up_pre).astype(jnp.bfloat16)
    block = down_w
    routed_part = jnp.dot(
        lax.all_gather(hidden, "local", axis=1, tiled=True),
        block,
        preferred_element_type=jnp.float32,
    )
    routed_cols = routed_part.astype(jnp.bfloat16)
    routed_own = lax.all_to_all(routed_cols, "local", split_axis=0, concat_axis=1, tiled=True)
    routed_slots = jnp.dot(select.T, routed_own, preferred_element_type=jnp.float32).astype(
        jnp.bfloat16
    )
    routed_back = lax.all_to_all(
        routed_slots.reshape(node_count, token_count, width),
        "node",
        split_axis=0,
        concat_axis=0,
        tiled=True,
    )
    routed_wide = routed_back.astype(jnp.float32)
    combined = jnp.einsum("te,etd->td", weights, routed_wide).astype(jnp.bfloat16)
    grad_wide = out_grad[0].astype(jnp.float32)
    prob_terms = jnp.einsum("td,etd->te", grad_wide, routed_wide)
    prob_grad = jnp.einsum("te,tke->tk", prob_terms, onehot)
    scaled = (weights.T[:, :, None] * grad_wide[None]).astype(jnp.bfloat16)
    grad_recv = lax.all_to_all(scaled, "node", split_axis=0, concat_axis=0, tiled=True)
    grad_own = jnp.dot(
        select, grad_recv.reshape(slot_count, width), preferred_element_type=jnp.float32
    ).astype(jnp.bfloat16)
    grad_cols = lax.all_to_all(grad_own, "local", split_axis=1, concat_axis=0, tiled=True)
    block = down_w
    hidden_grad = (
        lax.psum_scatter(
            lax.dot_general(
                block, grad_cols, (((1,), (1,)), ((), ())), preferred_element_type=jnp.float32
            ).astype(jnp.bfloat16),
            "local",
            scatter_dimension=0,
            tiled=True,
        )
        .astype(jnp.float32)
        .T
    )
    gate_grad = (
        hidden_grad * up_pre * sigmoid_gate * (1.0 + gate_pre * (1.0 - sigmoid_gate))
    ).astype(jnp.bfloat16)
    up_grad = (hidden_grad * silu_gate).astype(jnp.bfloat16)
    first = lax.dot_general(
        gate_grad, gate_w, (((1,), (1,)), ((), ())), preferred_element_type=jnp.float32
    )
    second = lax.dot_general(
        up_grad, up_w, (((1,), (1,)), ((), ())), preferred_element_type=jnp.float32
    )
    input_own = lax.psum_scatter(
        (first + second).astype(jnp.bfloat16), "local", scatter_dimension=0, tiled=True
    )
    input_slots = jnp.dot(select.T, input_own, preferred_element_type=jnp.float32).astype(
        jnp.bfloat16
    )
    input_back = lax.all_to_all(
        input_slots.reshape(node_count, token_count, width),
        "node",
        split_axis=0,
        concat_axis=0,
        tiled=True,
    )
    input_grad = jnp.sum(input_back.astype(jnp.float32), axis=0).astype(jnp.bfloat16)
    return (combined[None], input_grad[None], prob_grad[None])


def solution(mesh):
    node, local = mesh.shape["node"], mesh.shape["local"]
    if local == 2 and node % 2 == 0 and node <= 16:
        mesh = Mesh(mesh.devices.reshape(node // 2, 2, local), ("chip", "core", "local"))
        body, nodes = fast_device, ("chip", "core")
    else:
        body, nodes = per_device, "node"
    rows = P("local", nodes, None)
    weights = P(nodes, None, "local")
    return jax.shard_map(
        body,
        mesh=mesh,
        in_specs=(rows, rows, rows, weights, weights, weights, rows),
        out_specs=(rows, rows, rows),
        check_vma=False,
    )
```

```python
import functools

import jax
import jax.numpy as jnp
from jax import lax
from jax.experimental import pallas as pl
from jax.experimental.pallas import tpu as pltpu
from jax.sharding import Mesh
from jax.sharding import PartitionSpec as P

BF16 = jnp.bfloat16
F32 = jnp.float32
LANES = 128
COLS = 256
ROWS = 16
SPAN = COLS + LANES

NT = (((1,), (1,)), ((), ()))
VMEM = pl.BlockSpec(memory_space=pltpu.VMEM)
ANY = pl.BlockSpec(memory_space=pl.ANY)


def call(body, outs, ins, scratch=(), products=0, moved=0):
    return pl.pallas_call(
        body,
        out_shape=tuple(outs),
        in_specs=ins,
        out_specs=tuple(VMEM for _ in outs),
        scratch_shapes=list(scratch),
        compiler_params=pltpu.CompilerParams(vmem_limit_bytes=12 << 20),
        cost_estimate=pl.CostEstimate(
            flops=int(products), bytes_accessed=int(moved), transcendentals=0
        ),
    )


def shaped(shape, dtype):
    return jax.ShapeDtypeStruct(shape, dtype)


def in_hbm(*arrays):
    return tuple(pltpu.with_memory_space_constraint(a, pltpu.HBM) for a in arrays)


def dot(a, b):
    return jnp.dot(a, b, preferred_element_type=F32)


def dot_nt(a, b):
    return lax.dot_general(a, b, NT, preferred_element_type=F32)


def high_low(x):
    high = x.astype(BF16).astype(F32)
    return high, x - high


def pack_body(
    ids_hbm, probs_hbm, tok_hbm, grad_hbm, gate_hbm, up_hbm, down_hbm, out_ref, named_ref,
    wide, ids_ref, probs_ref, tok_ref, grad_ref, sems
):
    pairs = ((ids_hbm, ids_ref), (probs_hbm, probs_ref), (tok_hbm, tok_ref), (grad_hbm, grad_ref))
    copies = [pltpu.make_async_copy(a, b, sems.at[i]) for i, (a, b) in enumerate(pairs)]
    for copy in copies:
        copy.start()
    wide[...] = jnp.zeros_like(wide)
    lane = lax.broadcasted_iota(jnp.int32, (1, LANES), 1)
    weight = jnp.zeros((1, LANES), F32)
    for copy in copies:
        copy.wait()
    for k in range(ids_ref.shape[2]):
        named = lane == ids_ref[0, 0, k]
        weight = jnp.where(named, probs_ref[0, 0, k], weight)
        named_ref[k : k + 1, :] = named.astype(F32)
    width = tok_ref.shape[2]
    meta = width // COLS
    half = width // 2
    for i in range(meta):
        wide[i : i + 1, 0:COLS] = tok_ref[0, :, i * COLS : (i + 1) * COLS].astype(F32)
    high, low = high_low(weight)
    wide[meta : meta + 1, 0:LANES] = high
    wide[meta : meta + 1, LANES:COLS] = low
    for j in range(2):
        for i in range(half // LANES):
            at = j * half + i * LANES
            wide[i : i + 1, COLS:SPAN] = grad_ref[0, :, at : at + LANES].astype(F32)
        block = wide[...].astype(BF16)
        for i in range(j, out_ref.shape[0], 2):
            out_ref[i] = block


def side_rows(local, hidden, n):
    return pl.ds(pl.multiple_of(local * hidden + n * COLS, COLS), COLS)


def unpack_grads(wide, grads, first):
    count = wide.shape[0]
    for i in range(grads.shape[1] // LANES):
        grads[first : first + count, i * LANES : (i + 1) * LANES] = wide[:, i, COLS:SPAN].astype(BF16)


def unpack_row(wide, rows, first, i):
    count = wide.shape[0]
    rows[first : first + count, i * COLS : (i + 1) * COLS] = wide[:, i, 0:COLS].astype(BF16)


def unpack_weight(wide, weight_out, first, meta):
    count = wide.shape[0]
    expert = lax.axis_index("chip") * 2 + lax.axis_index("core")
    lane = lax.broadcasted_iota(jnp.int32, (count, LANES), 1)
    both = wide[:, meta, 0:LANES] + wide[:, meta, LANES:COLS]
    both = jnp.sum(jnp.where(lane == expert, both, 0.0), axis=1, keepdims=True)
    weight_out[first : first + count, :] = jnp.broadcast_to(both, (count, LANES))


def unpack_body(in_ref, rows, grads, weight_out, wide):
    meta = rows.shape[1] // COLS
    wide[...] = in_ref[...].astype(F32)
    unpack_grads(wide, grads, 0)
    for i in range(meta):
        unpack_row(wide, rows, 0, i)
    unpack_weight(wide, weight_out, 0, meta)


def cot_body(
    other_ref, rows_in, grads_in, weight_in, down_ref,
    away_ref, cot_ref, weight_out, rows,
    wide, grads,
):
    count = other_ref.shape[0]
    width = rows.shape[1]
    hidden = cot_ref.shape[1]
    local = lax.axis_index("local")
    steps = hidden // COLS
    meta = width // COLS
    wide[...] = other_ref[...].astype(F32)
    unpack_grads(wide, grads, count)
    grads[:count, :] = grads_in[...]
    grad = grads[...]
    for n in range(steps):
        at = slice(n * COLS, (n + 1) * COLS)
        away_ref[:, at] = dot_nt(grad, down_ref[side_rows(1 - local, hidden, n), :]).astype(BF16)
    for n in range(steps):
        at = slice(n * COLS, (n + 1) * COLS)
        cot_ref[:, at] = dot_nt(grad, down_ref[side_rows(local, hidden, n), :])
    for i in range(meta):
        unpack_row(wide, rows, count, i)
    unpack_weight(wide, weight_out, count, meta)
    weight_out[:count, :] = weight_in[...]
    rows[:count, :] = rows_in[...]


def forward_body(rows_ref, gate_ref, up_ref, gate_out, up_out, act_ref):
    tokens = rows_ref[...]
    for n in range(gate_ref.shape[1] // COLS):
        cols = slice(n * COLS, (n + 1) * COLS)
        gate, up = dot(tokens, gate_ref[:, cols]), dot(tokens, up_ref[:, cols])
        gate_out[:, cols] = gate
        up_out[:, cols] = up
        act_ref[:, cols] = (gate * jax.nn.sigmoid(gate) * up).astype(BF16)


def input_body(
    cot_ref, recv_ref, gate_in, up_in, act_ref, weight_in, gate_ref, up_ref,
    mine_ref, other_ref,
    wide,
):
    total = cot_ref.shape[0]
    count = total // 2
    width = up_ref.shape[0]
    expert = lax.axis_index("chip") * 2 + lax.axis_index("core")
    gate, up = gate_in[...], up_in[...]
    sig = jax.nn.sigmoid(gate)
    cot = cot_ref[...] + recv_ref[...].astype(F32)
    prob = jnp.sum(cot * act_ref[...].astype(F32), axis=1, keepdims=True)
    hidden_grad = cot * weight_in[:, 0:1]
    gate_grad = (hidden_grad * up * sig * (1.0 + gate * (1.0 - sig))).astype(BF16)
    up_grad = (hidden_grad * (gate * sig)).astype(BF16)
    gate_turned, up_turned = gate_grad.T, up_grad.T
    steps = width // COLS
    for n in range(steps):
        at = slice(n * COLS, (n + 1) * COLS)
        if n % 3 == 0:
            part = (dot(gate_ref[at, :], gate_turned) + dot(up_ref[at, :], up_turned)).T
        else:
            part = dot_nt(gate_grad, gate_ref[at, :]) + dot_nt(up_grad, up_ref[at, :])
        wide[:, n, :] = part
    lane = lax.broadcasted_iota(jnp.int32, (total, LANES), 1)
    high, low = high_low(jnp.where(lane == expert, prob, 0.0))
    wide[:, steps, 0:LANES] = high
    wide[:, steps, LANES:COLS] = low
    for n in range(steps + 1, ROWS):
        wide[:, n, :] = jnp.zeros((total, COLS), F32)
    mine_ref[...] = wide[:count].astype(BF16)
    other_ref[...] = wide[count:].astype(BF16)


def routed_body(
    act_ref, recv_ref, weight_in, down_ref, in_mine, in_away, mine_ref, other_ref, wide
):
    total, hidden = act_ref.shape
    count = total // 2
    feats = down_ref.shape[1]
    local = lax.axis_index("local")
    weight = weight_in[:, 0:1]
    act, recv = act_ref[...], recv_ref[...]
    own = pl.ds(pl.multiple_of(local * hidden, COLS), hidden)
    away = pl.ds(pl.multiple_of((1 - local) * hidden, COLS), hidden)
    for n in range(feats // COLS):
        cols = slice(n * COLS, (n + 1) * COLS)
        part = dot(act, down_ref[own, cols]) + dot(recv, down_ref[away, cols])
        part = part.astype(BF16).astype(F32) * weight
        wide[:, 2 * n, :] = part[:, :LANES]
        wide[:, 2 * n + 1, :] = part[:, LANES:]
    for n in range(feats // LANES, ROWS):
        wide[:, n, :] = jnp.zeros((total, LANES), F32)
    for ref, part, at in ((mine_ref, in_mine, 0), (other_ref, in_away, count)):
        ref[:, :, 0:COLS] = part[...]
        ref[:, :, COLS:SPAN] = wide[at : at + count].astype(BF16)


def final_body(in_ref, named_ref, comb_ref, grad_ref, prob_ref, wide):
    groups = in_ref.shape[0]
    width = comb_ref.shape[2]
    half = width // 2
    for j in range(2):
        total = in_ref[j].astype(F32)
        for i in range(j + 2, groups, 2):
            total = total + in_ref[i].astype(F32)
        wide[j] = total
    meta = width // COLS
    total = wide[0] + wide[1]
    grad_ref[0] = jnp.concatenate([total[c : c + 1, 0:COLS] for c in range(meta)], axis=1).astype(BF16)
    comb_ref[0] = jnp.concatenate(
        [wide[j, c : c + 1, COLS:SPAN] for j in range(2) for c in range(half // LANES)], axis=1
    ).astype(BF16)
    prob = wide[0, meta : meta + 1, 0:COLS] + wide[1, meta : meta + 1, 0:COLS]
    prob = prob[:, 0:LANES] + prob[:, LANES:COLS]
    lane = lax.broadcasted_iota(jnp.int32, (1, LANES), 1)
    top = named_ref.shape[0]
    out = jnp.zeros((1, LANES), F32)
    for k in range(top):
        value = jnp.sum(named_ref[k : k + 1, :] * prob, axis=1, keepdims=True)
        out = jnp.where(lane == k, value, out)
    prob_ref[0] = out[:, :top]


def swap(x, axis):
    return lax.ppermute(x, axis, [(0, 1), (1, 0)])


def fast_device(tokens, expert_ids, route_probs, gate_weight, up_weight, down_weight, out_grad):
    groups = lax.axis_size("chip") * 2
    total = 2 * groups
    width = tokens.shape[2]
    hidden = gate_weight.shape[2]
    feats = down_weight.shape[2]
    one = width * hidden * 2
    gate_w, up_w, down_w = gate_weight[0], up_weight[0], down_weight[0]
    packed, named = call(
        pack_body,
        [shaped((groups, ROWS, SPAN), BF16), shaped((expert_ids.shape[2], LANES), F32)],
        [ANY] * 7,
        [
            pltpu.VMEM((ROWS, SPAN), F32),
            pltpu.SMEM(expert_ids.shape, expert_ids.dtype),
            pltpu.SMEM(route_probs.shape, route_probs.dtype),
            pltpu.VMEM(tokens.shape, BF16),
            pltpu.VMEM(out_grad.shape, BF16),
            pltpu.SemaphoreType.DMA((4,)),
        ],
        moved=12 * one,
    )(*in_hbm(expert_ids, route_probs, tokens, out_grad, gate_w, up_w, down_w))
    own = lax.all_to_all(packed, ("chip", "local"), split_axis=0, concat_axis=0, tiled=True)
    other = swap(own, "core")
    own_rows, own_grads, own_weight = call(
        unpack_body,
        [
            shaped((groups, width), BF16),
            shaped((groups, feats), BF16),
            shaped((groups, LANES), F32),
        ],
        [VMEM],
        [pltpu.VMEM((groups, ROWS, SPAN), F32)],
        moved=one // 4,
    )(own)
    away, cot, weight, rows = call(
        cot_body,
        [
            shaped((total, hidden), BF16),
            shaped((total, hidden), F32),
            shaped((total, LANES), F32),
            shaped((total, width), BF16),
        ],
        [VMEM] * 5,
        [pltpu.VMEM((groups, ROWS, SPAN), F32), pltpu.VMEM((total, feats), BF16)],
        products=total * one,
        moved=one,
    )(other, own_rows, own_grads, own_weight, down_w)
    cot_recv = swap(away, "local")
    gate, up, act = call(
        forward_body,
        [
            shaped((total, hidden), F32),
            shaped((total, hidden), F32),
            shaped((total, hidden), BF16),
        ],
        [VMEM] * 3,
        products=total * 2 * one,
        moved=2 * one,
    )(rows, gate_w, up_w)
    act_recv = swap(act, "local")
    in_mine, in_away = call(
        input_body,
        [shaped((groups, ROWS, COLS), BF16)] * 2,
        [VMEM] * 8,
        [pltpu.VMEM((total, ROWS, COLS), F32)],
        products=total * 2 * one,
        moved=2 * one,
    )(cot, cot_recv, gate, up, act, weight, gate_w, up_w)
    mine, away = call(
        routed_body,
        [shaped((groups, ROWS, SPAN), BF16)] * 2,
        [VMEM] * 6,
        [pltpu.VMEM((total, ROWS, LANES), F32)],
        products=total * one,
        moved=one,
    )(act, act_recv, weight, down_w, in_mine, in_away)
    summed = (mine.astype(F32) + swap(away, "core").astype(F32)).astype(BF16)
    back = lax.all_to_all(summed, ("chip", "local"), split_axis=0, concat_axis=0, tiled=True)
    return call(
        final_body,
        [
            shaped((1, 1, width), BF16),
            shaped((1, 1, width), BF16),
            shaped(expert_ids.shape, F32),
        ],
        [VMEM, VMEM],
        [pltpu.VMEM((2, ROWS, SPAN), F32)],
    )(back, named)


def selector(flags, capacity):
    live = (flags > 0).astype(jnp.int32)
    order = jnp.cumsum(live) - live
    slot_ids = lax.broadcasted_iota(jnp.int32, (capacity, flags.shape[0]), 0)
    return ((slot_ids == order[None, :]) & (live[None, :] > 0)).astype(jnp.bfloat16)


def per_device(tokens, expert_ids, route_probs, gate_weight, up_weight, down_weight, out_grad):
    node_count = lax.axis_size("node")
    token_count = tokens.shape[1]
    width = tokens.shape[2]
    top_count = expert_ids.shape[2]
    column_rows = token_count * node_count
    capacity = min(column_rows, 5 * column_rows * top_count // (2 * node_count))
    slot_count = node_count * token_count
    gate_w = gate_weight[0]
    up_w = up_weight[0]
    down_w = down_weight[0]
    hidden_dev = gate_w.shape[1]
    onehot = (expert_ids[0][..., None] == jnp.arange(node_count, dtype=jnp.int32)).astype(
        jnp.float32
    )
    weights = jnp.einsum("tk,tke->te", route_probs[0], onehot)
    member = jnp.sum(onehot, axis=1)
    own_rows = tokens[0]
    zero_value = jnp.zeros((), jnp.bfloat16)
    own_flags = member.T.astype(jnp.bfloat16)
    send_rows = jnp.where(own_flags[:, :, None] > 0, own_rows[None], zero_value)
    recv_rows, recv_flags = (
        lax.all_to_all(send_rows, "node", split_axis=0, concat_axis=0, tiled=True),
        lax.all_to_all(own_flags, "node", split_axis=0, concat_axis=0, tiled=True),
    )
    select = selector(recv_flags.reshape(slot_count), capacity)
    packed_rows = jnp.dot(
        select, recv_rows.reshape(slot_count, width), preferred_element_type=jnp.float32
    ).astype(jnp.bfloat16)
    piece = lax.all_gather(packed_rows, "local", axis=0, tiled=True)
    gate_part = jnp.dot(piece, gate_w, preferred_element_type=jnp.float32)
    up_part = jnp.dot(piece, up_w, preferred_element_type=jnp.float32)
    joined = jnp.concatenate([gate_part, up_part], axis=1)
    gate_pre = joined[:, :hidden_dev]
    up_pre = joined[:, hidden_dev:]
    sigmoid_gate = jax.nn.sigmoid(gate_pre)
    silu_gate = gate_pre * sigmoid_gate
    hidden = (silu_gate * up_pre).astype(jnp.bfloat16)
    block = down_w
    routed_part = jnp.dot(
        lax.all_gather(hidden, "local", axis=1, tiled=True),
        block,
        preferred_element_type=jnp.float32,
    )
    routed_cols = routed_part.astype(jnp.bfloat16)
    routed_own = lax.all_to_all(routed_cols, "local", split_axis=0, concat_axis=1, tiled=True)
    routed_slots = jnp.dot(select.T, routed_own, preferred_element_type=jnp.float32).astype(
        jnp.bfloat16
    )
    routed_back = lax.all_to_all(
        routed_slots.reshape(node_count, token_count, width),
        "node",
        split_axis=0,
        concat_axis=0,
        tiled=True,
    )
    routed_wide = routed_back.astype(jnp.float32)
    combined = jnp.einsum("te,etd->td", weights, routed_wide).astype(jnp.bfloat16)
    grad_wide = out_grad[0].astype(jnp.float32)
    prob_terms = jnp.einsum("td,etd->te", grad_wide, routed_wide)
    prob_grad = jnp.einsum("te,tke->tk", prob_terms, onehot)
    scaled = (weights.T[:, :, None] * grad_wide[None]).astype(jnp.bfloat16)
    grad_recv = lax.all_to_all(scaled, "node", split_axis=0, concat_axis=0, tiled=True)
    grad_own = jnp.dot(
        select, grad_recv.reshape(slot_count, width), preferred_element_type=jnp.float32
    ).astype(jnp.bfloat16)
    grad_cols = lax.all_to_all(grad_own, "local", split_axis=1, concat_axis=0, tiled=True)
    block = down_w
    hidden_grad = (
        lax.psum_scatter(
            lax.dot_general(
                block, grad_cols, (((1,), (1,)), ((), ())), preferred_element_type=jnp.float32
            ).astype(jnp.bfloat16),
            "local",
            scatter_dimension=0,
            tiled=True,
        )
        .astype(jnp.float32)
        .T
    )
    gate_grad = (
        hidden_grad * up_pre * sigmoid_gate * (1.0 + gate_pre * (1.0 - sigmoid_gate))
    ).astype(jnp.bfloat16)
    up_grad = (hidden_grad * silu_gate).astype(jnp.bfloat16)
    first = lax.dot_general(
        gate_grad, gate_w, (((1,), (1,)), ((), ())), preferred_element_type=jnp.float32
    )
    second = lax.dot_general(
        up_grad, up_w, (((1,), (1,)), ((), ())), preferred_element_type=jnp.float32
    )
    input_own = lax.psum_scatter(
        (first + second).astype(jnp.bfloat16), "local", scatter_dimension=0, tiled=True
    )
    input_slots = jnp.dot(select.T, input_own, preferred_element_type=jnp.float32).astype(
        jnp.bfloat16
    )
    input_back = lax.all_to_all(
        input_slots.reshape(node_count, token_count, width),
        "node",
        split_axis=0,
        concat_axis=0,
        tiled=True,
    )
    input_grad = jnp.sum(input_back.astype(jnp.float32), axis=0).astype(jnp.bfloat16)
    return (combined[None], input_grad[None], prob_grad[None])


def solution(mesh):
    node, local = mesh.shape["node"], mesh.shape["local"]
    if local == 2 and node % 2 == 0 and node <= 16:
        mesh = Mesh(mesh.devices.reshape(node // 2, 2, local), ("chip", "core", "local"))
        body, nodes = fast_device, ("chip", "core")
    else:
        body, nodes = per_device, "node"
    rows = P("local", nodes, None)
    weights = P(nodes, None, "local")
    return jax.shard_map(
        body,
        mesh=mesh,
        in_specs=(rows, rows, rows, weights, weights, weights, rows),
        out_specs=(rows, rows, rows),
        check_vma=False,
    )
```

```python
import functools

import jax
import jax.numpy as jnp
from jax import lax
from jax.experimental import pallas as pl
from jax.experimental.pallas import tpu as pltpu
from jax.sharding import Mesh
from jax.sharding import PartitionSpec as P

BF16 = jnp.bfloat16
F32 = jnp.float32
LANES = 128
COLS = 256
ROWS = 16
SPAN = COLS + LANES

NT = (((1,), (1,)), ((), ()))
VMEM = pl.BlockSpec(memory_space=pltpu.VMEM)
ANY = pl.BlockSpec(memory_space=pl.ANY)


def call(body, outs, ins, scratch=(), products=0, moved=0):
    return pl.pallas_call(
        body,
        out_shape=tuple(outs),
        in_specs=ins,
        out_specs=tuple(VMEM for _ in outs),
        scratch_shapes=list(scratch),
        compiler_params=pltpu.CompilerParams(vmem_limit_bytes=12 << 20),
        cost_estimate=pl.CostEstimate(
            flops=int(products), bytes_accessed=int(moved), transcendentals=0
        ),
    )


def shaped(shape, dtype):
    return jax.ShapeDtypeStruct(shape, dtype)


def in_hbm(*arrays):
    return tuple(pltpu.with_memory_space_constraint(a, pltpu.HBM) for a in arrays)


def dot(a, b):
    return jnp.dot(a, b, preferred_element_type=F32)


def dot_nt(a, b):
    return lax.dot_general(a, b, NT, preferred_element_type=F32)


def high_low(x):
    high = x.astype(BF16).astype(F32)
    return high, x - high


def pack_body(
    ids_hbm, probs_hbm, tok_hbm, grad_hbm, gate_hbm, up_hbm, down_hbm, out_ref, named_ref,
    wide, ids_ref, probs_ref, tok_ref, grad_ref, sems
):
    pairs = ((ids_hbm, ids_ref), (probs_hbm, probs_ref), (tok_hbm, tok_ref), (grad_hbm, grad_ref))
    copies = [pltpu.make_async_copy(a, b, sems.at[i]) for i, (a, b) in enumerate(pairs)]
    for copy in copies:
        copy.start()
    wide[...] = jnp.zeros_like(wide)
    lane = lax.broadcasted_iota(jnp.int32, (1, LANES), 1)
    weight = jnp.zeros((1, LANES), F32)
    for copy in copies:
        copy.wait()
    for k in range(ids_ref.shape[2]):
        named = lane == ids_ref[0, 0, k]
        weight = jnp.where(named, probs_ref[0, 0, k], weight)
        named_ref[k : k + 1, :] = named.astype(F32)
    width = tok_ref.shape[2]
    meta = width // COLS
    half = width // 2
    for i in range(meta):
        wide[i : i + 1, 0:COLS] = tok_ref[0, :, i * COLS : (i + 1) * COLS].astype(F32)
    high, low = high_low(weight)
    wide[meta : meta + 1, 0:LANES] = high
    wide[meta : meta + 1, LANES:COLS] = low
    for j in range(2):
        for i in range(half // LANES):
            at = j * half + i * LANES
            wide[i : i + 1, COLS:SPAN] = grad_ref[0, :, at : at + LANES].astype(F32)
        block = wide[...].astype(BF16)
        for i in range(j, out_ref.shape[0], 2):
            out_ref[i] = block


def side_rows(local, hidden, n):
    return pl.ds(pl.multiple_of(local * hidden + n * COLS, COLS), COLS)


def unpack_grads(wide, grads, first):
    count = wide.shape[0]
    for i in range(grads.shape[1] // LANES):
        grads[first : first + count, i * LANES : (i + 1) * LANES] = wide[:, i, COLS:SPAN].astype(BF16)


def unpack_row(wide, rows, first, i):
    count = wide.shape[0]
    rows[first : first + count, i * COLS : (i + 1) * COLS] = wide[:, i, 0:COLS].astype(BF16)


def unpack_weight(wide, weight_out, first, meta):
    count = wide.shape[0]
    expert = lax.axis_index("chip") * 2 + lax.axis_index("core")
    lane = lax.broadcasted_iota(jnp.int32, (count, LANES), 1)
    both = wide[:, meta, 0:LANES] + wide[:, meta, LANES:COLS]
    both = jnp.sum(jnp.where(lane == expert, both, 0.0), axis=1, keepdims=True)
    weight_out[first : first + count, :] = jnp.broadcast_to(both, (count, LANES))


def unpack_body(in_ref, gate_ref, rows, grads, weight_out, gate_turned, wide):
    for n in range(gate_turned.shape[1] // COLS):
        at = slice(n * COLS, (n + 1) * COLS)
        gate_turned[:, at] = gate_ref[at, :].T
    meta = rows.shape[1] // COLS
    wide[...] = in_ref[...].astype(F32)
    unpack_grads(wide, grads, 0)
    for i in range(meta):
        unpack_row(wide, rows, 0, i)
    unpack_weight(wide, weight_out, 0, meta)


def cot_body(
    other_ref, rows_in, grads_in, weight_in, down_ref,
    away_ref, cot_ref, weight_out, rows,
    wide, grads,
):
    count = other_ref.shape[0]
    width = rows.shape[1]
    hidden = cot_ref.shape[1]
    local = lax.axis_index("local")
    steps = hidden // COLS
    meta = width // COLS
    wide[...] = other_ref[...].astype(F32)
    unpack_grads(wide, grads, count)
    grads[:count, :] = grads_in[...]
    grad = grads[...]
    for n in range(steps):
        at = slice(n * COLS, (n + 1) * COLS)
        away_ref[:, at] = dot_nt(grad, down_ref[side_rows(1 - local, hidden, n), :]).astype(BF16)
    for n in range(steps):
        at = slice(n * COLS, (n + 1) * COLS)
        cot_ref[:, at] = dot_nt(grad, down_ref[side_rows(local, hidden, n), :])
    for i in range(meta):
        unpack_row(wide, rows, count, i)
    unpack_weight(wide, weight_out, count, meta)
    weight_out[:count, :] = weight_in[...]
    rows[:count, :] = rows_in[...]


def forward_body(rows_ref, gate_ref, up_ref, gate_out, up_out, act_ref):
    tokens = rows_ref[...]
    for n in range(gate_ref.shape[1] // COLS):
        cols = slice(n * COLS, (n + 1) * COLS)
        gate, up = dot(tokens, gate_ref[:, cols]), dot(tokens, up_ref[:, cols])
        gate_out[:, cols] = gate
        up_out[:, cols] = up
        act_ref[:, cols] = (gate * jax.nn.sigmoid(gate) * up).astype(BF16)


def input_body(
    cot_ref, recv_ref, gate_in, up_in, act_ref, weight_in, gate_ref, up_ref, turned_ref,
    mine_ref, other_ref,
    wide,
):
    total = cot_ref.shape[0]
    count = total // 2
    width = up_ref.shape[0]
    expert = lax.axis_index("chip") * 2 + lax.axis_index("core")
    gate, up = gate_in[...], up_in[...]
    sig = jax.nn.sigmoid(gate)
    cot = cot_ref[...] + recv_ref[...].astype(F32)
    prob = jnp.sum(cot * act_ref[...].astype(F32), axis=1, keepdims=True)
    hidden_grad = cot * weight_in[:, 0:1]
    gate_grad = (hidden_grad * up * sig * (1.0 + gate * (1.0 - sig))).astype(BF16)
    up_grad = (hidden_grad * (gate * sig)).astype(BF16)
    gate_turned, up_turned = gate_grad.T, up_grad.T
    steps = width // COLS
    for n in range(steps):
        at = slice(n * COLS, (n + 1) * COLS)
        if n * COLS < turned_ref.shape[1]:
            part = dot(gate_grad, turned_ref[:, at]) + dot_nt(up_grad, up_ref[at, :])
        else:
            part = (dot(gate_ref[at, :], gate_turned) + dot(up_ref[at, :], up_turned)).T
        wide[:, n, :] = part
    lane = lax.broadcasted_iota(jnp.int32, (total, LANES), 1)
    high, low = high_low(jnp.where(lane == expert, prob, 0.0))
    wide[:, steps, 0:LANES] = high
    wide[:, steps, LANES:COLS] = low
    for n in range(steps + 1, ROWS):
        wide[:, n, :] = jnp.zeros((total, COLS), F32)
    mine_ref[...] = wide[:count].astype(BF16)
    other_ref[...] = wide[count:].astype(BF16)


def routed_body(
    act_ref, recv_ref, weight_in, down_ref, in_mine, in_away, mine_ref, other_ref, wide
):
    total, hidden = act_ref.shape
    count = total // 2
    feats = down_ref.shape[1]
    local = lax.axis_index("local")
    weight = weight_in[:, 0:1]
    act, recv = act_ref[...], recv_ref[...]
    own = pl.ds(pl.multiple_of(local * hidden, COLS), hidden)
    away = pl.ds(pl.multiple_of((1 - local) * hidden, COLS), hidden)
    for n in range(feats // COLS):
        cols = slice(n * COLS, (n + 1) * COLS)
        part = dot(act, down_ref[own, cols]) + dot(recv, down_ref[away, cols])
        part = part.astype(BF16).astype(F32) * weight
        wide[:, 2 * n, :] = part[:, :LANES]
        wide[:, 2 * n + 1, :] = part[:, LANES:]
    for n in range(feats // LANES, ROWS):
        wide[:, n, :] = jnp.zeros((total, LANES), F32)
    for ref, part, at in ((mine_ref, in_mine, 0), (other_ref, in_away, count)):
        ref[:, :, 0:COLS] = part[...]
        ref[:, :, COLS:SPAN] = wide[at : at + count].astype(BF16)


def final_body(in_ref, named_ref, comb_ref, grad_ref, prob_ref, wide):
    groups = in_ref.shape[0]
    width = comb_ref.shape[2]
    half = width // 2
    for j in range(2):
        total = in_ref[j].astype(F32)
        for i in range(j + 2, groups, 2):
            total = total + in_ref[i].astype(F32)
        wide[j] = total
    meta = width // COLS
    total = wide[0] + wide[1]
    grad_ref[0] = jnp.concatenate([total[c : c + 1, 0:COLS] for c in range(meta)], axis=1).astype(BF16)
    comb_ref[0] = jnp.concatenate(
        [wide[j, c : c + 1, COLS:SPAN] for j in range(2) for c in range(half // LANES)], axis=1
    ).astype(BF16)
    prob = wide[0, meta : meta + 1, 0:COLS] + wide[1, meta : meta + 1, 0:COLS]
    prob = prob[:, 0:LANES] + prob[:, LANES:COLS]
    lane = lax.broadcasted_iota(jnp.int32, (1, LANES), 1)
    top = named_ref.shape[0]
    out = jnp.zeros((1, LANES), F32)
    for k in range(top):
        value = jnp.sum(named_ref[k : k + 1, :] * prob, axis=1, keepdims=True)
        out = jnp.where(lane == k, value, out)
    prob_ref[0] = out[:, :top]


def swap(x, axis):
    return lax.ppermute(x, axis, [(0, 1), (1, 0)])


def fast_device(tokens, expert_ids, route_probs, gate_weight, up_weight, down_weight, out_grad):
    groups = lax.axis_size("chip") * 2
    total = 2 * groups
    width = tokens.shape[2]
    hidden = gate_weight.shape[2]
    feats = down_weight.shape[2]
    one = width * hidden * 2
    gate_w, up_w, down_w = gate_weight[0], up_weight[0], down_weight[0]
    packed, named = call(
        pack_body,
        [shaped((groups, ROWS, SPAN), BF16), shaped((expert_ids.shape[2], LANES), F32)],
        [ANY] * 7,
        [
            pltpu.VMEM((ROWS, SPAN), F32),
            pltpu.SMEM(expert_ids.shape, expert_ids.dtype),
            pltpu.SMEM(route_probs.shape, route_probs.dtype),
            pltpu.VMEM(tokens.shape, BF16),
            pltpu.VMEM(out_grad.shape, BF16),
            pltpu.SemaphoreType.DMA((4,)),
        ],
        moved=12 * one,
    )(*in_hbm(expert_ids, route_probs, tokens, out_grad, gate_w, up_w, down_w))
    own = lax.all_to_all(packed, ("chip", "local"), split_axis=0, concat_axis=0, tiled=True)
    other = swap(own, "core")
    early = width // COLS * 8 // 14 * COLS
    own_rows, own_grads, own_weight, gate_turned = call(
        unpack_body,
        [
            shaped((groups, width), BF16),
            shaped((groups, feats), BF16),
            shaped((groups, LANES), F32),
            pltpu.VMEM((hidden, early), BF16),
        ],
        [VMEM, VMEM],
        [pltpu.VMEM((groups, ROWS, SPAN), F32)],
        moved=one // 4,
    )(own, gate_w)
    away, cot, weight, rows = call(
        cot_body,
        [
            shaped((total, hidden), BF16),
            shaped((total, hidden), F32),
            shaped((total, LANES), F32),
            shaped((total, width), BF16),
        ],
        [VMEM] * 5,
        [pltpu.VMEM((groups, ROWS, SPAN), F32), pltpu.VMEM((total, feats), BF16)],
        products=total * one,
        moved=one,
    )(other, own_rows, own_grads, own_weight, down_w)
    cot_recv = swap(away, "local")
    gate, up, act = call(
        forward_body,
        [
            shaped((total, hidden), F32),
            shaped((total, hidden), F32),
            shaped((total, hidden), BF16),
        ],
        [VMEM] * 3,
        products=total * 2 * one,
        moved=2 * one,
    )(rows, gate_w, up_w)
    act_recv = swap(act, "local")
    in_mine, in_away = call(
        input_body,
        [shaped((groups, ROWS, COLS), BF16)] * 2,
        [VMEM] * 9,
        [pltpu.VMEM((total, ROWS, COLS), F32)],
        products=total * 2 * one,
        moved=2 * one,
    )(cot, cot_recv, gate, up, act, weight, gate_w, up_w, gate_turned)
    mine, away = call(
        routed_body,
        [shaped((groups, ROWS, SPAN), BF16)] * 2,
        [VMEM] * 6,
        [pltpu.VMEM((total, ROWS, LANES), F32)],
        products=total * one,
        moved=one,
    )(act, act_recv, weight, down_w, in_mine, in_away)
    summed = (mine.astype(F32) + swap(away, "core").astype(F32)).astype(BF16)
    back = lax.all_to_all(summed, ("chip", "local"), split_axis=0, concat_axis=0, tiled=True)
    return call(
        final_body,
        [
            shaped((1, 1, width), BF16),
            shaped((1, 1, width), BF16),
            shaped(expert_ids.shape, F32),
        ],
        [VMEM, VMEM],
        [pltpu.VMEM((2, ROWS, SPAN), F32)],
    )(back, named)


def selector(flags, capacity):
    live = (flags > 0).astype(jnp.int32)
    order = jnp.cumsum(live) - live
    slot_ids = lax.broadcasted_iota(jnp.int32, (capacity, flags.shape[0]), 0)
    return ((slot_ids == order[None, :]) & (live[None, :] > 0)).astype(jnp.bfloat16)


def per_device(tokens, expert_ids, route_probs, gate_weight, up_weight, down_weight, out_grad):
    node_count = lax.axis_size("node")
    token_count = tokens.shape[1]
    width = tokens.shape[2]
    top_count = expert_ids.shape[2]
    column_rows = token_count * node_count
    capacity = min(column_rows, 5 * column_rows * top_count // (2 * node_count))
    slot_count = node_count * token_count
    gate_w = gate_weight[0]
    up_w = up_weight[0]
    down_w = down_weight[0]
    hidden_dev = gate_w.shape[1]
    onehot = (expert_ids[0][..., None] == jnp.arange(node_count, dtype=jnp.int32)).astype(
        jnp.float32
    )
    weights = jnp.einsum("tk,tke->te", route_probs[0], onehot)
    member = jnp.sum(onehot, axis=1)
    own_rows = tokens[0]
    zero_value = jnp.zeros((), jnp.bfloat16)
    own_flags = member.T.astype(jnp.bfloat16)
    send_rows = jnp.where(own_flags[:, :, None] > 0, own_rows[None], zero_value)
    recv_rows, recv_flags = (
        lax.all_to_all(send_rows, "node", split_axis=0, concat_axis=0, tiled=True),
        lax.all_to_all(own_flags, "node", split_axis=0, concat_axis=0, tiled=True),
    )
    select = selector(recv_flags.reshape(slot_count), capacity)
    packed_rows = jnp.dot(
        select, recv_rows.reshape(slot_count, width), preferred_element_type=jnp.float32
    ).astype(jnp.bfloat16)
    piece = lax.all_gather(packed_rows, "local", axis=0, tiled=True)
    gate_part = jnp.dot(piece, gate_w, preferred_element_type=jnp.float32)
    up_part = jnp.dot(piece, up_w, preferred_element_type=jnp.float32)
    joined = jnp.concatenate([gate_part, up_part], axis=1)
    gate_pre = joined[:, :hidden_dev]
    up_pre = joined[:, hidden_dev:]
    sigmoid_gate = jax.nn.sigmoid(gate_pre)
    silu_gate = gate_pre * sigmoid_gate
    hidden = (silu_gate * up_pre).astype(jnp.bfloat16)
    block = down_w
    routed_part = jnp.dot(
        lax.all_gather(hidden, "local", axis=1, tiled=True),
        block,
        preferred_element_type=jnp.float32,
    )
    routed_cols = routed_part.astype(jnp.bfloat16)
    routed_own = lax.all_to_all(routed_cols, "local", split_axis=0, concat_axis=1, tiled=True)
    routed_slots = jnp.dot(select.T, routed_own, preferred_element_type=jnp.float32).astype(
        jnp.bfloat16
    )
    routed_back = lax.all_to_all(
        routed_slots.reshape(node_count, token_count, width),
        "node",
        split_axis=0,
        concat_axis=0,
        tiled=True,
    )
    routed_wide = routed_back.astype(jnp.float32)
    combined = jnp.einsum("te,etd->td", weights, routed_wide).astype(jnp.bfloat16)
    grad_wide = out_grad[0].astype(jnp.float32)
    prob_terms = jnp.einsum("td,etd->te", grad_wide, routed_wide)
    prob_grad = jnp.einsum("te,tke->tk", prob_terms, onehot)
    scaled = (weights.T[:, :, None] * grad_wide[None]).astype(jnp.bfloat16)
    grad_recv = lax.all_to_all(scaled, "node", split_axis=0, concat_axis=0, tiled=True)
    grad_own = jnp.dot(
        select, grad_recv.reshape(slot_count, width), preferred_element_type=jnp.float32
    ).astype(jnp.bfloat16)
    grad_cols = lax.all_to_all(grad_own, "local", split_axis=1, concat_axis=0, tiled=True)
    block = down_w
    hidden_grad = (
        lax.psum_scatter(
            lax.dot_general(
                block, grad_cols, (((1,), (1,)), ((), ())), preferred_element_type=jnp.float32
            ).astype(jnp.bfloat16),
            "local",
            scatter_dimension=0,
            tiled=True,
        )
        .astype(jnp.float32)
        .T
    )
    gate_grad = (
        hidden_grad * up_pre * sigmoid_gate * (1.0 + gate_pre * (1.0 - sigmoid_gate))
    ).astype(jnp.bfloat16)
    up_grad = (hidden_grad * silu_gate).astype(jnp.bfloat16)
    first = lax.dot_general(
        gate_grad, gate_w, (((1,), (1,)), ((), ())), preferred_element_type=jnp.float32
    )
    second = lax.dot_general(
        up_grad, up_w, (((1,), (1,)), ((), ())), preferred_element_type=jnp.float32
    )
    input_own = lax.psum_scatter(
        (first + second).astype(jnp.bfloat16), "local", scatter_dimension=0, tiled=True
    )
    input_slots = jnp.dot(select.T, input_own, preferred_element_type=jnp.float32).astype(
        jnp.bfloat16
    )
    input_back = lax.all_to_all(
        input_slots.reshape(node_count, token_count, width),
        "node",
        split_axis=0,
        concat_axis=0,
        tiled=True,
    )
    input_grad = jnp.sum(input_back.astype(jnp.float32), axis=0).astype(jnp.bfloat16)
    return (combined[None], input_grad[None], prob_grad[None])


def solution(mesh):
    node, local = mesh.shape["node"], mesh.shape["local"]
    if local == 2 and node % 2 == 0 and node <= 16:
        mesh = Mesh(mesh.devices.reshape(node // 2, 2, local), ("chip", "core", "local"))
        body, nodes = fast_device, ("chip", "core")
    else:
        body, nodes = per_device, "node"
    rows = P("local", nodes, None)
    weights = P(nodes, None, "local")
    return jax.shard_map(
        body,
        mesh=mesh,
        in_specs=(rows, rows, rows, weights, weights, weights, rows),
        out_specs=(rows, rows, rows),
        check_vma=False,
    )
```

```python
import functools

import jax
import jax.numpy as jnp
from jax import lax
from jax.experimental import pallas as pl
from jax.experimental.pallas import tpu as pltpu
from jax.sharding import Mesh
from jax.sharding import PartitionSpec as P

BF16 = jnp.bfloat16
F32 = jnp.float32
LANES = 128
COLS = 256
ROWS = 16
SPAN = COLS + LANES

NT = (((1,), (1,)), ((), ()))
VMEM = pl.BlockSpec(memory_space=pltpu.VMEM)
ANY = pl.BlockSpec(memory_space=pl.ANY)


def call(body, outs, ins, scratch=(), products=0, moved=0):
    return pl.pallas_call(
        body,
        out_shape=tuple(outs),
        in_specs=ins,
        out_specs=tuple(VMEM for _ in outs),
        scratch_shapes=list(scratch),
        compiler_params=pltpu.CompilerParams(vmem_limit_bytes=12 << 20),
        cost_estimate=pl.CostEstimate(
            flops=int(products), bytes_accessed=int(moved), transcendentals=0
        ),
    )


def shaped(shape, dtype):
    return jax.ShapeDtypeStruct(shape, dtype)


def in_hbm(*arrays):
    return tuple(pltpu.with_memory_space_constraint(a, pltpu.HBM) for a in arrays)


def dot(a, b):
    return jnp.dot(a, b, preferred_element_type=F32)


def dot_nt(a, b):
    return lax.dot_general(a, b, NT, preferred_element_type=F32)


def high_low(x):
    high = x.astype(BF16).astype(F32)
    return high, x - high


def pack_body(
    ids_hbm, probs_hbm, tok_hbm, grad_hbm, gate_hbm, up_hbm, down_hbm, out_ref, named_ref,
    wide, ids_ref, probs_ref, tok_ref, grad_ref, sems
):
    pairs = ((ids_hbm, ids_ref), (probs_hbm, probs_ref), (tok_hbm, tok_ref), (grad_hbm, grad_ref))
    copies = [pltpu.make_async_copy(a, b, sems.at[i]) for i, (a, b) in enumerate(pairs)]
    for copy in copies:
        copy.start()
    wide[...] = jnp.zeros_like(wide)
    lane = lax.broadcasted_iota(jnp.int32, (1, LANES), 1)
    weight = jnp.zeros((1, LANES), F32)
    for copy in copies:
        copy.wait()
    for k in range(ids_ref.shape[2]):
        named = lane == ids_ref[0, 0, k]
        weight = jnp.where(named, probs_ref[0, 0, k], weight)
        named_ref[k : k + 1, :] = named.astype(F32)
    width = tok_ref.shape[2]
    meta = width // COLS
    half = width // 2
    for i in range(meta):
        wide[i : i + 1, 0:COLS] = tok_ref[0, :, i * COLS : (i + 1) * COLS].astype(F32)
    high, low = high_low(weight)
    wide[meta : meta + 1, 0:LANES] = high
    wide[meta : meta + 1, LANES:COLS] = low
    for j in range(2):
        for i in range(half // LANES):
            at = j * half + i * LANES
            wide[i : i + 1, COLS:SPAN] = grad_ref[0, :, at : at + LANES].astype(F32)
        block = wide[...].astype(BF16)
        for i in range(j, out_ref.shape[0], 2):
            out_ref[i] = block


def side_rows(local, hidden, n):
    return pl.ds(pl.multiple_of(local * hidden + n * COLS, COLS), COLS)


def unpack_grads(wide, grads, first):
    count = wide.shape[0]
    for i in range(grads.shape[1] // LANES):
        grads[first : first + count, i * LANES : (i + 1) * LANES] = wide[:, i, COLS:SPAN].astype(BF16)


def unpack_row(wide, rows, first, i):
    count = wide.shape[0]
    rows[first : first + count, i * COLS : (i + 1) * COLS] = wide[:, i, 0:COLS].astype(BF16)


def unpack_weight(wide, weight_out, first, meta):
    count = wide.shape[0]
    expert = lax.axis_index("chip") * 2 + lax.axis_index("core")
    lane = lax.broadcasted_iota(jnp.int32, (count, LANES), 1)
    both = wide[:, meta, 0:LANES] + wide[:, meta, LANES:COLS]
    both = jnp.sum(jnp.where(lane == expert, both, 0.0), axis=1, keepdims=True)
    weight_out[first : first + count, :] = jnp.broadcast_to(both, (count, LANES))


def unpack_body(in_ref, gate_ref, rows, grads, weight_out, gate_turned, wide):
    for n in range(gate_turned.shape[1] // COLS):
        at = slice(n * COLS, (n + 1) * COLS)
        gate_turned[:, at] = gate_ref[at, :].T
    meta = rows.shape[1] // COLS
    wide[...] = in_ref[...].astype(F32)
    unpack_grads(wide, grads, 0)
    for i in range(meta):
        unpack_row(wide, rows, 0, i)
    unpack_weight(wide, weight_out, 0, meta)


def cot_body(
    other_ref, rows_in, grads_in, weight_in, down_ref,
    away_ref, cot_ref, weight_out, rows,
    wide, grads,
):
    count = other_ref.shape[0]
    width = rows.shape[1]
    hidden = cot_ref.shape[1]
    local = lax.axis_index("local")
    steps = hidden // COLS
    meta = width // COLS
    wide[...] = other_ref[...].astype(F32)
    unpack_grads(wide, grads, count)
    grads[:count, :] = grads_in[...]
    grad = grads[...]
    for n in range(steps):
        at = slice(n * COLS, (n + 1) * COLS)
        away_ref[:, at] = dot_nt(grad, down_ref[side_rows(1 - local, hidden, n), :]).astype(BF16)
    for n in range(steps):
        at = slice(n * COLS, (n + 1) * COLS)
        cot_ref[:, at] = dot_nt(grad, down_ref[side_rows(local, hidden, n), :])
    for i in range(meta):
        unpack_row(wide, rows, count, i)
    unpack_weight(wide, weight_out, count, meta)
    weight_out[:count, :] = weight_in[...]
    rows[:count, :] = rows_in[...]


def forward_body(rows_ref, gate_ref, up_ref, gate_out, up_out, act_ref, up_turned):
    tokens = rows_ref[...]
    steps = gate_ref.shape[1] // COLS
    for n in range(steps):
        for i in range(n, up_turned.shape[1] // COLS, steps):
            at = slice(i * COLS, (i + 1) * COLS)
            up_turned[:, at] = up_ref[at, :].T
        cols = slice(n * COLS, (n + 1) * COLS)
        gate, up = dot(tokens, gate_ref[:, cols]), dot(tokens, up_ref[:, cols])
        gate_out[:, cols] = gate
        up_out[:, cols] = up
        act_ref[:, cols] = (gate * jax.nn.sigmoid(gate) * up).astype(BF16)


def input_body(
    cot_ref, recv_ref, gate_in, up_in, act_ref, weight_in, gate_ref, up_ref, turned_ref, up_turned_ref,
    mine_ref, other_ref,
    wide,
):
    total = cot_ref.shape[0]
    count = total // 2
    width = up_ref.shape[0]
    expert = lax.axis_index("chip") * 2 + lax.axis_index("core")
    gate, up = gate_in[...], up_in[...]
    sig = jax.nn.sigmoid(gate)
    cot = cot_ref[...] + recv_ref[...].astype(F32)
    prob = jnp.sum(cot * act_ref[...].astype(F32), axis=1, keepdims=True)
    hidden_grad = cot * weight_in[:, 0:1]
    gate_grad = (hidden_grad * up * sig * (1.0 + gate * (1.0 - sig))).astype(BF16)
    up_grad = (hidden_grad * (gate * sig)).astype(BF16)
    steps = width // COLS
    for n in range(steps):
        at = slice(n * COLS, (n + 1) * COLS)
        if n * COLS < turned_ref.shape[1]:
            part = dot(gate_grad, turned_ref[:, at])
        else:
            part = dot_nt(gate_grad, gate_ref[at, :])
        if n * COLS < up_turned_ref.shape[1]:
            part += dot(up_grad, up_turned_ref[:, at])
        else:
            part += dot_nt(up_grad, up_ref[at, :])
        wide[:, n, :] = part
    lane = lax.broadcasted_iota(jnp.int32, (total, LANES), 1)
    high, low = high_low(jnp.where(lane == expert, prob, 0.0))
    wide[:, steps, 0:LANES] = high
    wide[:, steps, LANES:COLS] = low
    for n in range(steps + 1, ROWS):
        wide[:, n, :] = jnp.zeros((total, COLS), F32)
    mine_ref[...] = wide[:count].astype(BF16)
    other_ref[...] = wide[count:].astype(BF16)


def routed_body(
    act_ref, recv_ref, weight_in, down_ref, in_mine, in_away, mine_ref, other_ref, wide
):
    total, hidden = act_ref.shape
    count = total // 2
    feats = down_ref.shape[1]
    local = lax.axis_index("local")
    weight = weight_in[:, 0:1]
    act, recv = act_ref[...], recv_ref[...]
    own = pl.ds(pl.multiple_of(local * hidden, COLS), hidden)
    away = pl.ds(pl.multiple_of((1 - local) * hidden, COLS), hidden)
    for n in range(feats // COLS):
        cols = slice(n * COLS, (n + 1) * COLS)
        part = dot(act, down_ref[own, cols]) + dot(recv, down_ref[away, cols])
        part = part.astype(BF16).astype(F32) * weight
        wide[:, 2 * n, :] = part[:, :LANES]
        wide[:, 2 * n + 1, :] = part[:, LANES:]
    for n in range(feats // LANES, ROWS):
        wide[:, n, :] = jnp.zeros((total, LANES), F32)
    for ref, part, at in ((mine_ref, in_mine, 0), (other_ref, in_away, count)):
        ref[:, :, 0:COLS] = part[...]
        ref[:, :, COLS:SPAN] = wide[at : at + count].astype(BF16)


def final_body(in_ref, named_ref, comb_ref, grad_ref, prob_ref, wide):
    groups = in_ref.shape[0]
    width = comb_ref.shape[2]
    half = width // 2
    for j in range(2):
        total = in_ref[j].astype(F32)
        for i in range(j + 2, groups, 2):
            total = total + in_ref[i].astype(F32)
        wide[j] = total
    meta = width // COLS
    total = wide[0] + wide[1]
    grad_ref[0] = jnp.concatenate([total[c : c + 1, 0:COLS] for c in range(meta)], axis=1).astype(BF16)
    comb_ref[0] = jnp.concatenate(
        [wide[j, c : c + 1, COLS:SPAN] for j in range(2) for c in range(half // LANES)], axis=1
    ).astype(BF16)
    prob = wide[0, meta : meta + 1, 0:COLS] + wide[1, meta : meta + 1, 0:COLS]
    prob = prob[:, 0:LANES] + prob[:, LANES:COLS]
    lane = lax.broadcasted_iota(jnp.int32, (1, LANES), 1)
    top = named_ref.shape[0]
    out = jnp.zeros((1, LANES), F32)
    for k in range(top):
        value = jnp.sum(named_ref[k : k + 1, :] * prob, axis=1, keepdims=True)
        out = jnp.where(lane == k, value, out)
    prob_ref[0] = out[:, :top]


def swap(x, axis):
    return lax.ppermute(x, axis, [(0, 1), (1, 0)])


def fast_device(tokens, expert_ids, route_probs, gate_weight, up_weight, down_weight, out_grad):
    groups = lax.axis_size("chip") * 2
    total = 2 * groups
    width = tokens.shape[2]
    hidden = gate_weight.shape[2]
    feats = down_weight.shape[2]
    one = width * hidden * 2
    gate_w, up_w, down_w = gate_weight[0], up_weight[0], down_weight[0]
    packed, named = call(
        pack_body,
        [shaped((groups, ROWS, SPAN), BF16), shaped((expert_ids.shape[2], LANES), F32)],
        [ANY] * 7,
        [
            pltpu.VMEM((ROWS, SPAN), F32),
            pltpu.SMEM(expert_ids.shape, expert_ids.dtype),
            pltpu.SMEM(route_probs.shape, route_probs.dtype),
            pltpu.VMEM(tokens.shape, BF16),
            pltpu.VMEM(out_grad.shape, BF16),
            pltpu.SemaphoreType.DMA((4,)),
        ],
        moved=12 * one,
    )(*in_hbm(expert_ids, route_probs, tokens, out_grad, gate_w, up_w, down_w))
    own = lax.all_to_all(packed, ("chip", "local"), split_axis=0, concat_axis=0, tiled=True)
    other = swap(own, "core")
    early = width // COLS * 8 // 14 * COLS
    own_rows, own_grads, own_weight, gate_turned = call(
        unpack_body,
        [
            shaped((groups, width), BF16),
            shaped((groups, feats), BF16),
            shaped((groups, LANES), F32),
            pltpu.VMEM((hidden, early), BF16),
        ],
        [VMEM, VMEM],
        [pltpu.VMEM((groups, ROWS, SPAN), F32)],
        moved=one // 4,
    )(own, gate_w)
    away, cot, weight, rows = call(
        cot_body,
        [
            shaped((total, hidden), BF16),
            shaped((total, hidden), F32),
            shaped((total, LANES), F32),
            shaped((total, width), BF16),
        ],
        [VMEM] * 5,
        [pltpu.VMEM((groups, ROWS, SPAN), F32), pltpu.VMEM((total, feats), BF16)],
        products=total * one,
        moved=one,
    )(other, own_rows, own_grads, own_weight, down_w)
    cot_recv = swap(away, "local")
    gate, up, act, up_turned = call(
        forward_body,
        [
            shaped((total, hidden), F32),
            shaped((total, hidden), F32),
            shaped((total, hidden), BF16),
            pltpu.VMEM((hidden, width // COLS * 14 // 14 * COLS), BF16),
        ],
        [VMEM] * 3,
        products=total * 2 * one,
        moved=2 * one,
    )(rows, gate_w, up_w)
    act_recv = swap(act, "local")
    in_mine, in_away = call(
        input_body,
        [shaped((groups, ROWS, COLS), BF16)] * 2,
        [VMEM] * 10,
        [pltpu.VMEM((total, ROWS, COLS), F32)],
        products=total * 2 * one,
        moved=2 * one,
    )(cot, cot_recv, gate, up, act, weight, gate_w, up_w, gate_turned, up_turned)
    mine, away = call(
        routed_body,
        [shaped((groups, ROWS, SPAN), BF16)] * 2,
        [VMEM] * 6,
        [pltpu.VMEM((total, ROWS, LANES), F32)],
        products=total * one,
        moved=one,
    )(act, act_recv, weight, down_w, in_mine, in_away)
    summed = (mine.astype(F32) + swap(away, "core").astype(F32)).astype(BF16)
    back = lax.all_to_all(summed, ("chip", "local"), split_axis=0, concat_axis=0, tiled=True)
    return call(
        final_body,
        [
            shaped((1, 1, width), BF16),
            shaped((1, 1, width), BF16),
            shaped(expert_ids.shape, F32),
        ],
        [VMEM, VMEM],
        [pltpu.VMEM((2, ROWS, SPAN), F32)],
    )(back, named)


def selector(flags, capacity):
    live = (flags > 0).astype(jnp.int32)
    order = jnp.cumsum(live) - live
    slot_ids = lax.broadcasted_iota(jnp.int32, (capacity, flags.shape[0]), 0)
    return ((slot_ids == order[None, :]) & (live[None, :] > 0)).astype(jnp.bfloat16)


def per_device(tokens, expert_ids, route_probs, gate_weight, up_weight, down_weight, out_grad):
    node_count = lax.axis_size("node")
    token_count = tokens.shape[1]
    width = tokens.shape[2]
    top_count = expert_ids.shape[2]
    column_rows = token_count * node_count
    capacity = min(column_rows, 5 * column_rows * top_count // (2 * node_count))
    slot_count = node_count * token_count
    gate_w = gate_weight[0]
    up_w = up_weight[0]
    down_w = down_weight[0]
    hidden_dev = gate_w.shape[1]
    onehot = (expert_ids[0][..., None] == jnp.arange(node_count, dtype=jnp.int32)).astype(
        jnp.float32
    )
    weights = jnp.einsum("tk,tke->te", route_probs[0], onehot)
    member = jnp.sum(onehot, axis=1)
    own_rows = tokens[0]
    zero_value = jnp.zeros((), jnp.bfloat16)
    own_flags = member.T.astype(jnp.bfloat16)
    send_rows = jnp.where(own_flags[:, :, None] > 0, own_rows[None], zero_value)
    recv_rows, recv_flags = (
        lax.all_to_all(send_rows, "node", split_axis=0, concat_axis=0, tiled=True),
        lax.all_to_all(own_flags, "node", split_axis=0, concat_axis=0, tiled=True),
    )
    select = selector(recv_flags.reshape(slot_count), capacity)
    packed_rows = jnp.dot(
        select, recv_rows.reshape(slot_count, width), preferred_element_type=jnp.float32
    ).astype(jnp.bfloat16)
    piece = lax.all_gather(packed_rows, "local", axis=0, tiled=True)
    gate_part = jnp.dot(piece, gate_w, preferred_element_type=jnp.float32)
    up_part = jnp.dot(piece, up_w, preferred_element_type=jnp.float32)
    joined = jnp.concatenate([gate_part, up_part], axis=1)
    gate_pre = joined[:, :hidden_dev]
    up_pre = joined[:, hidden_dev:]
    sigmoid_gate = jax.nn.sigmoid(gate_pre)
    silu_gate = gate_pre * sigmoid_gate
    hidden = (silu_gate * up_pre).astype(jnp.bfloat16)
    block = down_w
    routed_part = jnp.dot(
        lax.all_gather(hidden, "local", axis=1, tiled=True),
        block,
        preferred_element_type=jnp.float32,
    )
    routed_cols = routed_part.astype(jnp.bfloat16)
    routed_own = lax.all_to_all(routed_cols, "local", split_axis=0, concat_axis=1, tiled=True)
    routed_slots = jnp.dot(select.T, routed_own, preferred_element_type=jnp.float32).astype(
        jnp.bfloat16
    )
    routed_back = lax.all_to_all(
        routed_slots.reshape(node_count, token_count, width),
        "node",
        split_axis=0,
        concat_axis=0,
        tiled=True,
    )
    routed_wide = routed_back.astype(jnp.float32)
    combined = jnp.einsum("te,etd->td", weights, routed_wide).astype(jnp.bfloat16)
    grad_wide = out_grad[0].astype(jnp.float32)
    prob_terms = jnp.einsum("td,etd->te", grad_wide, routed_wide)
    prob_grad = jnp.einsum("te,tke->tk", prob_terms, onehot)
    scaled = (weights.T[:, :, None] * grad_wide[None]).astype(jnp.bfloat16)
    grad_recv = lax.all_to_all(scaled, "node", split_axis=0, concat_axis=0, tiled=True)
    grad_own = jnp.dot(
        select, grad_recv.reshape(slot_count, width), preferred_element_type=jnp.float32
    ).astype(jnp.bfloat16)
    grad_cols = lax.all_to_all(grad_own, "local", split_axis=1, concat_axis=0, tiled=True)
    block = down_w
    hidden_grad = (
        lax.psum_scatter(
            lax.dot_general(
                block, grad_cols, (((1,), (1,)), ((), ())), preferred_element_type=jnp.float32
            ).astype(jnp.bfloat16),
            "local",
            scatter_dimension=0,
            tiled=True,
        )
        .astype(jnp.float32)
        .T
    )
    gate_grad = (
        hidden_grad * up_pre * sigmoid_gate * (1.0 + gate_pre * (1.0 - sigmoid_gate))
    ).astype(jnp.bfloat16)
    up_grad = (hidden_grad * silu_gate).astype(jnp.bfloat16)
    first = lax.dot_general(
        gate_grad, gate_w, (((1,), (1,)), ((), ())), preferred_element_type=jnp.float32
    )
    second = lax.dot_general(
        up_grad, up_w, (((1,), (1,)), ((), ())), preferred_element_type=jnp.float32
    )
    input_own = lax.psum_scatter(
        (first + second).astype(jnp.bfloat16), "local", scatter_dimension=0, tiled=True
    )
    input_slots = jnp.dot(select.T, input_own, preferred_element_type=jnp.float32).astype(
        jnp.bfloat16
    )
    input_back = lax.all_to_all(
        input_slots.reshape(node_count, token_count, width),
        "node",
        split_axis=0,
        concat_axis=0,
        tiled=True,
    )
    input_grad = jnp.sum(input_back.astype(jnp.float32), axis=0).astype(jnp.bfloat16)
    return (combined[None], input_grad[None], prob_grad[None])


def solution(mesh):
    node, local = mesh.shape["node"], mesh.shape["local"]
    if local == 2 and node % 2 == 0 and node <= 16:
        mesh = Mesh(mesh.devices.reshape(node // 2, 2, local), ("chip", "core", "local"))
        body, nodes = fast_device, ("chip", "core")
    else:
        body, nodes = per_device, "node"
    rows = P("local", nodes, None)
    weights = P(nodes, None, "local")
    return jax.shard_map(
        body,
        mesh=mesh,
        in_specs=(rows, rows, rows, weights, weights, weights, rows),
        out_specs=(rows, rows, rows),
        check_vma=False,
    )
```

```python
import functools

import jax
import jax.numpy as jnp
from jax import lax
from jax.experimental import pallas as pl
from jax.experimental.pallas import tpu as pltpu
from jax.sharding import Mesh
from jax.sharding import PartitionSpec as P

BF16 = jnp.bfloat16
F32 = jnp.float32
LANES = 128
COLS = 256
ROWS = 16
SPAN = COLS + LANES

NT = (((1,), (1,)), ((), ()))
VMEM = pl.BlockSpec(memory_space=pltpu.VMEM)
ANY = pl.BlockSpec(memory_space=pl.ANY)


def call(body, outs, ins, scratch=(), products=0, moved=0):
    return pl.pallas_call(
        body,
        out_shape=tuple(outs),
        in_specs=ins,
        out_specs=tuple(VMEM for _ in outs),
        scratch_shapes=list(scratch),
        compiler_params=pltpu.CompilerParams(vmem_limit_bytes=12 << 20),
        cost_estimate=pl.CostEstimate(
            flops=int(products), bytes_accessed=int(moved), transcendentals=0
        ),
    )


def shaped(shape, dtype):
    return jax.ShapeDtypeStruct(shape, dtype)


def in_hbm(*arrays):
    return tuple(pltpu.with_memory_space_constraint(a, pltpu.HBM) for a in arrays)


def dot(a, b):
    return jnp.dot(a, b, preferred_element_type=F32)


def dot_nt(a, b):
    return lax.dot_general(a, b, NT, preferred_element_type=F32)


def high_low(x):
    high = x.astype(BF16).astype(F32)
    return high, x - high


def pack_body(
    ids_hbm, probs_hbm, tok_hbm, grad_hbm, gate_hbm, up_hbm, down_hbm, out_ref, named_ref,
    wide, ids_ref, probs_ref, tok_ref, grad_ref, sems
):
    pairs = ((ids_hbm, ids_ref), (probs_hbm, probs_ref), (tok_hbm, tok_ref), (grad_hbm, grad_ref))
    copies = [pltpu.make_async_copy(a, b, sems.at[i]) for i, (a, b) in enumerate(pairs)]
    for copy in copies:
        copy.start()
    wide[...] = jnp.zeros_like(wide)
    lane = lax.broadcasted_iota(jnp.int32, (1, LANES), 1)
    weight = jnp.zeros((1, LANES), F32)
    for copy in copies:
        copy.wait()
    for k in range(ids_ref.shape[2]):
        named = lane == ids_ref[0, 0, k]
        weight = jnp.where(named, probs_ref[0, 0, k], weight)
        named_ref[k : k + 1, :] = named.astype(F32)
    width = tok_ref.shape[2]
    meta = width // COLS
    half = width // 2
    for i in range(meta):
        wide[i : i + 1, 0:COLS] = tok_ref[0, :, i * COLS : (i + 1) * COLS].astype(F32)
    high, low = high_low(weight)
    wide[meta : meta + 1, 0:LANES] = high
    wide[meta : meta + 1, LANES:COLS] = low
    for j in range(2):
        for i in range(half // LANES):
            at = j * half + i * LANES
            wide[i : i + 1, COLS:SPAN] = grad_ref[0, :, at : at + LANES].astype(F32)
        block = wide[...].astype(BF16)
        for i in range(j, out_ref.shape[0], 2):
            out_ref[i] = block


def side_rows(local, hidden, n):
    return pl.ds(pl.multiple_of(local * hidden + n * COLS, COLS), COLS)


def unpack_grads(wide, grads, first):
    count = wide.shape[0]
    for i in range(grads.shape[1] // LANES):
        grads[first : first + count, i * LANES : (i + 1) * LANES] = wide[:, i, COLS:SPAN].astype(BF16)


def unpack_row(wide, rows, first, i):
    count = wide.shape[0]
    rows[first : first + count, i * COLS : (i + 1) * COLS] = wide[:, i, 0:COLS].astype(BF16)


def unpack_weight(wide, weight_out, first, meta):
    count = wide.shape[0]
    expert = lax.axis_index("chip") * 2 + lax.axis_index("core")
    lane = lax.broadcasted_iota(jnp.int32, (count, LANES), 1)
    both = wide[:, meta, 0:LANES] + wide[:, meta, LANES:COLS]
    both = jnp.sum(jnp.where(lane == expert, both, 0.0), axis=1, keepdims=True)
    weight_out[first : first + count, :] = jnp.broadcast_to(both, (count, LANES))


def unpack_body(in_ref, gate_ref, rows, grads, weight_out, gate_turned, wide):
    for n in range(gate_turned.shape[1] // COLS):
        at = slice(n * COLS, (n + 1) * COLS)
        gate_turned[:, at] = gate_ref[at, :].T
    meta = rows.shape[1] // COLS
    wide[...] = in_ref[...].astype(F32)
    unpack_grads(wide, grads, 0)
    for i in range(meta):
        unpack_row(wide, rows, 0, i)
    unpack_weight(wide, weight_out, 0, meta)


def cot_body(
    other_ref, rows_in, grads_in, weight_in, down_ref, gate_ref,
    away_ref, cot_ref, weight_out, rows, gate_late,
    wide, grads,
):
    count = other_ref.shape[0]
    width = rows.shape[1]
    hidden = cot_ref.shape[1]
    local = lax.axis_index("local")
    steps = hidden // COLS
    meta = width // COLS
    wide[...] = other_ref[...].astype(F32)
    unpack_grads(wide, grads, count)
    grads[:count, :] = grads_in[...]
    grad = grads[...].T
    late = gate_late.shape[1]
    for n in range(steps):
        at = slice(n * COLS, (n + 1) * COLS)
        away_ref[:, at] = dot(down_ref[side_rows(1 - local, hidden, n), :], grad).astype(BF16).T
        for i in range(n, late // COLS, steps):
            first = gate_ref.shape[0] - late + i * COLS
            gate_late[:, i * COLS : (i + 1) * COLS] = gate_ref[first : first + COLS, :].T
    for n in range(steps):
        at = slice(n * COLS, (n + 1) * COLS)
        cot_ref[:, at] = dot(down_ref[side_rows(local, hidden, n), :], grad).T
    for i in range(meta):
        unpack_row(wide, rows, count, i)
    unpack_weight(wide, weight_out, count, meta)
    weight_out[:count, :] = weight_in[...]
    rows[:count, :] = rows_in[...]


def forward_body(rows_ref, gate_ref, up_ref, gate_out, up_out, act_ref, up_turned):
    tokens = rows_ref[...]
    steps = gate_ref.shape[1] // COLS
    for n in range(steps):
        for i in range(n, up_turned.shape[1] // COLS, steps):
            at = slice(i * COLS, (i + 1) * COLS)
            up_turned[:, at] = up_ref[at, :].T
        cols = slice(n * COLS, (n + 1) * COLS)
        gate, up = dot(tokens, gate_ref[:, cols]), dot(tokens, up_ref[:, cols])
        gate_out[:, cols] = gate
        up_out[:, cols] = up
        act_ref[:, cols] = (gate * jax.nn.sigmoid(gate) * up).astype(BF16)


def input_body(
    cot_ref, recv_ref, gate_in, up_in, act_ref, weight_in, gate_first, gate_late, up_turned,
    mine_ref, other_ref,
    wide,
):
    total = cot_ref.shape[0]
    count = total // 2
    width, early = up_turned.shape[1], gate_first.shape[1]
    expert = lax.axis_index("chip") * 2 + lax.axis_index("core")
    gate, up = gate_in[...], up_in[...]
    sig = jax.nn.sigmoid(gate)
    cot = cot_ref[...] + recv_ref[...].astype(F32)
    prob = jnp.sum(cot * act_ref[...].astype(F32), axis=1, keepdims=True)
    hidden_grad = cot * weight_in[:, 0:1]
    gate_grad = (hidden_grad * up * sig * (1.0 + gate * (1.0 - sig))).astype(BF16)
    up_grad = (hidden_grad * (gate * sig)).astype(BF16)
    steps = width // COLS
    for n in range(steps):
        at = slice(n * COLS, (n + 1) * COLS)
        if n * COLS < early:
            gate_part = gate_first[:, at]
        else:
            gate_part = gate_late[:, n * COLS - early : (n + 1) * COLS - early]
        part = dot(gate_grad, gate_part) + dot(up_grad, up_turned[:, at])
        wide[:, n, :] = part
    lane = lax.broadcasted_iota(jnp.int32, (total, LANES), 1)
    high, low = high_low(jnp.where(lane == expert, prob, 0.0))
    wide[:, steps, 0:LANES] = high
    wide[:, steps, LANES:COLS] = low
    for n in range(steps + 1, ROWS):
        wide[:, n, :] = jnp.zeros((total, COLS), F32)
    mine_ref[...] = wide[:count].astype(BF16)
    other_ref[...] = wide[count:].astype(BF16)


def routed_body(
    act_ref, recv_ref, weight_in, down_ref, in_mine, in_away, mine_ref, other_ref, wide
):
    total, hidden = act_ref.shape
    count = total // 2
    feats = down_ref.shape[1]
    local = lax.axis_index("local")
    weight = weight_in[:, 0:1]
    act, recv = act_ref[...], recv_ref[...]
    own = pl.ds(pl.multiple_of(local * hidden, COLS), hidden)
    away = pl.ds(pl.multiple_of((1 - local) * hidden, COLS), hidden)
    for n in range(feats // COLS):
        cols = slice(n * COLS, (n + 1) * COLS)
        part = dot(act, down_ref[own, cols]) + dot(recv, down_ref[away, cols])
        part = part.astype(BF16).astype(F32) * weight
        wide[:, 2 * n, :] = part[:, :LANES]
        wide[:, 2 * n + 1, :] = part[:, LANES:]
    for n in range(feats // LANES, ROWS):
        wide[:, n, :] = jnp.zeros((total, LANES), F32)
    for ref, part, at in ((mine_ref, in_mine, 0), (other_ref, in_away, count)):
        ref[:, :, 0:COLS] = part[...]
        ref[:, :, COLS:SPAN] = wide[at : at + count].astype(BF16)


def final_body(in_ref, named_ref, comb_ref, grad_ref, prob_ref, wide):
    groups = in_ref.shape[0]
    width = comb_ref.shape[2]
    half = width // 2
    for j in range(2):
        total = in_ref[j].astype(F32)
        for i in range(j + 2, groups, 2):
            total = total + in_ref[i].astype(F32)
        wide[j] = total
    meta = width // COLS
    total = wide[0] + wide[1]
    grad_ref[0] = jnp.concatenate([total[c : c + 1, 0:COLS] for c in range(meta)], axis=1).astype(BF16)
    comb_ref[0] = jnp.concatenate(
        [wide[j, c : c + 1, COLS:SPAN] for j in range(2) for c in range(half // LANES)], axis=1
    ).astype(BF16)
    prob = wide[0, meta : meta + 1, 0:COLS] + wide[1, meta : meta + 1, 0:COLS]
    prob = prob[:, 0:LANES] + prob[:, LANES:COLS]
    lane = lax.broadcasted_iota(jnp.int32, (1, LANES), 1)
    top = named_ref.shape[0]
    out = jnp.zeros((1, LANES), F32)
    for k in range(top):
        value = jnp.sum(named_ref[k : k + 1, :] * prob, axis=1, keepdims=True)
        out = jnp.where(lane == k, value, out)
    prob_ref[0] = out[:, :top]


def swap(x, axis):
    return lax.ppermute(x, axis, [(0, 1), (1, 0)])


def fast_device(tokens, expert_ids, route_probs, gate_weight, up_weight, down_weight, out_grad):
    groups = lax.axis_size("chip") * 2
    total = 2 * groups
    width = tokens.shape[2]
    hidden = gate_weight.shape[2]
    feats = down_weight.shape[2]
    one = width * hidden * 2
    gate_w, up_w, down_w = gate_weight[0], up_weight[0], down_weight[0]
    packed, named = call(
        pack_body,
        [shaped((groups, ROWS, SPAN), BF16), shaped((expert_ids.shape[2], LANES), F32)],
        [ANY] * 7,
        [
            pltpu.VMEM((ROWS, SPAN), F32),
            pltpu.SMEM(expert_ids.shape, expert_ids.dtype),
            pltpu.SMEM(route_probs.shape, route_probs.dtype),
            pltpu.VMEM(tokens.shape, BF16),
            pltpu.VMEM(out_grad.shape, BF16),
            pltpu.SemaphoreType.DMA((4,)),
        ],
        moved=12 * one,
    )(*in_hbm(expert_ids, route_probs, tokens, out_grad, gate_w, up_w, down_w))
    own = lax.all_to_all(packed, ("chip", "local"), split_axis=0, concat_axis=0, tiled=True)
    other = swap(own, "core")
    early = width // COLS * 8 // 14 * COLS
    own_rows, own_grads, own_weight, gate_turned = call(
        unpack_body,
        [
            shaped((groups, width), BF16),
            shaped((groups, feats), BF16),
            shaped((groups, LANES), F32),
            pltpu.VMEM((hidden, early), BF16),
        ],
        [VMEM, VMEM],
        [pltpu.VMEM((groups, ROWS, SPAN), F32)],
        moved=one // 4,
    )(own, gate_w)
    away, cot, weight, rows, gate_late = call(
        cot_body,
        [
            shaped((total, hidden), BF16),
            shaped((total, hidden), F32),
            shaped((total, LANES), F32),
            shaped((total, width), BF16),
            pltpu.VMEM((hidden, width - early), BF16),
        ],
        [VMEM] * 6,
        [pltpu.VMEM((groups, ROWS, SPAN), F32), pltpu.VMEM((total, feats), BF16)],
        products=total * one,
        moved=one,
    )(other, own_rows, own_grads, own_weight, down_w, gate_w)
    cot_recv = swap(away, "local")
    gate, up, act, up_turned = call(
        forward_body,
        [
            shaped((total, hidden), F32),
            shaped((total, hidden), F32),
            shaped((total, hidden), BF16),
            pltpu.VMEM((hidden, width // COLS * 14 // 14 * COLS), BF16),
        ],
        [VMEM] * 3,
        products=total * 2 * one,
        moved=2 * one,
    )(rows, gate_w, up_w)
    act_recv = swap(act, "local")
    in_mine, in_away = call(
        input_body,
        [shaped((groups, ROWS, COLS), BF16)] * 2,
        [VMEM] * 9,
        [pltpu.VMEM((total, ROWS, COLS), F32)],
        products=total * 2 * one,
        moved=2 * one,
    )(cot, cot_recv, gate, up, act, weight, gate_turned, gate_late, up_turned)
    mine, away = call(
        routed_body,
        [shaped((groups, ROWS, SPAN), BF16)] * 2,
        [VMEM] * 6,
        [pltpu.VMEM((total, ROWS, LANES), F32)],
        products=total * one,
        moved=one,
    )(act, act_recv, weight, down_w, in_mine, in_away)
    summed = (mine.astype(F32) + swap(away, "core").astype(F32)).astype(BF16)
    back = lax.all_to_all(summed, ("chip", "local"), split_axis=0, concat_axis=0, tiled=True)
    return call(
        final_body,
        [
            shaped((1, 1, width), BF16),
            shaped((1, 1, width), BF16),
            shaped(expert_ids.shape, F32),
        ],
        [VMEM, VMEM],
        [pltpu.VMEM((2, ROWS, SPAN), F32)],
    )(back, named)


def selector(flags, capacity):
    live = (flags > 0).astype(jnp.int32)
    order = jnp.cumsum(live) - live
    slot_ids = lax.broadcasted_iota(jnp.int32, (capacity, flags.shape[0]), 0)
    return ((slot_ids == order[None, :]) & (live[None, :] > 0)).astype(jnp.bfloat16)


def per_device(tokens, expert_ids, route_probs, gate_weight, up_weight, down_weight, out_grad):
    node_count = lax.axis_size("node")
    token_count = tokens.shape[1]
    width = tokens.shape[2]
    top_count = expert_ids.shape[2]
    column_rows = token_count * node_count
    capacity = min(column_rows, 5 * column_rows * top_count // (2 * node_count))
    slot_count = node_count * token_count
    gate_w = gate_weight[0]
    up_w = up_weight[0]
    down_w = down_weight[0]
    hidden_dev = gate_w.shape[1]
    onehot = (expert_ids[0][..., None] == jnp.arange(node_count, dtype=jnp.int32)).astype(
        jnp.float32
    )
    weights = jnp.einsum("tk,tke->te", route_probs[0], onehot)
    member = jnp.sum(onehot, axis=1)
    own_rows = tokens[0]
    zero_value = jnp.zeros((), jnp.bfloat16)
    own_flags = member.T.astype(jnp.bfloat16)
    send_rows = jnp.where(own_flags[:, :, None] > 0, own_rows[None], zero_value)
    recv_rows, recv_flags = (
        lax.all_to_all(send_rows, "node", split_axis=0, concat_axis=0, tiled=True),
        lax.all_to_all(own_flags, "node", split_axis=0, concat_axis=0, tiled=True),
    )
    select = selector(recv_flags.reshape(slot_count), capacity)
    packed_rows = jnp.dot(
        select, recv_rows.reshape(slot_count, width), preferred_element_type=jnp.float32
    ).astype(jnp.bfloat16)
    piece = lax.all_gather(packed_rows, "local", axis=0, tiled=True)
    gate_part = jnp.dot(piece, gate_w, preferred_element_type=jnp.float32)
    up_part = jnp.dot(piece, up_w, preferred_element_type=jnp.float32)
    joined = jnp.concatenate([gate_part, up_part], axis=1)
    gate_pre = joined[:, :hidden_dev]
    up_pre = joined[:, hidden_dev:]
    sigmoid_gate = jax.nn.sigmoid(gate_pre)
    silu_gate = gate_pre * sigmoid_gate
    hidden = (silu_gate * up_pre).astype(jnp.bfloat16)
    block = down_w
    routed_part = jnp.dot(
        lax.all_gather(hidden, "local", axis=1, tiled=True),
        block,
        preferred_element_type=jnp.float32,
    )
    routed_cols = routed_part.astype(jnp.bfloat16)
    routed_own = lax.all_to_all(routed_cols, "local", split_axis=0, concat_axis=1, tiled=True)
    routed_slots = jnp.dot(select.T, routed_own, preferred_element_type=jnp.float32).astype(
        jnp.bfloat16
    )
    routed_back = lax.all_to_all(
        routed_slots.reshape(node_count, token_count, width),
        "node",
        split_axis=0,
        concat_axis=0,
        tiled=True,
    )
    routed_wide = routed_back.astype(jnp.float32)
    combined = jnp.einsum("te,etd->td", weights, routed_wide).astype(jnp.bfloat16)
    grad_wide = out_grad[0].astype(jnp.float32)
    prob_terms = jnp.einsum("td,etd->te", grad_wide, routed_wide)
    prob_grad = jnp.einsum("te,tke->tk", prob_terms, onehot)
    scaled = (weights.T[:, :, None] * grad_wide[None]).astype(jnp.bfloat16)
    grad_recv = lax.all_to_all(scaled, "node", split_axis=0, concat_axis=0, tiled=True)
    grad_own = jnp.dot(
        select, grad_recv.reshape(slot_count, width), preferred_element_type=jnp.float32
    ).astype(jnp.bfloat16)
    grad_cols = lax.all_to_all(grad_own, "local", split_axis=1, concat_axis=0, tiled=True)
    block = down_w
    hidden_grad = (
        lax.psum_scatter(
            lax.dot_general(
                block, grad_cols, (((1,), (1,)), ((), ())), preferred_element_type=jnp.float32
            ).astype(jnp.bfloat16),
            "local",
            scatter_dimension=0,
            tiled=True,
        )
        .astype(jnp.float32)
        .T
    )
    gate_grad = (
        hidden_grad * up_pre * sigmoid_gate * (1.0 + gate_pre * (1.0 - sigmoid_gate))
    ).astype(jnp.bfloat16)
    up_grad = (hidden_grad * silu_gate).astype(jnp.bfloat16)
    first = lax.dot_general(
        gate_grad, gate_w, (((1,), (1,)), ((), ())), preferred_element_type=jnp.float32
    )
    second = lax.dot_general(
        up_grad, up_w, (((1,), (1,)), ((), ())), preferred_element_type=jnp.float32
    )
    input_own = lax.psum_scatter(
        (first + second).astype(jnp.bfloat16), "local", scatter_dimension=0, tiled=True
    )
    input_slots = jnp.dot(select.T, input_own, preferred_element_type=jnp.float32).astype(
        jnp.bfloat16
    )
    input_back = lax.all_to_all(
        input_slots.reshape(node_count, token_count, width),
        "node",
        split_axis=0,
        concat_axis=0,
        tiled=True,
    )
    input_grad = jnp.sum(input_back.astype(jnp.float32), axis=0).astype(jnp.bfloat16)
    return (combined[None], input_grad[None], prob_grad[None])


def solution(mesh):
    node, local = mesh.shape["node"], mesh.shape["local"]
    if local == 2 and node % 2 == 0 and node <= 16:
        mesh = Mesh(mesh.devices.reshape(node // 2, 2, local), ("chip", "core", "local"))
        body, nodes = fast_device, ("chip", "core")
    else:
        body, nodes = per_device, "node"
    rows = P("local", nodes, None)
    weights = P(nodes, None, "local")
    return jax.shard_map(
        body,
        mesh=mesh,
        in_specs=(rows, rows, rows, weights, weights, weights, rows),
        out_specs=(rows, rows, rows),
        check_vma=False,
    )
```
